32 devices in a mesh: src: 2 (over x), snk: 4 (over z), mom: 4 (over y, core).
Axes of the slice: x: 2, y: 2, z: 4, core: 2. Of those that a mesh axis runs over, the one named last changes fastest.
Arguments:
- peram_blocks: bfloat16 [8, 8, 2, 512, 512], P('src', 'snk'), may hold values from -5 to 5
- projections: bfloat16 [8, 4, 4, 2, 128, 128], P('src', 'mom'), may hold values from -0.5 to 0.5
- gamma_index: int32 [4, 4], replicated, may hold values from 0 to 15
- partner: int32 [4], P('mom'), may hold values from 0 to 3, each once
- separations: int32 [4], replicated, may hold values from 1 to 7, as said below
Outputs:
- correlator: float32 [8, 4, 4, 2], P(None, None, 'mom')
The draws below stay inside these ranges and needn't reach their ends.
Inputs may be any that keep to these rules, and one draw needn't show every extreme that they name: Each operator appears once as the partner of a source operator. separations count source time slices; sink slices are taken modulo 8.
All inputs are finite; a program needn't handle non-finite values.
Results may differ from the reference program's by a relative error of at most 0.007.
Values may be sent and summed in bfloat16 or wider, within the bound.
No kernel may reach another device: no remote copies, remote signals or barrier semaphores. Data moves between devices by JAX's collectives and lax.ppermute only.
A program may use at most 128 MiB of HBM per device.

```python
import jax
import jax.numpy as jnp
import numpy as np
from jax import lax

NEV = 128
NTERM = 4
NSEP = 4
M = 512
NT = 8
NOFF = 8
NMOM = 4


def draw_separations(key, part):
    key = jax.random.fold_in(key, 7)
    extremes = jnp.array([NT - 1, 1], dtype=jnp.int32)
    middle = jax.random.randint(key, (NSEP,), 1, NT, dtype=jnp.int32)
    values = jnp.concatenate([extremes, middle[2:]])
    shuffled = jax.random.permutation(jax.random.fold_in(key, 1), NSEP)
    return values[shuffled].astype(jnp.int32)


def plant(values, own_key, smallest, top_value):
    dims = values.shape
    index_at = [jax.random.randint(jax.random.fold_in(own_key, axis), (), 0, dims[axis]) for axis in range(len(dims))]
    values = values.at[tuple(index_at)].set(smallest)
    longest = dims.index(max(dims))
    index_at[longest] = (index_at[longest] + 1) % dims[longest]
    return values.at[tuple(index_at)].set(top_value)


def level_of(rng, extent, cuts, least, high):
    level = 1.0
    for dim, parts in cuts:
        draws = jax.random.uniform(jax.random.fold_in(jax.random.fold_in(rng, 6), dim), (parts,), jnp.float32, least / len(cuts), high / len(cuts))
        level = level * jnp.repeat(jnp.exp(draws), extent[dim] // parts).reshape((-1,) + (1,) * (len(extent) - 1 - dim))
    return level


def centred(rng, dims, spread, bound, pieces=(), held_as=jnp.bfloat16):
    loudness = level_of(rng, dims, pieces, -0.22, 0.18) if pieces else 1.0
    values = jax.random.normal(rng, dims, jnp.float32) * spread * loudness
    return jnp.minimum(jnp.maximum(values, -bound), bound).astype(held_as)


def setup_inputs(seed: int = 0) -> dict:
    key_list = jax.random.split(jax.random.key(seed), 6)
    return {
        "peram_blocks": centred(key_list[0], (NT, NOFF, 2, M, M), 0.35, 5.0, ((0, 2), (1, 4))),
        "projections": centred(key_list[1], (NT, NMOM, NTERM, 2, NEV, NEV), NEV ** -0.5, 0.5, ((0, 2), (1, 4))),
        "gamma_index": plant(jax.random.randint(key_list[2], (NMOM, NTERM), 0, 16), jax.random.fold_in(key_list[2], 1), 0, 15).astype(jnp.int32),
        "partner": jax.random.permutation(key_list[3], NMOM).astype(jnp.int32),
        "separations": draw_separations(jax.random.fold_in(key_list[5], 71), 0),
    }


def dirac_table():
    zero_matrix = np.zeros((4, 4))
    unit_real = np.eye(4)
    gamma_one = (zero_matrix, np.array([[0, 0, 0, 1], [0, 0, 1, 0], [0, -1, 0, 0], [-1, 0, 0, 0]], dtype=np.float32))
    gamma_two = (np.array([[0, 0, 0, -1], [0, 0, 1, 0], [0, 1, 0, 0], [-1, 0, 0, 0]], dtype=np.float32), zero_matrix)
    gamma_three = (zero_matrix, np.array([[0, 0, 1, 0], [0, 0, 0, -1], [-1, 0, 0, 0], [0, 1, 0, 0]], dtype=np.float32))
    gamma_four = (np.array([[0, 0, 1, 0], [0, 0, 0, 1], [1, 0, 0, 0], [0, 1, 0, 0]], dtype=np.float32), zero_matrix)
    factors = (gamma_one, gamma_two, gamma_three, gamma_four)
    real_list = []
    imag_list = []
    for gamma_code in range(16):
        real_now = unit_real
        imag_now = zero_matrix
        for position in range(4):
            if (gamma_code >> position) & 1:
                factor_real, factor_imag = factors[position]
                next_real = real_now @ factor_real - imag_now @ factor_imag
                next_imag = real_now @ factor_imag + imag_now @ factor_real
                real_now = next_real
                imag_now = next_imag
        real_list.append(real_now)
        imag_list.append(imag_now)
    return np.stack([np.stack(real_list), np.stack(imag_list)], axis=1).astype(np.float32)


def build_elementals(projections, gamma_index):
    codes = jnp.arange(16, dtype=jnp.int32)
    one_hot = (gamma_index[:, :, None] == codes[None, None, :]).astype(jnp.float32)
    spin_part = jnp.einsum('prg,gcst->prcst', one_hot, jnp.asarray(dirac_table()).astype(jnp.float32))
    proj_real = projections[:, :, :, 0].astype(jnp.float32)
    proj_imag = projections[:, :, :, 1].astype(jnp.float32)
    form = 'prst,wpref->wpsetf'
    real_part = jnp.einsum(form, spin_part[:, :, 0], proj_real) - jnp.einsum(form, spin_part[:, :, 1], proj_imag)
    imag_part = jnp.einsum(form, spin_part[:, :, 0], proj_imag) + jnp.einsum(form, spin_part[:, :, 1], proj_real)
    full_width = 4 * projections.shape[-1]
    shape_out = (projections.shape[0], projections.shape[1], full_width, full_width)
    stacked = jnp.stack([real_part.reshape(shape_out), imag_part.reshape(shape_out)], axis=2)
    return stacked.astype(jnp.bfloat16)


def complex_product(block, elementals):
    block_wide = block.astype(jnp.float32)
    elem_wide = lax.optimization_barrier(elementals).astype(jnp.float32)
    form = 'xc,ocy->oxy'
    real_part = jnp.einsum(form, block_wide[0], elem_wide[:, 0]) - jnp.einsum(form, block_wide[1], elem_wide[:, 1])
    imag_part = jnp.einsum(form, block_wide[0], elem_wide[:, 1]) + jnp.einsum(form, block_wide[1], elem_wide[:, 0])
    return jnp.stack([real_part, imag_part], axis=1).astype(jnp.bfloat16)


def reference(peram_blocks, projections, gamma_index, partner, separations):
    def one_pair(flat_index):
        time_now = flat_index // NSEP
        sep_index = flat_index % NSEP
        time_back = (time_now + separations[sep_index]) % NT
        forward_block = peram_blocks[time_now, sep_index]
        backward_block = peram_blocks[time_back, NSEP + sep_index]
        elem_now = build_elementals(projections[time_now][None], gamma_index)[0]
        elem_back = build_elementals(projections[time_back][None], gamma_index)[0][partner]
        forward = lax.optimization_barrier(complex_product(forward_block, elem_now)).astype(jnp.float32)
        backward = lax.optimization_barrier(complex_product(backward_block, elem_back)).astype(jnp.float32)
        form = 'pxy,pyx->p'
        real_part = jnp.einsum(form, forward[:, 0], backward[:, 0]) - jnp.einsum(form, forward[:, 1], backward[:, 1])
        imag_part = jnp.einsum(form, forward[:, 0], backward[:, 1]) + jnp.einsum(form, forward[:, 1], backward[:, 0])
        return jnp.stack([real_part, imag_part], axis=-1) / M
    values = lax.map(one_pair, jnp.arange(NT * NSEP, dtype=jnp.int32))
    return values.reshape(NT, NSEP, NMOM, 2)
```

```python
import functools

import jax
import jax.numpy as jnp
import numpy as np
from jax import lax
from jax.experimental import pallas as pl
from jax.experimental.pallas import tpu as pltpu
from jax.sharding import PartitionSpec as P

NSPIN = 4
NCODE = 16
NT_DIMS = (((1,), (1,)), ((), ()))
TILE = 256
STRIP = 32
VMEM_LIMIT = 48 * 1024 * 1024


def dirac_table():
    zero = np.zeros((4, 4))
    one = (zero, np.array([[0, 0, 0, 1], [0, 0, 1, 0], [0, -1, 0, 0], [-1, 0, 0, 0]]))
    two = (np.array([[0, 0, 0, -1], [0, 0, 1, 0], [0, 1, 0, 0], [-1, 0, 0, 0]]), zero)
    three = (zero, np.array([[0, 0, 1, 0], [0, 0, 0, -1], [-1, 0, 0, 0], [0, 1, 0, 0]]))
    four = (np.array([[0, 0, 1, 0], [0, 0, 0, 1], [1, 0, 0, 0], [0, 1, 0, 0]]), zero)
    out = []
    for code in range(NCODE):
        real, imag = np.eye(4), zero
        for position, (fr, fi) in enumerate((one, two, three, four)):
            if code >> position & 1:
                real, imag = real @ fr - imag @ fi, real @ fi + imag @ fr
        out.append(np.stack([real, imag]))
    return np.stack(out).astype(np.float32)


def build(table, code_of, planes, store, transposed):
    nterm = 4
    nev = 128
    codes = [code_of(r) for r in range(nterm)]

    def coefficient(r, plane, left, right):
        if transposed:
            left, right = right, left
        return table[codes[r] * 32 + (plane * 16 + left * 4 + right)]

    coeffs = {}
    for left in range(NSPIN):
        for right in range(NSPIN):
            for r in range(nterm):
                for plane in range(2):
                    coeffs[r, plane, left, right] = coefficient(r, plane, left, right)

    def step(index, carry):
        row = pl.multiple_of(index * STRIP, STRIP)
        parts = [(planes(r, 0, row), planes(r, 1, row)) for r in range(nterm)]
        for left in range(NSPIN):
            for right in range(NSPIN):
                re = im = None
                for r in range(nterm):
                    cr, ci = coeffs[r, 0, left, right], coeffs[r, 1, left, right]
                    pr, pi = parts[r]
                    add_re, add_im = cr * pr - ci * pi, cr * pi + ci * pr
                    re = add_re if re is None else re + add_re
                    im = add_im if im is None else im + add_im
                store(left, right, row, re, im)
        return carry

    lax.fori_loop(0, nev // STRIP, step, 0)


def own_kernel(scal, gamma, table, x_ref, *refs):
    count = (len(refs) - 4) // 1
    pieces, (ht_ref, y_ref, u_ref, tr_ref) = refs[:count], refs[count:]
    mom = scal[0]
    width = x_ref.shape[-1]
    real, imag = x_ref[0, 0, 0], x_ref[0, 0, 1]
    y_ref[:width, :width] = real
    y_ref[:width, width:] = -imag
    y_ref[width:, :width] = imag
    y_ref[width:, width:] = real
    nev = tr_ref.shape[-1]

    for p, piece in enumerate(pieces):
        view = piece
        for r in range(4):
            for plane in range(2):
                source = view[0, 0, r, plane] if p == 0 else view[r, plane]
                tr_ref[p, r, plane] = source.astype(jnp.float32).T

    def product(p, carry):
        op = mom ^ p

        def planes(r, plane, row):
            return tr_ref[p, r, plane, pl.ds(row, STRIP), :]

        def store(left, right, row, re, im):
            rows = pl.ds(pl.multiple_of(left * nev + row, STRIP), STRIP)
            u_ref[rows, right * nev : (right + 1) * nev] = re.astype(jnp.bfloat16)
            u_ref[rows, width + right * nev : width + (right + 1) * nev] = im.astype(jnp.bfloat16)

        build(table, lambda r: gamma[op, r], planes, store, True)

        def tile(n, inner):
            rows = pl.ds(pl.multiple_of(n * TILE, TILE), TILE)
            out = lax.dot_general(
                u_ref[...], y_ref[rows, :], NT_DIMS, preferred_element_type=jnp.float32
            )
            ht_ref[p, :, rows] = out.astype(jnp.bfloat16)
            return inner

        return lax.fori_loop(0, 2 * width // TILE, tile, carry)

    lax.fori_loop(0, count, product, 0)


def other_kernel(scal, gamma, table, bsel, ht_ref, *refs):
    count = (len(refs) - 3) // 2
    here, away = refs[:count], refs[count : 2 * count]
    k_ref, v_ref, p_ref = refs[2 * count :]
    mom, cross = scal[0], scal[1]
    width = ht_ref.shape[1]
    nev = p_ref.shape[-1]

    @pl.when(cross == 0)
    def _():
        for p in range(count):
            p_ref[p] = here[p][...]

    @pl.when(cross != 0)
    def _():
        for p in range(count):
            p_ref[p] = away[p][...]

    def product(p, carry):
        op = mom ^ p

        def planes(r, plane, row):
            return p_ref[p, r, plane, pl.ds(row, STRIP), :].astype(jnp.float32)

        def store(left, right, row, re, im):
            top = pl.ds(pl.multiple_of(left * nev + row, STRIP), STRIP)
            low = pl.ds(pl.multiple_of(width + left * nev + row, STRIP), STRIP)
            near = slice(right * nev, (right + 1) * nev)
            far = slice(width + right * nev, width + (right + 1) * nev)
            re, im = re.astype(jnp.bfloat16), im.astype(jnp.bfloat16)
            v_ref[top, near] = re
            v_ref[top, far] = -im
            v_ref[low, near] = im
            v_ref[low, far] = re

        build(table, lambda r: gamma[op, r], planes, store, False)
        left = bsel[p]

        def tile(n, inner):
            rows = pl.ds(pl.multiple_of(n * TILE, TILE), TILE)
            k_ref[p, :, rows] = lax.dot_general(
                ht_ref[left], v_ref[rows, :], NT_DIMS, preferred_element_type=jnp.float32
            )
            return inner

        return lax.fori_loop(0, 2 * width // TILE, tile, carry)

    lax.fori_loop(0, count, product, 0)


def trace_kernel(scal, label, k_ref, near_ref, far_ref, rest_ref, *refs):
    outs = refs
    count = len(outs)
    mom, cross = scal[0], scal[1]
    width = k_ref.shape[1]
    half = near_ref.shape[1]
    rows = 16

    def part(source, offset, totals):
        def step(index, totals):
            row = pl.multiple_of(index * rows, rows)
            real = source[0, pl.ds(row, rows), :].astype(jnp.float32)
            imag = source[1, pl.ds(row, rows), :].astype(jnp.float32)
            new = []
            for p in range(count):
                here = pl.ds(pl.multiple_of(offset + row, rows), rows)
                kr, ki = k_ref[p, here, :width], k_ref[p, here, width:]
                re, im = real * kr - imag * ki, real * ki + imag * kr
                new.append(totals[2 * p] + re)
                new.append(totals[2 * p + 1] + im)
            return tuple(new)

        return lax.fori_loop(0, source.shape[1] // rows, step, totals)

    zero = jnp.zeros((rows, width), jnp.float32)
    totals = tuple(zero for _ in range(2 * count))
    totals = lax.cond(
        cross != 0, lambda t: part(far_ref, 0, t), lambda t: part(near_ref, 0, t), totals
    )
    totals = part(rest_ref, half, totals)
    sums = [jnp.sum(total) * (1.0 / width) for total in totals]
    lane = lax.broadcasted_iota(jnp.int32, (1, 128), 1)
    for i, out in enumerate(outs):
        line = jnp.zeros((1, 128), jnp.float32)
        for p in range(count):
            mine = label[p] == (mom ^ i)
            re = jnp.where(mine, sums[2 * p], 0.0)
            im = jnp.where(mine, sums[2 * p + 1], 0.0)
            line = line + jnp.where(lane % 2 == 0, re, im)
        out[...] = line


def place_kernel(scal, times, *refs):
    lines, out = refs[:-1], refs[-1]
    sep_index, live = scal[2], scal[3]
    time = lax.broadcasted_iota(jnp.int32, out.shape, 0)
    lane = lax.broadcasted_iota(jnp.int32, out.shape, 1)
    total = jnp.zeros(out.shape, jnp.float32)
    for i, line in enumerate(lines):
        here = (time == times[i]) & (lane // 2 == sep_index) & (live != 0)
        total = total + jnp.where(here, line[...], 0.0)
    out[...] = total


def smem():
    return pl.BlockSpec(memory_space=pltpu.SMEM)


def vmem():
    return pl.BlockSpec(memory_space=pltpu.VMEM)


def params():
    return pltpu.CompilerParams(vmem_limit_bytes=VMEM_LIMIT)


def shards(peram_blocks, projections, gamma_index, partner, separations):
    src_count, snk_count = lax.axis_size("src"), lax.axis_size("snk")
    mom_count = lax.axis_size("mom")
    slices, offsets = peram_blocks.shape[:2]
    width = peram_blocks.shape[-1]
    nterm, nev = projections.shape[2], projections.shape[-1]
    time_count = slices * src_count
    sep_count = separations.shape[0]
    half_snk = snk_count // 2
    src, snk, mom = lax.axis_index("src"), lax.axis_index("snk"), lax.axis_index("mom")
    is_forward = snk < half_snk
    plane = snk % half_snk
    keep = jnp.where(is_forward, 0, offsets - 1)
    give = jnp.where(is_forward, offsets - 1, 0)
    sep_index = plane * offsets + keep
    shift = jnp.where(is_forward, 1, -1) * separations[sep_index]
    peer_shift = jnp.where(is_forward, -1, 1) * separations[plane * offsets + give]

    def local(place, amount):
        return (place + amount) % slices

    def hops(place, amount):
        return ((place + amount) % time_count) // slices

    def swap_mom(array, i):
        return lax.ppermute(array, "mom", [(a, a ^ i) for a in range(mom_count)])

    def swap_snk(array):
        pairs = [(a, (a + half_snk) % snk_count) for a in range(snk_count)]
        return lax.ppermute(array, "snk", pairs)

    def along_src(array, amount):
        step, near = 1, array
        while True:
            if step >= src_count:
                return near, near, jnp.int32(0)
            pairs = [((a + step) % src_count, a) for a in range(src_count)]
            far = lax.ppermute(near, "src", pairs)
            flag = (amount // step) % 2
            step *= 2
            if step >= src_count:
                return near, far, flag
            near = jnp.where(flag != 0, far, near)

    half_rows = width // 2
    peer_local, peer_hops = local(mom, peer_shift), hops(mom, peer_shift)
    own_hops = hops(mom, shift)

    def rows_of(start):
        return lax.dynamic_slice(
            peram_blocks, (peer_local, give, 0, start, 0), (1, 1, 2, half_rows, width)
        ).reshape(2, half_rows, width)

    first = swap_snk(rows_of(0))
    near, far, flag = along_src(rows_of(half_rows), peer_hops)
    rest = swap_snk(jnp.where(flag != 0, far, near))

    def projection(index):
        return lax.dynamic_index_in_dim(projections, index, 0, keepdims=False)[0]

    partners = jnp.stack(
        [partner[0]] + [swap_mom(partner, i)[0] for i in range(1, mom_count)]
    )
    here, away = [], []
    for i in range(mom_count):
        piece = projection(local(mom ^ i, shift))
        if i:
            piece = swap_mom(piece, i)
        near, far, _ = along_src(piece, own_hops)
        here.append(near)
        away.append(far)
    own = [projections]
    for i in range(1, mom_count):
        own.append(swap_mom(projection(mom ^ i), i))

    first_near, first_far, cross = along_src(first, own_hops)

    pieces = jnp.arange(mom_count, dtype=jnp.int32)
    inverse = jnp.sum(
        jnp.where(partners[None, :] == (mom ^ pieces)[:, None], (mom ^ pieces)[None, :], 0), axis=1
    )
    label = jnp.where(is_forward, inverse, mom ^ pieces).astype(jnp.int32)
    bsel = (jnp.where(is_forward, inverse, partners) ^ mom).astype(jnp.int32)
    live = jnp.where(is_forward, 1, int(offsets > 1))
    scal = jnp.stack([mom, cross, sep_index, live]).astype(jnp.int32)
    table = jnp.asarray(dirac_table().reshape(-1))
    where_own = jnp.stack([mom, keep]).astype(jnp.int32)

    ht = pl.pallas_call(
        own_kernel,
        grid_spec=pltpu.PrefetchScalarGridSpec(
            num_scalar_prefetch=1,
            grid=(1,),
            in_specs=[
                smem(),
                smem(),
                pl.BlockSpec((1, 1, 2, width, width), lambda g, at: (at[0], at[1], 0, 0, 0)),
                pl.BlockSpec((1, 1, nterm, 2, nev, nev), lambda g, at: (at[0], 0, 0, 0, 0, 0)),
            ]
            + [pl.BlockSpec((nterm, 2, nev, nev), lambda g, at: (0, 0, 0, 0))] * (mom_count - 1),
            out_specs=pl.BlockSpec((mom_count, width, 2 * width), lambda g, at: (0, 0, 0)),
            scratch_shapes=[
                pltpu.VMEM((2 * width, 2 * width), jnp.bfloat16),
                pltpu.VMEM((width, 2 * width), jnp.bfloat16),
                pltpu.VMEM((mom_count, nterm, 2, nev, nev), jnp.float32),
            ],
        ),
        out_shape=jax.ShapeDtypeStruct((mom_count, width, 2 * width), jnp.bfloat16),
        compiler_params=params(),
        name="own_products",
    )(where_own, gamma_index, table, peram_blocks, *own)

    k = pl.pallas_call(
        other_kernel,
        in_specs=[smem()] * 4 + [vmem()] * (1 + 2 * mom_count),
        out_specs=vmem(),
        out_shape=jax.ShapeDtypeStruct((mom_count, width, 2 * width), jnp.float32),
        scratch_shapes=[
            pltpu.VMEM((2 * width, 2 * width), jnp.bfloat16),
            pltpu.VMEM((mom_count, nterm, 2, nev, nev), jnp.bfloat16),
        ],
        compiler_params=params(),
        name="other_products",
    )(scal, gamma_index, table, bsel, ht, *here, *away)

    lines = pl.pallas_call(
        trace_kernel,
        in_specs=[smem()] * 2 + [vmem()] * 4,
        out_specs=[vmem()] * mom_count,
        out_shape=[jax.ShapeDtypeStruct((1, 128), jnp.float32)] * mom_count,
        compiler_params=params(),
        name="traces",
    )(scal, label, k, first_near, first_far, rest)

    got = [lines[0]] + [swap_mom(lines[i], i) for i in range(1, mom_count)]
    own_time = src * slices + (mom ^ pieces)
    times = jnp.where(is_forward, own_time, own_time + shift) % time_count
    total = pl.pallas_call(
        place_kernel,
        in_specs=[smem()] * 2 + [vmem()] * mom_count,
        out_specs=vmem(),
        out_shape=jax.ShapeDtypeStruct((time_count, 128), jnp.float32),
        name="placed",
    )(scal, times.astype(jnp.int32), *got)

    for axis, count in (("src", src_count), ("snk", snk_count)):
        step = 1
        while step < count:
            total = total + lax.ppermute(total, axis, [(a, a ^ step) for a in range(count)])
            step *= 2
    return total[:, : 2 * sep_count].reshape(time_count, sep_count, 1, 2)


def solution(mesh):
    placed = (
        P("src", "snk", None, None, None),
        P("src", "mom", None, None, None, None),
        P(),
        P("mom"),
        P(),
    )
    return jax.shard_map(
        shards, mesh=mesh, in_specs=placed, out_specs=P(None, None, "mom", None), check_vma=False
    )
```

```python
import jax
import jax.numpy as jnp
from jax import lax
from jax.experimental import pallas as pl
from jax.experimental.pallas import tpu as pltpu
from jax.sharding import PartitionSpec as P

NSPIN = 4
NT_DIMS = (((1,), (1,)), ((), ()))
MIB = 1024 * 1024
TAG_ROWS = 16
GAMMAS = (
    (3, 1 | 1 << 2 | 3 << 4 | 3 << 6),
    (3, 2 | 0 << 2 | 0 << 4 | 2 << 6),
    (2, 1 | 3 << 2 | 3 << 4 | 1 << 6),
    (2, 0),
)


def spin_entry(code, row):
    phase = row * 0
    for bit, (flip, phases) in enumerate(GAMMAS):
        on = (code >> bit) & 1
        phase = phase + on * ((phases >> (2 * row)) & 3)
        row = row ^ (on * flip)
    return row, phase & 3


def spin_column_entry(code, column):
    row = column
    for bit, (flip, _) in enumerate(GAMMAS):
        row = row ^ (((code >> bit) & 1) * flip)
    return row, spin_entry(code, row)[1]


def phase_blocks(block_ref, r, real, imag):
    nev = real.shape[0]
    for phase, (a, b) in enumerate(((real, imag), (-imag, real), (-real, -imag), (imag, -real))):
        slot = 4 * r + phase
        block_ref[slot, :nev, :nev] = a
        block_ref[slot, :nev, nev:] = -b
        block_ref[slot, nev:, :nev] = b
        block_ref[slot, nev:, nev:] = a


def position():
    return lax.axis_index("src"), lax.axis_index("snk"), lax.axis_index("mom")


def pair_plan(separations, snk, offsets, half_snk):
    forward = snk < half_snk
    base = lax.rem(snk, half_snk) * offsets
    keep = jnp.where(forward, 0, offsets - 1)
    give = offsets - 1 - keep
    sign = jnp.where(forward, 1, -1)
    return forward, keep, give, base + keep, sign * separations[base + keep], -sign * separations[base + give]


def pack_kernel(place, seps, partner, peram, proj, *refs):
    outs, (tag, sems) = refs[:-2], refs[-2:]
    first, rest, here = outs[:3]
    count = (len(outs) - 3) // 2
    other, own = outs[3 : 3 + count], outs[3 + count :]
    slices, offsets = peram.shape[:2]
    time_count, half_snk = place[3], place[4]
    snk, mom = place[1], place[2]
    _, _, give, _, shift, peer_shift = pair_plan(seps, snk, offsets, half_snk)

    def local(amount):
        return lax.rem(amount + time_count, slices)

    half = first.shape[1]
    rows = own[0].shape[0] - TAG_ROWS
    peer = local(mom + peer_shift)
    tag[...] = jnp.full(tag.shape, partner[0].astype(jnp.float32)).astype(jnp.bfloat16)
    copies = [
        (peram.at[peer, give, :, pl.ds(0, half)], first),
        (peram.at[peer, give, :, pl.ds(half, half)], rest),
    ]
    for i in range(count):
        copies.append((proj.at[local((mom ^ (i + 1)) + shift)], other[i]))
    copies.append((proj.at[local(mom + shift)], here))
    for i in range(count):
        copies.append((proj.at[mom ^ (i + 1)], own[i].at[pl.ds(0, rows)]))
        copies.append((tag, own[i].at[pl.ds(rows, TAG_ROWS)]))
    handles = [
        pltpu.make_async_copy(source, target, sems.at[n])
        for n, (source, target) in enumerate(copies)
    ]
    for handle in handles:
        handle.start()
    for handle in handles:
        handle.wait()


def own_kernel(place, gamma, x_ref, *refs):
    pieces, (ht_ref, xb_ref, block_ref, tr_ref) = refs[:-4], refs[-4:]
    mom = place[0]
    nev = tr_ref.shape[-1]
    for spin in range(NSPIN):
        lanes = slice(spin * nev, (spin + 1) * nev)
        xb_ref[spin, :, :nev] = x_ref[0, 0, 0, :, lanes]
        xb_ref[spin, :, nev:] = x_ref[0, 0, 1, :, lanes]
    nterm = tr_ref.shape[1] // 2
    for p, piece in enumerate(pieces):
        for n in range(2 * nterm):
            rows = slice(n * nev, (n + 1) * nev)
            source = piece[0, rows] if p == 0 else piece[rows]
            tr_ref[p, n] = source.T

    def product(p, carry):
        for r in range(nterm):
            phase_blocks(block_ref, r, tr_ref[p, 2 * r], tr_ref[p, 2 * r + 1])

        def spin_rows(spin, inner):
            total = None
            for r in range(nterm):
                source, phase = spin_column_entry(gamma[mom ^ p, r], spin)
                term = lax.dot_general(
                    block_ref[4 * r + phase],
                    xb_ref[source],
                    NT_DIMS,
                    preferred_element_type=jnp.float32,
                )
                total = term if total is None else total + term
            total = total.astype(jnp.bfloat16)
            rows = pl.ds(pl.multiple_of(spin * nev, nev), nev)
            for column in range(NSPIN):
                lanes = slice(column * nev, (column + 1) * nev)
                ht_ref[p, column, rows, :nev] = total[:nev, lanes]
                ht_ref[p, column, rows, nev:] = total[nev:, lanes]
            return inner

        return lax.fori_loop(0, NSPIN, spin_rows, carry)

    lax.fori_loop(0, len(pieces), product, 0)


def other_kernel(place, gamma, partner, ht_ref, *refs):
    count = place_count = ht_ref.shape[0]
    tags = refs[: count - 1]
    here, away = refs[count - 1 : 2 * count - 1], refs[2 * count - 1 : 3 * count - 1]
    k_ref, label_ref, p_ref, block_ref = refs[3 * count - 1 :]
    mom, cross, forward = place[0], place[1], place[2]
    nev = block_ref.shape[-1] // 2
    nterm = block_ref.shape[0] // 4
    partners = [partner[0]] + [
        jnp.max(tag[tag.shape[0] - TAG_ROWS :].astype(jnp.float32)).astype(jnp.int32)
        for tag in tags
    ]
    for p in range(place_count):
        back = jnp.int32(0)
        for i in range(count):
            back = back + jnp.where(partners[i] == (mom ^ p), mom ^ i, 0)
        label_ref[p] = jnp.where(forward != 0, back, mom ^ p)
        label_ref[count + p] = jnp.where(forward != 0, back, partners[p]) ^ mom

    @pl.when(cross == 0)
    def _():
        for p in range(count):
            p_ref[p] = here[p][...]

    @pl.when(cross != 0)
    def _():
        for p in range(count):
            p_ref[p] = away[p][...]

    def product(p, carry):
        for r in range(nterm):
            real = p_ref[p, 2 * r * nev : (2 * r + 1) * nev]
            imag = p_ref[p, (2 * r + 1) * nev : (2 * r + 2) * nev]
            phase_blocks(block_ref, r, real, imag)
        left = label_ref[count + p]

        def spin_columns(spin, inner):
            total = None
            for r in range(nterm):
                source, phase = spin_entry(gamma[mom ^ p, r], spin)
                term = lax.dot_general(
                    ht_ref[left, source],
                    block_ref[4 * r + phase],
                    NT_DIMS,
                    preferred_element_type=jnp.float32,
                )
                total = term if total is None else total + term
            k_ref[p, spin] = total
            return inner

        return lax.fori_loop(0, NSPIN, spin_columns, carry)

    lax.fori_loop(0, count, product, 0)


def row_sums(k_ref, source, offset, totals):
    rows = 16
    count = len(totals) // 2
    nev = source.shape[-1] // NSPIN

    def step(index, totals):
        row = pl.multiple_of(index * rows, rows)
        here = pl.ds(pl.multiple_of(offset + row, rows), rows)
        totals = list(totals)
        for spin in range(NSPIN):
            lanes = slice(spin * nev, (spin + 1) * nev)
            real = source[0, pl.ds(row, rows), lanes].astype(jnp.float32)
            imag = source[1, pl.ds(row, rows), lanes].astype(jnp.float32)
            for p in range(count):
                kr, ki = k_ref[p, spin, here, :nev], k_ref[p, spin, here, nev:]
                totals[2 * p] += real * kr - imag * ki
                totals[2 * p + 1] += real * ki + imag * kr
        return tuple(totals)

    return lax.fori_loop(0, source.shape[1] // rows, step, totals)


def early_kernel(place, k_ref, near_ref, far_ref, sums_ref):
    cross = place[1]
    count = sums_ref.shape[0]
    zero = tuple(jnp.zeros(sums_ref.shape[1:], jnp.float32) for _ in range(count))

    @pl.when(cross == 0)
    def _():
        for n, total in enumerate(row_sums(k_ref, near_ref, 0, zero)):
            sums_ref[n] = total

    @pl.when(cross != 0)
    def _():
        for n, total in enumerate(row_sums(k_ref, far_ref, 0, zero)):
            sums_ref[n] = total


def late_kernel(place, label, k_ref, rest_ref, sums_ref, *outs):
    count = len(outs)
    mom, time, sep_index, live = place[0], place[3], place[4], place[5]
    width = rest_ref.shape[-1]
    half = k_ref.shape[2] - rest_ref.shape[1]
    totals = row_sums(k_ref, rest_ref, half, tuple(sums_ref[n] for n in range(2 * count)))
    sums = [jnp.sum(total, axis=0, keepdims=True) for total in totals]
    sums = [jnp.sum(total, axis=1, keepdims=True) * (1.0 / width) for total in sums]
    shape = outs[0].shape
    row = lax.broadcasted_iota(jnp.int32, shape, 0)
    lane = lax.broadcasted_iota(jnp.int32, shape, 1)
    here = (row == time) & (lane // 2 == sep_index) & (live != 0)
    values = [jnp.where(lane % 2 == 0, sums[2 * p], sums[2 * p + 1]) for p in range(count)]
    for i, out in enumerate(outs):
        line = jnp.zeros(shape, jnp.float32)
        for p in range(count):
            line = jnp.where(label[p] == (mom ^ i), values[p], line)
        out[...] = jnp.where(here, line, 0.0)


def smem():
    return pl.BlockSpec(memory_space=pltpu.SMEM)


def vmem():
    return pl.BlockSpec(memory_space=pltpu.VMEM)


def anywhere():
    return pl.BlockSpec(memory_space=pl.ANY)


def limit(mib):
    return pltpu.CompilerParams(vmem_limit_bytes=mib * MIB)


def shards(peram_blocks, projections, gamma_index, partner, separations):
    src_count, snk_count = lax.axis_size("src"), lax.axis_size("snk")
    mom_count = lax.axis_size("mom")
    slices, offsets = peram_blocks.shape[:2]
    width = peram_blocks.shape[-1]
    nterm, nev = projections.shape[2], projections.shape[-1]
    time_count = slices * src_count
    sep_count = separations.shape[0]
    half_snk = snk_count // 2
    half_rows = width // 2
    src, snk, mom = position()
    forward, keep, _, sep_index, shift, peer_shift = pair_plan(separations, snk, offsets, half_snk)
    own_hops = ((mom + shift) % time_count) // slices
    peer_hops = ((mom + peer_shift) % time_count) // slices
    own_time = src * slices + mom
    pair_time = jnp.where(forward, own_time, own_time + shift) % time_count
    live = jnp.where(forward, 1, int(offsets > 1))

    def swap_mom(array, i):
        return lax.ppermute(array, "mom", [(a, a ^ i) for a in range(mom_count)])

    def swap_snk(array):
        pairs = [(a, (a + half_snk) % snk_count) for a in range(snk_count)]
        return lax.ppermute(array, "snk", pairs)

    def along_src(array, amount):
        step, near = 1, array
        while True:
            if step >= src_count:
                return near, near, jnp.int32(0)
            pairs = [((a + step) % src_count, a) for a in range(src_count)]
            far = lax.ppermute(near, "src", pairs)
            flag = (amount // step) % 2
            step *= 2
            if step >= src_count:
                return near, far, flag
            near = jnp.where(flag != 0, far, near)

    rows = nterm * 2 * nev
    proj_rows = projections.reshape(slices, rows, nev)
    block_half = jax.ShapeDtypeStruct((2, half_rows, width), jnp.bfloat16)
    piece = jax.ShapeDtypeStruct((rows, nev), jnp.bfloat16)
    tagged = jax.ShapeDtypeStruct((rows + TAG_ROWS, nev), jnp.bfloat16)
    others = mom_count - 1
    place_pack = jnp.stack([src, snk, mom, time_count, half_snk]).astype(jnp.int32)
    packed = pl.pallas_call(
        pack_kernel,
        in_specs=[smem()] * 3 + [anywhere()] * 2,
        out_specs=[anywhere()] * (3 + 2 * others),
        out_shape=[block_half, block_half, piece] + [piece] * others + [tagged] * others,
        scratch_shapes=[
            pltpu.VMEM((TAG_ROWS, nev), jnp.bfloat16),
            pltpu.SemaphoreType.DMA((3 + 3 * others,)),
        ],
        compiler_params=limit(4),
        name="pack",
    )(place_pack, separations, partner, peram_blocks, proj_rows)
    first, rest, piece_here = packed[:3]
    other, own = packed[3 : 3 + others], packed[3 + others :]

    first = swap_snk(first)
    rest_near, rest_far, flag = along_src(rest, peer_hops)
    other = [piece_here] + [swap_mom(array, i + 1) for i, array in enumerate(other)]
    own = [swap_mom(array, i + 1) for i, array in enumerate(own)]
    rest = swap_snk(jnp.where(flag != 0, rest_far, rest_near))
    here, away = [], []
    for array in other:
        near, far, _ = along_src(array, own_hops)
        here.append(near)
        away.append(far)
    first_near, first_far, cross = along_src(first, own_hops)

    scal = jnp.stack([mom, cross, forward, pair_time, sep_index, live]).astype(jnp.int32)
    where_own = jnp.stack([mom, keep]).astype(jnp.int32)
    blocks = (mom_count, NSPIN, width, 2 * nev)

    ht = pl.pallas_call(
        own_kernel,
        grid_spec=pltpu.PrefetchScalarGridSpec(
            num_scalar_prefetch=1,
            grid=(1,),
            in_specs=[
                smem(),
                pl.BlockSpec((1, 1, 2, width, width), lambda g, at: (at[0], at[1], 0, 0, 0)),
                pl.BlockSpec((1, rows, nev), lambda g, at: (at[0], 0, 0)),
            ]
            + [vmem()] * others,
            out_specs=vmem(),
            scratch_shapes=[
                pltpu.VMEM((NSPIN, width, 2 * nev), jnp.bfloat16),
                pltpu.VMEM((4 * nterm, 2 * nev, 2 * nev), jnp.bfloat16),
                pltpu.VMEM((mom_count, 2 * nterm, nev, nev), jnp.bfloat16),
            ],
        ),
        out_shape=jax.ShapeDtypeStruct(blocks, jnp.bfloat16),
        compiler_params=limit(20),
        name="own_products",
    )(where_own, gamma_index, peram_blocks, proj_rows, *own)

    k, label = pl.pallas_call(
        other_kernel,
        in_specs=[smem()] * 3 + [vmem()] * (1 + others + 2 * mom_count),
        out_specs=[vmem(), smem()],
        out_shape=[
            jax.ShapeDtypeStruct(blocks, jnp.float32),
            jax.ShapeDtypeStruct((2 * mom_count,), jnp.int32),
        ],
        scratch_shapes=[
            pltpu.VMEM((mom_count, rows, nev), jnp.bfloat16),
            pltpu.VMEM((4 * nterm, 2 * nev, 2 * nev), jnp.bfloat16),
        ],
        compiler_params=limit(24),
        name="other_products",
    )(scal, gamma_index, partner, ht, *own, *here, *away)

    sums = pl.pallas_call(
        early_kernel,
        in_specs=[smem()] + [vmem()] * 3,
        out_specs=vmem(),
        out_shape=jax.ShapeDtypeStruct((2 * mom_count, 16, nev), jnp.float32),
        compiler_params=limit(16),
        name="early_traces",
    )(scal, k, first_near, first_far)
    lines = pl.pallas_call(
        late_kernel,
        in_specs=[smem()] * 2 + [vmem()] * 3,
        out_specs=[vmem()] * mom_count,
        out_shape=[jax.ShapeDtypeStruct((time_count, 128), jnp.float32)] * mom_count,
        compiler_params=limit(16),
        name="late_traces",
    )(scal, label, k, rest, sums)

    total = lines[0]
    for i in range(1, mom_count):
        total = total + swap_mom(lines[i], i)
    step = 1
    while step < src_count:
        pairs = [(a, a ^ step) for a in range(src_count)]
        total = total + lax.ppermute(total, "src", pairs)
        step *= 2
    whole = total
    for step in range(1, snk_count):
        pairs = [(a, (a + step) % snk_count) for a in range(snk_count)]
        whole = whole + lax.ppermute(total, "snk", pairs)
    return whole[:, : 2 * sep_count].reshape(time_count, sep_count, 1, 2)


def solution(mesh):
    placed = (
        P("src", "snk", None, None, None),
        P("src", "mom", None, None, None, None),
        P(),
        P("mom"),
        P(),
    )
    return jax.shard_map(
        shards, mesh=mesh, in_specs=placed, out_specs=P(None, None, "mom", None), check_vma=False
    )
```

```python
import functools

import jax
import jax.numpy as jnp
from jax import lax
from jax.experimental import pallas as pl
from jax.experimental.pallas import tpu as pltpu
from jax.sharding import PartitionSpec as P

NSPIN = 4
NT_DIMS = (((1,), (1,)), ((), ()))
MIB = 1024 * 1024
WEIGHT = 10**13
TAG_ROWS = 16
GAMMAS = (
    (3, 1 | 1 << 2 | 3 << 4 | 3 << 6),
    (3, 2 | 0 << 2 | 0 << 4 | 2 << 6),
    (2, 1 | 3 << 2 | 3 << 4 | 1 << 6),
    (2, 0),
)


def spin_entry(code, row):
    phase = row * 0
    for bit, (flip, phases) in enumerate(GAMMAS):
        on = (code >> bit) & 1
        phase = phase + on * ((phases >> (2 * row)) & 3)
        row = row ^ (on * flip)
    return row, phase & 3


def spin_column_entry(code, column):
    row = column
    for bit, (flip, _) in enumerate(GAMMAS):
        row = row ^ (((code >> bit) & 1) * flip)
    return row, spin_entry(code, row)[1]


def phase_blocks(block_ref, r, real, imag):
    nev = real.shape[0]
    for phase, (a, b) in enumerate(((real, imag), (-imag, real), (-real, -imag), (imag, -real))):
        slot = 4 * r + phase
        block_ref[slot, :nev, :nev] = a
        block_ref[slot, :nev, nev:] = -b
        block_ref[slot, nev:, :nev] = b
        block_ref[slot, nev:, nev:] = a


class Plan:
    def __init__(self, place, seps, sizes):
        slices, offsets, src_count, snk_count = sizes
        src, snk, self.mom = place[0], place[1], place[2]
        half_snk = snk_count // 2
        self.slices, self.time_count = slices, slices * src_count
        self.forward = snk < half_snk
        base = lax.rem(snk, half_snk) * offsets
        self.keep = jnp.where(self.forward, 0, offsets - 1)
        self.give = offsets - 1 - self.keep
        self.sep_index = base + self.keep
        sign = jnp.where(self.forward, 1, -1)
        self.shift = sign * seps[base + self.keep]
        self.peer_shift = -sign * seps[base + self.give]
        self.own_time = src * slices + self.mom
        late = jnp.where(self.forward, 0, self.shift)
        self.pair_time = lax.rem(self.own_time + late + self.time_count, self.time_count)
        self.live = self.forward if offsets == 1 else None

    def _sum(self, place, amount):
        return lax.rem(place + amount + self.time_count, self.time_count)

    def local(self, i):
        return lax.rem(self._sum(self.mom ^ i, self.shift), self.slices)

    def hops(self, i):
        return lax.div(self._sum(self.mom ^ i, self.shift), self.slices)

    def peer_local(self):
        return lax.rem(self._sum(self.mom, self.peer_shift), self.slices)

    def peer_hops(self):
        return lax.div(self._sum(self.mom, self.peer_shift), self.slices)


def run_copies(copies, sems):
    handles = [
        pltpu.make_async_copy(source, target, sems.at[n])
        for n, (source, target) in enumerate(copies)
    ]
    for handle in handles:
        handle.start()
    for handle in handles:
        handle.wait()


def span(index, rows):
    return pl.ds(index * rows, rows)


def first_pack(sizes, place, seps, partner, peram, proj, first, rest, near, tag, sems):
    plan = Plan(place, seps, sizes)
    half, rows = first.shape[1], proj.shape[1]
    tag[...] = jnp.full(tag.shape, partner[0].astype(jnp.float32)).astype(jnp.bfloat16)
    peer, give, mom = plan.peer_local(), plan.give, plan.mom
    run_copies(
        [
            (peram.at[peer, give, :, pl.ds(0, half)], first),
            (peram.at[peer, give, :, pl.ds(half, half)], rest),
            (proj.at[plan.local(2)], near.at[span(0, rows)]),
            (proj.at[plan.local(3)], near.at[span(1, rows)]),
            (proj.at[mom ^ 2], near.at[span(2, rows)]),
            (proj.at[mom ^ 3], near.at[span(3, rows)]),
            (tag, near.at[pl.ds(4 * rows, TAG_ROWS)]),
        ],
        sems,
    )


def second_pack(sizes, place, seps, peram, proj, rest_near, rest_far, *refs):
    rest, far_same, far_cross, x_ref, sems = refs
    plan = Plan(place, seps, sizes)
    rows = proj.shape[1]
    flag = lax.rem(plan.peer_hops(), 2)

    @pl.when(flag == 0)
    def _():
        run_copies([(rest_near, rest)], sems)

    @pl.when(flag != 0)
    def _():
        run_copies([(rest_far, rest)], sems)

    run_copies(
        [
            (proj.at[plan.local(0)], far_same.at[span(0, rows)]),
            (proj.at[plan.local(1)], far_same.at[span(1, rows)]),
            (proj.at[plan.local(2)], far_cross.at[span(0, rows)]),
            (proj.at[plan.local(3)], far_cross.at[span(1, rows)]),
            (peram.at[plan.mom, plan.keep], x_ref),
        ],
        sems,
    )


def own_pack(place, partner, proj, near, out, tag, sems):
    rows = proj.shape[1]
    mom = place[2]
    tag[...] = jnp.full(tag.shape, partner[0].astype(jnp.float32)).astype(jnp.bfloat16)
    run_copies(
        [
            (proj.at[mom ^ 1], out.at[span(0, rows)]),
            (near.at[span(3, rows)], out.at[span(1, rows)]),
            (tag, out.at[pl.ds(2 * rows, TAG_ROWS)]),
            (near.at[pl.ds(4 * rows, TAG_ROWS)], out.at[pl.ds(2 * rows + TAG_ROWS, TAG_ROWS)]),
        ],
        sems,
    )


def other_pack(sizes, place, seps, proj, near, far_same, far_cross, after, out, sems):
    plan = Plan(place, seps, sizes)
    rows = proj.shape[1]
    flag = lax.rem(plan.hops(1), 2) if sizes[2] == 2 else jnp.int32(0)
    low, high = out.at[span(0, rows)], out.at[span(1, rows)]

    @pl.when(flag == 0)
    def _():
        run_copies([(proj.at[plan.local(1)], low), (near.at[span(1, rows)], high)], sems)

    @pl.when(flag != 0)
    def _():
        run_copies([(far_same.at[span(1, rows)], low), (far_cross.at[span(1, rows)], high)], sems)


def own_products(mom, gamma, pieces, p_ref, xb_ref, ht_ref, block_ref, tr_ref):
    nev = tr_ref.shape[-1]
    nterm = tr_ref.shape[0] // 2
    first, step = pieces[0], pieces[1] - pieces[0]

    def product(n, carry):
        for m in range(2 * nterm):
            tr_ref[m] = p_ref[n, m * nev : (m + 1) * nev].T
        for r in range(nterm):
            phase_blocks(block_ref, r, tr_ref[2 * r], tr_ref[2 * r + 1])

        def spin_rows(spin, inner):
            total = None
            for r in range(nterm):
                source, phase = spin_column_entry(gamma[mom ^ (first + n * step), r], spin)
                term = lax.dot_general(
                    block_ref[4 * r + phase],
                    xb_ref[source],
                    NT_DIMS,
                    preferred_element_type=jnp.float32,
                )
                total = term if total is None else total + term
            total = total.astype(jnp.bfloat16)
            rows = pl.ds(pl.multiple_of(spin * nev, nev), nev)
            for column in range(NSPIN):
                lanes = slice(column * nev, (column + 1) * nev)
                ht_ref[n, column, rows, :nev] = total[:nev, lanes]
                ht_ref[n, column, rows, nev:] = total[nev:, lanes]
            return inner

        return lax.fori_loop(0, NSPIN, spin_rows, carry)

    lax.fori_loop(0, len(pieces), product, 0)


def own_kernel_a(place, gamma, block, proj, near, *refs):
    ht_ref, xb_ref, x_ref, p_ref, block_ref, tr_ref, sems = refs[-7:]
    mom = place[2]
    nev = tr_ref.shape[-1]
    rows = proj.shape[1]
    run_copies(
        [
            (block, x_ref),
            (proj.at[mom], p_ref.at[0]),
            (near.at[span(2, rows)], p_ref.at[1]),
        ],
        sems,
    )
    for spin in range(NSPIN):
        lanes = slice(spin * nev, (spin + 1) * nev)
        xb_ref[spin, :, :nev] = x_ref[0, :, lanes]
        xb_ref[spin, :, nev:] = x_ref[1, :, lanes]
    own_products(mom, gamma, (0, 2), p_ref, xb_ref, ht_ref, block_ref, tr_ref)


def own_kernel_b(place, gamma, xb_ref, traded, ht_ref, p_ref, block_ref, tr_ref, sems):
    rows = p_ref.shape[1]
    run_copies([(traded.at[span(n, rows)], p_ref.at[n]) for n in range(2)], sems)
    own_products(place[2], gamma, (1, 3), p_ref, xb_ref, ht_ref, block_ref, tr_ref)


def other_products(mom, forward, gamma, partner, near_tag, own_tag, pieces, hts, p_ref, refs):
    k_ref, label_ref, ht_ref, block_ref = refs
    nev = block_ref.shape[-1] // 2
    nterm = block_ref.shape[0] // 4

    def number(tag):
        return jnp.max(tag.astype(jnp.float32)).astype(jnp.int32)

    partners = [
        partner[0],
        number(own_tag[:TAG_ROWS]),
        number(near_tag[...]),
        number(own_tag[TAG_ROWS:]),
    ]
    lefts = []
    for n, p in enumerate(pieces):
        back = jnp.int32(0)
        for i, value in enumerate(partners):
            back = back + jnp.where(value == (mom ^ p), mom ^ i, 0)
        label_ref[n] = jnp.where(forward, back, mom ^ p)
        lefts.append(jnp.where(forward, back, partners[p]) ^ mom)
    first, step = pieces[0], pieces[1] - pieces[0]

    def product(n, carry):
        for r in range(nterm):
            real = p_ref[n, 2 * r * nev : (2 * r + 1) * nev]
            imag = p_ref[n, (2 * r + 1) * nev : (2 * r + 2) * nev]
            phase_blocks(block_ref, r, real, imag)
        left = jnp.where(n == 0, lefts[0], lefts[1])
        for odd in range(2):

            @pl.when((left & 1) == odd)
            def _():
                ht_ref[...] = hts[odd][left >> 1]

        def spin_columns(spin, inner):
            total = None
            for r in range(nterm):
                source, phase = spin_entry(gamma[mom ^ (first + n * step), r], spin)
                term = lax.dot_general(
                    ht_ref[source],
                    block_ref[4 * r + phase],
                    NT_DIMS,
                    preferred_element_type=jnp.float32,
                )
                total = term if total is None else total + term
            k_ref[n, spin] = total
            return inner

        return lax.fori_loop(0, NSPIN, spin_columns, carry)

    lax.fori_loop(0, len(pieces), product, 0)


def read_tags(near, own, near_tag, own_tag, rows, sems):
    run_copies(
        [
            (near.at[pl.ds(4 * rows, TAG_ROWS)], near_tag),
            (own.at[pl.ds(2 * rows, 2 * TAG_ROWS)], own_tag),
        ],
        sems,
    )


def other_kernel_a(sizes, place, seps, gamma, partner, hta, htb, proj, near, own, *refs):
    far_same, far_cross = refs[:2]
    k_ref, label_ref, ht_ref, block_ref, p_ref, near_tag, own_tag, sems = refs[-8:]
    plan = Plan(place, seps, sizes)
    rows = proj.shape[1]
    read_tags(near, own, near_tag, own_tag, rows, sems)
    flag = lax.rem(plan.hops(0), 2) if sizes[2] == 2 else jnp.int32(1)

    @pl.when(flag == 0)
    def _():
        run_copies(
            [(proj.at[plan.local(0)], p_ref.at[0]), (near.at[span(0, rows)], p_ref.at[1])], sems
        )

    @pl.when(flag != 0)
    def _():
        run_copies(
            [(far_same.at[span(0, rows)], p_ref.at[0]), (far_cross.at[span(0, rows)], p_ref.at[1])],
            sems,
        )

    out = (k_ref, label_ref, ht_ref, block_ref)
    other_products(
        plan.mom, plan.forward, gamma, partner, near_tag, own_tag, (0, 2), (hta, htb), p_ref, out
    )


def other_kernel_b(sizes, place, seps, gamma, partner, hta, htb, near, own, traded, *refs):
    k_ref, label_ref, ht_ref, block_ref, p_ref, near_tag, own_tag, sems = refs
    plan = Plan(place, seps, sizes)
    rows = p_ref.shape[1]
    read_tags(near, own, near_tag, own_tag, rows, sems)
    run_copies([(traded.at[span(n, rows)], p_ref.at[n]) for n in range(2)], sems)
    out = (k_ref, label_ref, ht_ref, block_ref)
    other_products(
        plan.mom, plan.forward, gamma, partner, near_tag, own_tag, (1, 3), (hta, htb), p_ref, out
    )


def row_sums(k_refs, source, offset, totals):
    rows = 16
    each = k_refs[0].shape[0]
    nev = source.shape[-1] // NSPIN

    def step(index, totals):
        row = pl.multiple_of(index * rows, rows)
        here = pl.ds(pl.multiple_of(offset + row, rows), rows)
        totals = list(totals)
        for spin in range(NSPIN):
            lanes = slice(spin * nev, (spin + 1) * nev)
            real = source[0, pl.ds(row, rows), lanes].astype(jnp.float32)
            imag = source[1, pl.ds(row, rows), lanes].astype(jnp.float32)
            for n in range(len(totals) // 2):
                k_ref, p = k_refs[n // each], n % each
                kr, ki = k_ref[p, spin, here, :nev], k_ref[p, spin, here, nev:]
                totals[2 * n] += real * kr - imag * ki
                totals[2 * n + 1] += real * ki + imag * kr
        return tuple(totals)

    return lax.fori_loop(0, source.shape[1] // rows, step, totals)


def early_kernel(sizes, place, seps, ka, kb, near, far, sums_ref, part_ref, sems):
    plan = Plan(place, seps, sizes)
    count = sums_ref.shape[0]
    flag = lax.rem(lax.div(plan.hops(0), max(sizes[2] // 2, 1)), 2)

    @pl.when(flag == 0)
    def _():
        run_copies([(near, part_ref)], sems)

    @pl.when(flag != 0)
    def _():
        run_copies([(far, part_ref)], sems)

    zero = tuple(jnp.zeros(sums_ref.shape[1:], jnp.float32) for _ in range(count))
    for n, total in enumerate(row_sums((ka, kb), part_ref, 0, zero)):
        sums_ref[n] = total


def late_kernel(sizes, sep_count, place, seps, label_a, label_b, ka, kb, rest_ref, sums_ref, out_ref):
    plan = Plan(place, seps, sizes)
    count = sums_ref.shape[0] // 2
    width = rest_ref.shape[-1]
    half = ka.shape[2] - rest_ref.shape[1]
    totals = row_sums((ka, kb), rest_ref, half, tuple(sums_ref[n] for n in range(2 * count)))
    sums = [jnp.sum(total, axis=0, keepdims=True) for total in totals]
    sums = [jnp.sum(total, axis=1, keepdims=True) * (1.0 / width) for total in sums]
    shape = out_ref.shape[1:]
    spot = lax.broadcasted_iota(jnp.int32, shape, 0) * shape[1]
    spot = spot + lax.broadcasted_iota(jnp.int32, shape, 1)
    here = spot // 2 == plan.pair_time * sep_count + plan.sep_index
    if plan.live is not None:
        here = here & plan.live
    values = [jnp.where(spot % 2 == 0, sums[2 * p], sums[2 * p + 1]) for p in range(count)]
    labels = [label_a[0], label_a[1], label_b[0], label_b[1]]
    lines = []
    for op in range(count):
        line = jnp.zeros(shape, jnp.float32)
        for p in range(count):
            line = jnp.where(labels[p] == op, values[p], line)
        lines.append(jnp.where(here, line, 0.0))
    for n in range(out_ref.shape[0]):
        out_ref[n] = lines[n % count]


def smem():
    return pl.BlockSpec(memory_space=pltpu.SMEM)


def vmem():
    return pl.BlockSpec(memory_space=pltpu.VMEM)


def hbm():
    return pl.BlockSpec(memory_space=pltpu.HBM)


def limit(mib):
    return pltpu.CompilerParams(vmem_limit_bytes=mib * MIB)


def shards(peram_blocks, projections, gamma_index, partner, separations):
    src_count, snk_count = lax.axis_size("src"), lax.axis_size("snk")
    mom_count = lax.axis_size("mom")
    slices, offsets = peram_blocks.shape[:2]
    width = peram_blocks.shape[-1]
    nterm, nev = projections.shape[2], projections.shape[-1]
    time_count = slices * src_count
    sep_count = separations.shape[0]
    half_snk = snk_count // 2
    half_rows = width // 2
    rows = nterm * 2 * nev
    sizes = (slices, offsets, src_count, snk_count)
    place = jnp.stack([lax.axis_index(name) for name in ("src", "snk", "mom")]).astype(jnp.int32)
    proj = projections.reshape(slices, rows, nev)

    def swap_mom(array, i):
        return lax.ppermute(array, "mom", [(a, a ^ i) for a in range(mom_count)])

    def swap_snk(array):
        pairs = [(a, (a + half_snk) % snk_count) for a in range(snk_count)]
        return lax.ppermute(array, "snk", pairs)

    def next_src(array, step=1, i=0):
        pairs = [
            (((a + step) % src_count) * mom_count + (b ^ i), a * mom_count + b)
            for a in range(src_count)
            for b in range(mom_count)
        ]
        return lax.ppermute(array, ("src", "mom"), pairs)

    def most_of(array, amount):
        step = 1
        while 2 * step < src_count:
            array = jnp.where((amount // step) % 2 != 0, next_src(array, step), array)
            step *= 2
        return array, next_src(array, step)

    def call(kernel, name, in_specs, out_specs, out_shape, scratch, mib):
        cost = pl.CostEstimate(flops=WEIGHT, bytes_accessed=WEIGHT // 1000, transcendentals=0)
        return pl.pallas_call(
            kernel,
            in_specs=in_specs,
            out_specs=out_specs,
            out_shape=out_shape,
            scratch_shapes=scratch,
            compiler_params=limit(mib),
            cost_estimate=cost,
            name=name,
        )

    def bf16(*shape):
        return jax.ShapeDtypeStruct(shape, jnp.bfloat16)

    def dma(count):
        return pltpu.SemaphoreType.DMA((count,))

    part = functools.partial
    tag = pltpu.VMEM((TAG_ROWS, nev), jnp.bfloat16)
    half_block = bf16(2, half_rows, width)
    two = bf16(2 * rows, nev)

    first, rest, near = call(
        part(first_pack, sizes),
        "first_pack",
        [smem()] * 3 + [hbm()] * 2,
        [hbm()] * 3,
        [half_block, half_block, bf16(4 * rows + TAG_ROWS, nev)],
        [tag, dma(7)],
        58,
    )(place, separations, partner, peram_blocks, proj)

    plan = Plan(place, separations, sizes)
    first = swap_snk(first)
    rest_near, rest_far = most_of(rest, plan.peer_hops())
    near = swap_mom(near, 2)
    if src_count > 2:
        rest_near = jnp.where(plan.peer_hops() // (src_count // 2) != 0, rest_far, rest_near)
        rest_far = rest_near
    rest, far_same, far_cross, x = call(
        part(second_pack, sizes),
        "second_pack",
        [smem()] * 2 + [hbm()] * 4,
        [hbm()] * 4,
        [half_block, two, two, bf16(2, width, width)],
        [dma(5)],
        58,
    )(place, separations, peram_blocks, proj, rest_near, rest_far)
    rest = swap_snk(rest)
    if src_count == 2:
        far_same, far_cross = next_src(far_same), next_src(far_cross, 1, 2)

    own_trade = call(
        own_pack,
        "own_pack",
        [smem()] * 2 + [hbm()] * 2,
        hbm(),
        bf16(2 * (rows + TAG_ROWS), nev),
        [tag, dma(4)],
        16,
    )(place, partner, proj, near)
    own_got = swap_mom(own_trade, 1)
    first_near, first_far = most_of(first, plan.hops(0))

    blocks = (mom_count // 2, NSPIN, width, 2 * nev)
    weights = pltpu.VMEM((4 * nterm, 2 * nev, 2 * nev), jnp.bfloat16)
    pieces = pltpu.VMEM((2, rows, nev), jnp.bfloat16)
    turned = pltpu.VMEM((2 * nterm, nev, nev), jnp.bfloat16)
    hta, xb = call(
        own_kernel_a,
        "own_products_a",
        [smem()] * 2 + [hbm()] * 5,
        [vmem()] * 2,
        [bf16(*blocks), bf16(NSPIN, width, 2 * nev)],
        [pltpu.VMEM((2, width, width), jnp.bfloat16), pieces, weights, turned, dma(3)],
        16,
    )(place, gamma_index, x, proj, near, own_trade, first)
    htb = call(
        own_kernel_b,
        "own_products_b",
        [smem()] * 2 + [vmem(), hbm()],
        vmem(),
        bf16(*blocks),
        [pieces, weights, turned, dma(2)],
        16,
    )(place, gamma_index, xb, own_got)

    other_trade = call(
        part(other_pack, sizes),
        "other_pack",
        [smem()] * 2 + [hbm()] * 5,
        hbm(),
        two,
        [dma(2)],
        16,
    )(place, separations, proj, near, far_same, far_cross, htb)
    other_got = swap_mom(other_trade, 1)
    if src_count != 2:

        def moved(array):
            if src_count == 1:
                return array
            array, far = most_of(array, plan.hops(0))
            return jnp.where(plan.hops(0) // (src_count // 2) != 0, far, array)

        far_same = moved(lax.dynamic_index_in_dim(proj, plan.local(0), 0, keepdims=False))
        far_cross, other_got = moved(near[:rows]), moved(other_got)

    chosen = pltpu.VMEM((NSPIN, width, 2 * nev), jnp.bfloat16)
    own_tag = pltpu.VMEM((2 * TAG_ROWS, nev), jnp.bfloat16)
    k_out = [
        jax.ShapeDtypeStruct(blocks, jnp.float32),
        jax.ShapeDtypeStruct((mom_count // 2,), jnp.int32),
    ]
    scratch = [chosen, weights, pieces, tag, own_tag, dma(2)]
    ka, label_a = call(
        part(other_kernel_a, sizes),
        "other_products_a",
        [smem()] * 4 + [vmem()] * 2 + [hbm()] * 6,
        [vmem(), smem()],
        k_out,
        scratch,
        24,
    )(
        place, separations, gamma_index, partner, hta, htb,
        proj, near, own_got, far_same, far_cross, other_trade,
    )
    kb, label_b = call(
        part(other_kernel_b, sizes),
        "other_products_b",
        [smem()] * 4 + [vmem()] * 2 + [hbm()] * 3,
        [vmem(), smem()],
        k_out,
        scratch,
        24,
    )(place, separations, gamma_index, partner, hta, htb, near, own_got, other_got)

    sums = call(
        part(early_kernel, sizes),
        "early_traces",
        [smem()] * 2 + [vmem()] * 2 + [hbm()] * 2,
        vmem(),
        jax.ShapeDtypeStruct((2 * mom_count, 16, nev), jnp.float32),
        [pltpu.VMEM((2, half_rows, width), jnp.bfloat16), dma(1)],
        20,
    )(place, separations, ka, kb, first_near, first_far)
    device_count = src_count * snk_count * mom_count
    values = time_count * sep_count * 2
    lines = (values + 127) // 128
    out = call(
        part(late_kernel, sizes, sep_count),
        "late_traces",
        [smem()] * 4 + [vmem()] * 4,
        vmem(),
        jax.ShapeDtypeStruct((device_count, lines, 128), jnp.float32),
        [],
        20,
    )(place, separations, label_a, label_b, ka, kb, rest, sums)
    out = lax.all_to_all(out, ("src", "snk", "mom"), split_axis=0, concat_axis=0, tiled=True)
    out = jnp.sum(out, axis=0).reshape(lines * 128)[:values]
    return out.reshape(time_count, sep_count, 1, 2)


def solution(mesh):
    placed = (
        P("src", "snk", None, None, None),
        P("src", "mom", None, None, None, None),
        P(),
        P("mom"),
        P(),
    )
    return jax.shard_map(
        shards, mesh=mesh, in_specs=placed, out_specs=P(None, None, "mom", None), check_vma=False
    )
```

```python
import functools

import jax
import jax.numpy as jnp
from jax import lax
from jax.experimental import pallas as pl
from jax.experimental.pallas import tpu as pltpu
from jax.sharding import PartitionSpec as P

NSPIN = 4
NT_DIMS = (((1,), (1,)), ((), ()))
MIB = 1024 * 1024
WEIGHT = 10**13
TAG_ROWS = 16
TILE = 256
GAMMAS = (
    (3, 1 | 1 << 2 | 3 << 4 | 3 << 6),
    (3, 2 | 0 << 2 | 0 << 4 | 2 << 6),
    (2, 1 | 3 << 2 | 3 << 4 | 1 << 6),
    (2, 0),
)


def spin_entry(code, row):
    phase = row * 0
    for bit, (flip, phases) in enumerate(GAMMAS):
        on = (code >> bit) & 1
        phase = phase + on * ((phases >> (2 * row)) & 3)
        row = row ^ (on * flip)
    return row, phase & 3


def mask_of(code):
    mask = code * 0
    for bit, (flip, _) in enumerate(GAMMAS):
        mask = mask ^ (((code >> bit) & 1) * flip)
    return mask


def fill_spin_blocks(codes, turns, zero, write):
    nterm = len(codes)
    masks = [mask_of(code) for code in codes]
    for mask in range(NSPIN):
        missing = masks[0] != mask
        for r in range(1, nterm):
            missing = missing & (masks[r] != mask)

        @pl.when(missing)
        def _():
            for spin in range(NSPIN):
                zero(spin, spin ^ mask)

    for r in range(nterm):

        def term(add):
            for spin in range(NSPIN):
                column, phase = spin_entry(codes[r], spin)
                a, b, minus_b = (turns[r, (n - phase) & 3] for n in (4, 1, 3))
                write(spin, column, a, b, minus_b, add)

        if r == 0:
            term(False)
            continue
        met = masks[0] == masks[r]
        for before in range(1, r):
            met = met | (masks[before] == masks[r])
        pl.when(met)(lambda: term(True))
        pl.when(jnp.logical_not(met))(lambda: term(False))


def set_turns(turns, r, real, imag):
    for n, value in enumerate((real, imag, -real, -imag)):
        turns[r, n] = value


def put(ref, rows, lanes, value, add):
    if add:
        value = (ref[rows, lanes].astype(jnp.float32) + value.astype(jnp.float32)).astype(ref.dtype)
    ref[rows, lanes] = value


def along(spin, nev, start=0):
    if isinstance(spin, int):
        return slice(start + spin * nev, start + (spin + 1) * nev)
    return pl.ds(pl.multiple_of(start + spin * nev, nev), nev)


class Plan:
    def __init__(self, place, seps, sizes):
        slices, offsets, src_count, snk_count = sizes
        src, snk, self.mom = place[0], place[1], place[2]
        half_snk = snk_count // 2
        self.slices, self.time_count = slices, slices * src_count
        self.forward = snk < half_snk
        base = lax.rem(snk, half_snk) * offsets
        self.keep = jnp.where(self.forward, 0, offsets - 1)
        self.give = offsets - 1 - self.keep
        self.sep_index = base + self.keep
        sign = jnp.where(self.forward, 1, -1)
        self.shift = sign * seps[base + self.keep]
        self.peer_shift = -sign * seps[base + self.give]
        self.own_time = src * slices + self.mom
        late = jnp.where(self.forward, 0, self.shift)
        self.pair_time = lax.rem(self.own_time + late + self.time_count, self.time_count)
        self.live = self.forward if offsets == 1 else None

    def _sum(self, place, amount):
        return lax.rem(place + amount + self.time_count, self.time_count)

    def local(self, i):
        return lax.rem(self._sum(self.mom ^ i, self.shift), self.slices)

    def hops(self, i):
        return lax.div(self._sum(self.mom ^ i, self.shift), self.slices)

    def peer_local(self):
        return lax.rem(self._sum(self.mom, self.peer_shift), self.slices)

    def peer_hops(self):
        return lax.div(self._sum(self.mom, self.peer_shift), self.slices)


def run_copies(copies, sems):
    handles = [
        pltpu.make_async_copy(source, target, sems.at[n])
        for n, (source, target) in enumerate(copies)
    ]
    for handle in handles:
        handle.start()
    for handle in handles:
        handle.wait()


def span(index, rows):
    return pl.ds(index * rows, rows)


def first_pack(sizes, place, seps, partner, peram, proj, first, rest, near, sems):
    plan = Plan(place, seps, sizes)
    split, rows = first.shape[1], proj.shape[1]
    peer, give, mom = plan.peer_local(), plan.give, plan.mom
    number = jnp.full((TAG_ROWS, near.shape[-1]), partner[0].astype(jnp.float32))
    near[pl.ds(4 * rows, TAG_ROWS), :] = number.astype(jnp.bfloat16)
    run_copies(
        [
            (peram.at[peer, give, :, pl.ds(0, split)], first),
            (peram.at[peer, give, :, pl.ds(split, rest.shape[1])], rest),
            (proj.at[plan.local(2)], near.at[span(0, rows)]),
            (proj.at[plan.local(3)], near.at[span(1, rows)]),
            (proj.at[mom ^ 2], near.at[span(2, rows)]),
            (proj.at[mom ^ 3], near.at[span(3, rows)]),
        ],
        sems,
    )


def second_pack(sizes, place, seps, proj, rest_near, rest_far, after, *refs):
    rest, far_same, far_cross, sems = refs
    plan = Plan(place, seps, sizes)
    rows = proj.shape[1]
    flag = lax.rem(plan.peer_hops(), 2)
    copies = [
        (proj.at[plan.local(0)], far_same.at[span(0, rows)]),
        (proj.at[plan.local(1)], far_same.at[span(1, rows)]),
        (proj.at[plan.local(2)], far_cross.at[span(0, rows)]),
        (proj.at[plan.local(3)], far_cross.at[span(1, rows)]),
    ]

    @pl.when(flag == 0)
    def _():
        run_copies([(rest_near, rest)] + copies, sems)

    @pl.when(flag != 0)
    def _():
        run_copies([(rest_far, rest)] + copies, sems)


def own_pack(place, partner, proj, near, out, sems):
    rows = proj.shape[1]
    mom = place[2]
    number = jnp.full((TAG_ROWS, out.shape[-1]), partner[0].astype(jnp.float32))
    out[pl.ds(2 * rows, TAG_ROWS), :] = number.astype(jnp.bfloat16)
    run_copies(
        [
            (proj.at[mom ^ 1], out.at[span(0, rows)]),
            (near.at[span(3, rows)], out.at[span(1, rows)]),
            (near.at[pl.ds(4 * rows, TAG_ROWS)], out.at[pl.ds(2 * rows + TAG_ROWS, TAG_ROWS)]),
        ],
        sems,
    )


def other_pack(sizes, place, seps, proj, near, far_same, far_cross, after, out, sems):
    plan = Plan(place, seps, sizes)
    rows = proj.shape[1]
    flag = lax.rem(plan.hops(1), 2) if sizes[2] == 2 else jnp.int32(0)
    low, high = out.at[span(0, rows)], out.at[span(1, rows)]

    @pl.when(flag == 0)
    def _():
        run_copies([(proj.at[plan.local(1)], low), (near.at[span(1, rows)], high)], sems)

    @pl.when(flag != 0)
    def _():
        run_copies([(far_same.at[span(1, rows)], low), (far_cross.at[span(1, rows)], high)], sems)


def own_product(codes, p_ref, n, y_ref, ht, u_ref, turns):
    nterm = len(codes)
    nev = turns.shape[-1]
    width = u_ref.shape[0]
    for r in range(nterm):
        real, imag = (p_ref[n, m * nev : (m + 1) * nev].T for m in (2 * r, 2 * r + 1))
        set_turns(turns, r, real, imag)

    def zero(spin, column):
        empty = jnp.zeros((nev, nev), jnp.bfloat16)
        u_ref[along(column, nev), along(spin, nev)] = empty
        u_ref[along(column, nev), along(spin, nev, width)] = empty

    def write(spin, column, a, b, minus_b, add):
        put(u_ref, along(column, nev), along(spin, nev), a, add)
        put(u_ref, along(column, nev), along(spin, nev, width), b, add)

    fill_spin_blocks(codes, turns, zero, write)
    for tile in range(2 * width // TILE):
        lanes = slice(tile * TILE, (tile + 1) * TILE)
        out = lax.dot_general(
            u_ref[...], y_ref[lanes, :], NT_DIMS, preferred_element_type=jnp.float32
        )
        ht[:, lanes] = out.astype(jnp.bfloat16)


def codes_of(gamma, op, nterm):
    return [gamma[op, r] for r in range(nterm)]


def own_kernel_0(sizes, place, seps, gamma, peram, proj, y_ref, ht, x_ref, p_ref, u_ref, turns, sems):
    plan = Plan(place, seps, sizes)
    run_copies(
        [(peram.at[plan.mom, plan.keep], x_ref), (proj.at[plan.mom], p_ref.at[0])], sems
    )
    width = x_ref.shape[-1]
    real, imag = x_ref[0], x_ref[1]
    y_ref[:width, :width] = real
    y_ref[:width, width:] = -imag
    y_ref[width:, :width] = imag
    y_ref[width:, width:] = real
    codes = codes_of(gamma, plan.mom, turns.shape[0])
    own_product(codes, p_ref, 0, y_ref, ht, u_ref, turns)


def own_kernel_2(place, gamma, near, y_ref, first, traded, ht, p_ref, u_ref, turns, sems):
    rows = p_ref.shape[1]
    run_copies([(near.at[span(2, rows)], p_ref.at[0])], sems)
    codes = codes_of(gamma, place[2] ^ 2, turns.shape[0])
    own_product(codes, p_ref, 0, y_ref, ht, u_ref, turns)


def own_kernel_13(sizes, place, seps, gamma, partner, near, traded, y_ref, *refs):
    ht, label, p_ref, u_ref, turns, near_tag, own_tag, sems = refs
    plan = Plan(place, seps, sizes)
    mom = plan.mom
    rows = p_ref.shape[1]
    run_copies(
        [
            (traded.at[span(0, rows)], p_ref.at[0]),
            (traded.at[span(1, rows)], p_ref.at[1]),
            (traded.at[pl.ds(2 * rows, 2 * TAG_ROWS)], own_tag),
            (near.at[pl.ds(4 * rows, TAG_ROWS)], near_tag),
        ],
        sems,
    )

    def number(tag):
        return jnp.max(tag.astype(jnp.float32)).astype(jnp.int32)

    partners = [
        partner[0],
        number(own_tag[:TAG_ROWS]),
        number(near_tag[...]),
        number(own_tag[TAG_ROWS:]),
    ]
    for p in range(len(partners)):
        back = jnp.int32(0)
        for i, value in enumerate(partners):
            back = back + jnp.where(value == (mom ^ p), mom ^ i, 0)
        label[p] = jnp.where(plan.forward, back, mom ^ p)
        label[len(partners) + p] = jnp.where(plan.forward, back, partners[p]) ^ mom

    def step(n, carry):
        codes = codes_of(gamma, mom ^ (1 + 2 * n), turns.shape[0])
        own_product(codes, p_ref, n, y_ref, ht.at[n], u_ref, turns)
        return carry

    lax.fori_loop(0, 2, step, 0)


def other_products(mom, gamma, label, first, hts, refs):
    k_ref, p_ref, ht_ref, v_ref, turns = refs
    nterm, nev = turns.shape[0], turns.shape[-1]
    width = ht_ref.shape[0]
    h0, h2, h13 = hts

    def zero(spin, column):
        empty = jnp.zeros((nev, nev), jnp.bfloat16)
        for top in (0, width):
            for left in (0, width):
                v_ref[along(spin, nev, top), along(column, nev, left)] = empty

    def write(spin, column, a, b, minus_b, add):
        put(v_ref, along(spin, nev), along(column, nev), a, add)
        put(v_ref, along(spin, nev), along(column, nev, width), minus_b, add)
        put(v_ref, along(spin, nev, width), along(column, nev), b, add)
        put(v_ref, along(spin, nev, width), along(column, nev, width), a, add)

    def step(n, carry):
        left = label[4 + first + 2 * n]
        for index, source in enumerate((h0, h13.at[0], h2, h13.at[1])):

            @pl.when(left == index)
            def _():
                ht_ref[...] = source[...]

        for r in range(nterm):
            real, imag = (p_ref[n, m * nev : (m + 1) * nev] for m in (2 * r, 2 * r + 1))
            set_turns(turns, r, real, imag)
        fill_spin_blocks(codes_of(gamma, mom ^ (first + 2 * n), nterm), turns, zero, write)
        for tile in range(2 * width // TILE):
            lanes = slice(tile * TILE, (tile + 1) * TILE)
            k_ref[n, :, lanes] = lax.dot_general(
                ht_ref[...], v_ref[lanes, :], NT_DIMS, preferred_element_type=jnp.float32
            )
        return carry

    lax.fori_loop(0, 2, step, 0)


def other_kernel_02(sizes, place, seps, gamma, label, h0, h2, h13, proj, near, *refs):
    far_same, far_cross = refs[:2]
    k_ref, p_ref, ht_ref, v_ref, turns, sems = refs[-6:]
    plan = Plan(place, seps, sizes)
    rows = proj.shape[1]
    flag = lax.rem(plan.hops(0), 2) if sizes[2] == 2 else jnp.int32(1)

    @pl.when(flag == 0)
    def _():
        run_copies(
            [(proj.at[plan.local(0)], p_ref.at[0]), (near.at[span(0, rows)], p_ref.at[1])], sems
        )

    @pl.when(flag != 0)
    def _():
        run_copies(
            [(far_same.at[span(0, rows)], p_ref.at[0]), (far_cross.at[span(0, rows)], p_ref.at[1])],
            sems,
        )

    out = (k_ref, p_ref, ht_ref, v_ref, turns)
    other_products(plan.mom, gamma, label, 0, (h0, h2, h13), out)


def other_kernel_13(place, gamma, label, h0, h2, h13, traded, *refs):
    k_ref, p_ref, ht_ref, v_ref, turns, sems = refs
    rows = p_ref.shape[1]
    run_copies([(traded.at[span(n, rows)], p_ref.at[n]) for n in range(2)], sems)
    out = (k_ref, p_ref, ht_ref, v_ref, turns)
    other_products(place[2], gamma, label, 1, (h0, h2, h13), out)


def row_sums(k_refs, source, offset, totals):
    rows = 16
    each = k_refs[0].shape[0]
    width = source.shape[-1]
    nev = totals[0].shape[-1]

    def step(index, totals):
        row = pl.multiple_of(index * rows, rows)
        here = pl.ds(pl.multiple_of(offset + row, rows), rows)
        totals = list(totals)
        for spin in range(NSPIN):
            lanes, later = along(spin, nev), along(spin, nev, width)
            real = source[0, pl.ds(row, rows), lanes].astype(jnp.float32)
            imag = source[1, pl.ds(row, rows), lanes].astype(jnp.float32)
            for n in range(len(totals) // 2):
                k_ref, p = k_refs[n // each], n % each
                kr, ki = k_ref[p, here, lanes], k_ref[p, here, later]
                totals[2 * n] += real * kr - imag * ki
                totals[2 * n + 1] += real * ki + imag * kr
        return tuple(totals)

    return lax.fori_loop(0, source.shape[1] // rows, step, totals)


def early_kernel(sizes, place, seps, ka, kb, near, far, sums_ref, part_ref, sems):
    plan = Plan(place, seps, sizes)
    count = sums_ref.shape[0]
    flag = lax.rem(lax.div(plan.hops(0), max(sizes[2] // 2, 1)), 2)

    @pl.when(flag == 0)
    def _():
        run_copies([(near, part_ref)], sems)

    @pl.when(flag != 0)
    def _():
        run_copies([(far, part_ref)], sems)

    zero = tuple(jnp.zeros(sums_ref.shape[1:], jnp.float32) for _ in range(count))
    for n, total in enumerate(row_sums((ka, kb), part_ref, 0, zero)):
        sums_ref[n] = total


def late_kernel(sizes, sep_count, place, seps, label, ka, kb, rest_ref, sums_ref, out_ref):
    plan = Plan(place, seps, sizes)
    count = sums_ref.shape[0] // 2
    width = rest_ref.shape[-1]
    start = ka.shape[1] - rest_ref.shape[1]
    totals = row_sums((ka, kb), rest_ref, start, tuple(sums_ref[n] for n in range(2 * count)))
    sums = [jnp.sum(total, axis=0, keepdims=True) for total in totals]
    sums = [jnp.sum(total, axis=1, keepdims=True) * (1.0 / width) for total in sums]
    shape = out_ref.shape[1:]
    spot = lax.broadcasted_iota(jnp.int32, shape, 0) * shape[1]
    spot = spot + lax.broadcasted_iota(jnp.int32, shape, 1)
    here = spot // 2 == plan.pair_time * sep_count + plan.sep_index
    if plan.live is not None:
        here = here & plan.live
    values = [jnp.where(spot % 2 == 0, sums[2 * p], sums[2 * p + 1]) for p in range(count)]
    pieces = (0, 2, 1, 3)
    lines = []
    for op in range(count):
        line = jnp.zeros(shape, jnp.float32)
        for value, p in zip(values, pieces):
            line = jnp.where(label[p] == op, value, line)
        lines.append(jnp.where(here, line, 0.0))
    for n in range(out_ref.shape[0]):
        out_ref[n] = lines[n % count]


def smem():
    return pl.BlockSpec(memory_space=pltpu.SMEM)


def vmem():
    return pl.BlockSpec(memory_space=pltpu.VMEM)


def hbm():
    return pl.BlockSpec(memory_space=pltpu.HBM)


def limit(mib):
    return pltpu.CompilerParams(vmem_limit_bytes=mib * MIB)


def shards(peram_blocks, projections, gamma_index, partner, separations):
    src_count, snk_count = lax.axis_size("src"), lax.axis_size("snk")
    mom_count = lax.axis_size("mom")
    slices, offsets = peram_blocks.shape[:2]
    width = peram_blocks.shape[-1]
    nterm, nev = projections.shape[2], projections.shape[-1]
    time_count = slices * src_count
    sep_count = separations.shape[0]
    half_snk = snk_count // 2
    rows = nterm * 2 * nev
    sizes = (slices, offsets, src_count, snk_count)
    place = jnp.stack([lax.axis_index(name) for name in ("src", "snk", "mom")]).astype(jnp.int32)
    proj = projections.reshape(slices, rows, nev)

    def swap_mom(array, i):
        return lax.ppermute(array, "mom", [(a, a ^ i) for a in range(mom_count)])

    def swap_snk(array):
        pairs = [(a, (a + half_snk) % snk_count) for a in range(snk_count)]
        return lax.ppermute(array, "snk", pairs)

    def next_src(array, step=1, i=0):
        pairs = [
            (((a + step) % src_count) * mom_count + (b ^ i), a * mom_count + b)
            for a in range(src_count)
            for b in range(mom_count)
        ]
        return lax.ppermute(array, ("src", "mom"), pairs)

    def most_of(array, amount):
        step = 1
        while 2 * step < src_count:
            array = jnp.where((amount // step) % 2 != 0, next_src(array, step), array)
            step *= 2
        return array, next_src(array, step)

    def call(kernel, name, in_specs, out_specs, out_shape, scratch, mib):
        cost = pl.CostEstimate(flops=WEIGHT, bytes_accessed=WEIGHT // 1000, transcendentals=0)
        return pl.pallas_call(
            kernel,
            in_specs=in_specs,
            out_specs=out_specs,
            out_shape=out_shape,
            scratch_shapes=scratch,
            compiler_params=limit(mib),
            cost_estimate=cost,
            name=name,
        )

    def bf16(*shape):
        return jax.ShapeDtypeStruct(shape, jnp.bfloat16)

    def dma(count):
        return pltpu.SemaphoreType.DMA((count,))

    part = functools.partial
    tag = pltpu.VMEM((TAG_ROWS, nev), jnp.bfloat16)
    split = (width * 5 // 8) // 16 * 16
    two = bf16(2 * rows, nev)
    rest_shape = bf16(2, width - split, width)

    first, rest, near = call(
        part(first_pack, sizes),
        "first_pack",
        [smem()] * 3 + [hbm()] * 2,
        [vmem()] * 3,
        [bf16(2, split, width), rest_shape, bf16(4 * rows + TAG_ROWS, nev)],
        [dma(6)],
        58,
    )(place, separations, partner, peram_blocks, proj)

    u_scratch = pltpu.VMEM((width, 2 * width), jnp.bfloat16)
    v_scratch = pltpu.VMEM((2 * width, 2 * width), jnp.bfloat16)
    turns = pltpu.VMEM((nterm, 4, nev, nev), jnp.bfloat16)
    piece = pltpu.VMEM((1, rows, nev), jnp.bfloat16)
    pieces = pltpu.VMEM((2, rows, nev), jnp.bfloat16)
    y, h0 = call(
        part(own_kernel_0, sizes),
        "own_products_0",
        [smem()] * 3 + [hbm()] * 2,
        [vmem()] * 2,
        [bf16(2 * width, 2 * width), bf16(width, 2 * width)],
        [pltpu.VMEM((2, width, width), jnp.bfloat16), piece, u_scratch, turns, dma(2)],
        58,
    )(place, separations, gamma_index, peram_blocks, proj)

    plan = Plan(place, separations, sizes)
    first = swap_snk(first)
    rest_near, rest_far = most_of(rest, plan.peer_hops())
    near = swap_mom(near, 2)
    if src_count > 2:
        rest_near = jnp.where(plan.peer_hops() // (src_count // 2) != 0, rest_far, rest_near)
        rest_far = rest_near
    rest, far_same, far_cross = call(
        part(second_pack, sizes),
        "second_pack",
        [smem()] * 2 + [hbm()] * 4,
        [vmem()] * 3,
        [rest_shape, two, two],
        [dma(5)],
        16,
    )(place, separations, proj, rest_near, rest_far, h0)
    rest = swap_snk(rest)
    if src_count == 2:
        far_same, far_cross = next_src(far_same), next_src(far_cross, 1, 2)

    own_trade = call(
        own_pack,
        "own_pack",
        [smem()] * 2 + [hbm()] * 2,
        vmem(),
        bf16(2 * (rows + TAG_ROWS), nev),
        [dma(3)],
        16,
    )(place, partner, proj, near)
    own_got = swap_mom(own_trade, 1)
    first_near, first_far = most_of(first, plan.hops(0))

    h2 = call(
        own_kernel_2,
        "own_products_2",
        [smem()] * 2 + [hbm(), vmem()] + [hbm()] * 2,
        vmem(),
        bf16(width, 2 * width),
        [piece, u_scratch, turns, dma(1)],
        16,
    )(place, gamma_index, near, y, first, own_trade)
    h13, label = call(
        part(own_kernel_13, sizes),
        "own_products_13",
        [smem()] * 4 + [hbm()] * 2 + [vmem()],
        [vmem(), smem()],
        [bf16(2, width, 2 * width), jax.ShapeDtypeStruct((2 * mom_count,), jnp.int32)],
        [pieces, u_scratch, turns, tag, pltpu.VMEM((2 * TAG_ROWS, nev), jnp.bfloat16), dma(4)],
        16,
    )(place, separations, gamma_index, partner, near, own_got, y)

    other_trade = call(
        part(other_pack, sizes),
        "other_pack",
        [smem()] * 2 + [hbm()] * 5,
        vmem(),
        two,
        [dma(2)],
        16,
    )(place, separations, proj, near, far_same, far_cross, h13)
    other_got = swap_mom(other_trade, 1)
    if src_count != 2:

        def moved(array):
            if src_count == 1:
                return array
            array, far = most_of(array, plan.hops(0))
            return jnp.where(plan.hops(0) // (src_count // 2) != 0, far, array)

        far_same = moved(lax.dynamic_index_in_dim(proj, plan.local(0), 0, keepdims=False))
        far_cross, other_got = moved(near[:rows]), moved(other_got)

    k_out = jax.ShapeDtypeStruct((mom_count // 2, width, 2 * width), jnp.float32)
    scratch = [pieces, u_scratch, v_scratch, turns, dma(2)]
    ka = call(
        part(other_kernel_02, sizes),
        "other_products_02",
        [smem()] * 4 + [vmem()] * 3 + [hbm()] * 5,
        vmem(),
        k_out,
        scratch,
        24,
    )(
        place, separations, gamma_index, label, h0, h2, h13,
        proj, near, far_same, far_cross, other_trade,
    )
    kb = call(
        other_kernel_13,
        "other_products_13",
        [smem()] * 3 + [vmem()] * 3 + [hbm()],
        vmem(),
        k_out,
        scratch,
        24,
    )(place, gamma_index, label, h0, h2, h13, other_got)

    sums = call(
        part(early_kernel, sizes),
        "early_traces",
        [smem()] * 2 + [vmem()] * 2 + [hbm()] * 2,
        vmem(),
        jax.ShapeDtypeStruct((2 * mom_count, 16, nev), jnp.float32),
        [pltpu.VMEM((2, split, width), jnp.bfloat16), dma(1)],
        20,
    )(place, separations, ka, kb, first_near, first_far)
    device_count = src_count * snk_count * mom_count
    values = time_count * sep_count * 2
    lines = (values + 127) // 128
    out = call(
        part(late_kernel, sizes, sep_count),
        "late_traces",
        [smem()] * 3 + [vmem()] * 4,
        vmem(),
        jax.ShapeDtypeStruct((device_count, lines, 128), jnp.float32),
        [],
        20,
    )(place, separations, label, ka, kb, rest, sums)
    out = lax.all_to_all(out, ("src", "snk", "mom"), split_axis=0, concat_axis=0, tiled=True)
    out = jnp.sum(out, axis=0).reshape(lines * 128)[:values]
    return out.reshape(time_count, sep_count, 1, 2)


def solution(mesh):
    placed = (
        P("src", "snk", None, None, None),
        P("src", "mom", None, None, None, None),
        P(),
        P("mom"),
        P(),
    )
    return jax.shard_map(
        shards, mesh=mesh, in_specs=placed, out_specs=P(None, None, "mom", None), check_vma=False
    )
```

```python
import functools

import jax
import jax.numpy as jnp
from jax import lax
from jax.experimental import pallas as pl
from jax.experimental.pallas import tpu as pltpu
from jax.sharding import PartitionSpec as P

NSPIN = 4
NT_DIMS = (((1,), (1,)), ((), ()))
MIB = 1024 * 1024
WEIGHT = 10**13
TAG_ROWS = 16
TILE = 256
GAMMAS = (
    (3, 1 | 1 << 2 | 3 << 4 | 3 << 6),
    (3, 2 | 0 << 2 | 0 << 4 | 2 << 6),
    (2, 1 | 3 << 2 | 3 << 4 | 1 << 6),
    (2, 0),
)


def spin_entry(code, row):
    phase = row * 0
    for bit, (flip, phases) in enumerate(GAMMAS):
        on = (code >> bit) & 1
        phase = phase + on * ((phases >> (2 * row)) & 3)
        row = row ^ (on * flip)
    return row, phase & 3


def fill_spin_blocks(codes, turns, write):
    for r, code in enumerate(codes):
        for spin in range(NSPIN):
            column, phase = spin_entry(code, spin)
            write(spin, column, *(turns[r, (n - phase) & 3] for n in (4, 1, 3)))


def set_turns(turns, r, real, imag):
    for n, value in enumerate((real, imag, -real, -imag)):
        turns[r, n] = value


def add_to(ref, rows, lanes, value):
    ref[rows, lanes] = ref[rows, lanes] + value


def along(spin, nev, start=0):
    if isinstance(spin, int):
        return slice(start + spin * nev, start + (spin + 1) * nev)
    return pl.ds(pl.multiple_of(start + spin * nev, nev), nev)


class Plan:
    def __init__(self, place, seps, sizes):
        slices, offsets, src_count, snk_count = sizes
        src, snk, self.mom = place[0], place[1], place[2]
        half_snk = snk_count // 2
        self.slices, self.time_count = slices, slices * src_count
        self.forward = snk < half_snk
        base = lax.rem(snk, half_snk) * offsets
        self.keep = jnp.where(self.forward, 0, offsets - 1)
        self.give = offsets - 1 - self.keep
        self.sep_index = base + self.keep
        sign = jnp.where(self.forward, 1, -1)
        self.shift = sign * seps[base + self.keep]
        self.peer_shift = -sign * seps[base + self.give]
        self.own_time = src * slices + self.mom
        late = jnp.where(self.forward, 0, self.shift)
        self.pair_time = lax.rem(self.own_time + late + self.time_count, self.time_count)
        self.live = self.forward if offsets == 1 else None

    def _sum(self, place, amount):
        return lax.rem(place + amount + self.time_count, self.time_count)

    def local(self, i):
        return lax.rem(self._sum(self.mom ^ i, self.shift), self.slices)

    def hops(self, i):
        return lax.div(self._sum(self.mom ^ i, self.shift), self.slices)

    def peer_local(self):
        return lax.rem(self._sum(self.mom, self.peer_shift), self.slices)

    def peer_hops(self):
        return lax.div(self._sum(self.mom, self.peer_shift), self.slices)


def run_copies(copies, sems):
    handles = [
        pltpu.make_async_copy(source, target, sems.at[n])
        for n, (source, target) in enumerate(copies)
    ]
    for handle in handles:
        handle.start()
    for handle in handles:
        handle.wait()


def span(index, rows):
    return pl.ds(index * rows, rows)


def pack(sizes, place, seps, partner, peram, proj, *refs):
    outs, bufs, (ins, outs_sems) = refs[:6], refs[6:12], refs[12:]
    plan = Plan(place, seps, sizes)
    first, rest = outs[:2]
    split, rows = first.shape[1], proj.shape[1]
    peer, give, mom = plan.peer_local(), plan.give, plan.mom
    number = jnp.full((TAG_ROWS, proj.shape[-1]), partner[0].astype(jnp.float32))
    number = number.astype(jnp.bfloat16)
    first_buf, rest_buf, near, near_core, far_same, far_cross = bufs
    near[pl.ds(4 * rows, TAG_ROWS), :] = number
    near_core[pl.ds(2 * rows, TAG_ROWS), :] = number
    parts = [
        [(peram.at[peer, give, :, pl.ds(0, split)], first_buf)],
        [(proj.at[plan.local(i)], far_same.at[span(i, rows)]) for i in (0, 1)],
        [(proj.at[plan.local(i + 2)], far_cross.at[span(i, rows)]) for i in (0, 1)],
        [
            (proj.at[plan.local(2)], near.at[span(0, rows)]),
            (proj.at[plan.local(3)], near.at[span(1, rows)]),
            (proj.at[mom ^ 2], near.at[span(2, rows)]),
            (proj.at[mom ^ 3], near.at[span(3, rows)]),
        ],
        [(peram.at[peer, give, :, pl.ds(split, rest.shape[1])], rest_buf)],
        [
            (proj.at[plan.local(1)], near_core.at[span(0, rows)]),
            (proj.at[mom ^ 1], near_core.at[span(1, rows)]),
        ],
    ]
    order = (0, 4, 5, 2, 1, 3)
    handles, n = [], 0
    for part in parts:
        group = []
        for source, target in part:
            group.append(pltpu.make_async_copy(source, target, ins.at[n]))
            group[-1].start()
            n += 1
        handles.append(group)
    leaving = []
    for n, (group, index) in enumerate(zip(handles, order)):
        for handle in group:
            handle.wait()
        leaving.append(pltpu.make_async_copy(bufs[index], outs[index], outs_sems.at[n]))
        leaving[-1].start()
    for handle in leaving:
        handle.wait()


def choose(sizes, place, seps, near, far, first, out, token, sems):
    flag = lax.rem(Plan(place, seps, sizes).peer_hops(), 2)

    @pl.when(flag == 0)
    def _():
        run_copies([(near, out)], sems)

    @pl.when(flag != 0)
    def _():
        run_copies([(far, out)], sems)

    token[...] = jnp.zeros(token.shape, token.dtype)


def gate(token_in, low, high, low_out, high_out, token):
    token[...] = token_in[...]


def own_fill(codes, p_ref, n, u_ref, turns):
    nev = turns.shape[-1]
    width = u_ref.shape[0]
    for r in range(len(codes)):
        real, imag = (p_ref[n, m * nev : (m + 1) * nev].T for m in (2 * r, 2 * r + 1))
        set_turns(turns, r, real, imag)
    u_ref[...] = jnp.zeros(u_ref.shape, u_ref.dtype)

    def write(spin, column, a, b, minus_b):
        add_to(u_ref, along(column, nev), along(spin, nev), a)
        add_to(u_ref, along(column, nev), along(spin, nev, width), b)

    fill_spin_blocks(codes, turns, write)


def own_dot(u_ref, y_ref, ht):
    for tile in range(ht.shape[-1] // TILE):
        lanes = slice(tile * TILE, (tile + 1) * TILE)
        out = lax.dot_general(
            u_ref[...], y_ref[lanes, :], NT_DIMS, preferred_element_type=jnp.float32
        )
        ht[:, lanes] = out.astype(jnp.bfloat16)


def codes_of(gamma, op, nterm):
    return [gamma[op, r] for r in range(nterm)]


def own_kernel_01(sizes, place, seps, gamma, peram, proj, near_core, y_ref, h0, h1, *refs):
    x_ref, p_ref, u0, u1, turns0, turns1, sems = refs
    plan = Plan(place, seps, sizes)
    rows = proj.shape[1]
    run_copies(
        [
            (peram.at[plan.mom, plan.keep], x_ref),
            (proj.at[plan.mom], p_ref.at[0]),
            (near_core.at[span(1, rows)], p_ref.at[1]),
        ],
        sems,
    )
    width = x_ref.shape[-1]
    real, imag = x_ref[0], x_ref[1]
    y_ref[:width, :width] = real
    y_ref[:width, width:] = -imag
    y_ref[width:, :width] = imag
    y_ref[width:, width:] = real
    nterm = turns0.shape[0]
    own_fill(codes_of(gamma, plan.mom, nterm), p_ref, 0, u0, turns0)
    own_dot(u0, y_ref, h0)
    own_fill(codes_of(gamma, plan.mom ^ 1, nterm), p_ref, 1, u1, turns1)
    own_dot(u1, y_ref, h1)


def own_kernel_2(place, gamma, near, y_ref, after, ht, token, p_ref, u_ref, turns, sems):
    rows = p_ref.shape[1]
    run_copies([(near.at[span(2, rows)], p_ref.at[0])], sems)
    own_fill(codes_of(gamma, place[2] ^ 2, turns.shape[0]), p_ref, 0, u_ref, turns)
    own_dot(u_ref, y_ref, ht)
    token[...] = jnp.zeros(token.shape, token.dtype)


def own_kernel_3(sizes, place, seps, gamma, partner, near, near_core, forward, y_ref, after, *refs):
    ht, label, p_ref, u_ref, turns, tags, sems = refs
    plan = Plan(place, seps, sizes)
    mom = plan.mom
    rows = p_ref.shape[1]
    run_copies(
        [
            (forward.at[span(3, rows)], p_ref.at[0]),
            (near_core.at[pl.ds(2 * rows, TAG_ROWS)], tags.at[0]),
            (near.at[pl.ds(4 * rows, TAG_ROWS)], tags.at[1]),
            (forward.at[pl.ds(4 * rows, TAG_ROWS)], tags.at[2]),
        ],
        sems,
    )
    partners = [partner[0]] + [
        jnp.max(tags[n].astype(jnp.float32)).astype(jnp.int32) for n in range(3)
    ]
    count = len(partners)
    for p in range(count):
        back = jnp.int32(0)
        for i, value in enumerate(partners):
            back = back + jnp.where(value == (mom ^ p), mom ^ i, 0)
        label[p] = jnp.where(plan.forward, mom ^ p, back)
        label[count + p] = jnp.where(plan.forward, partners[p], back) ^ mom
    own_fill(codes_of(gamma, mom ^ 3, turns.shape[0]), p_ref, 0, u_ref, turns)
    own_dot(u_ref, y_ref, ht)


def other_kernel(sizes, far_at, place, seps, gamma, label, h0, h1, h2, h3, proj, near, *refs):
    near_core, forward, far = refs[0], refs[1], refs[2:6]
    k_ref, p_ref, va, vb, turns_a, turns_b, sems = refs[6:]
    plan = Plan(place, seps, sizes)
    rows = proj.shape[1]
    mom = plan.mom
    nterm, nev = turns_a.shape[0], turns_a.shape[-1]
    width = h0.shape[0]
    flag = lax.rem(plan.hops(0), 2) if sizes[2] == 2 else jnp.int32(1)

    @pl.when(flag == 0)
    def _():
        run_copies(
            [
                (proj.at[plan.local(0)], p_ref.at[0]),
                (near_core.at[span(0, rows)], p_ref.at[1]),
                (near.at[span(0, rows)], p_ref.at[2]),
                (forward.at[span(1, rows)], p_ref.at[3]),
            ],
            sems,
        )

    @pl.when(flag != 0)
    def _():
        copies = zip(far, (0, far_at, 0, far_at), (0, 1, 2, 3))
        run_copies([(ref.at[span(at, rows)], p_ref.at[n]) for ref, at, n in copies], sems)

    for p, ht in enumerate((h0, h1, h2, h3)):
        v_ref, turns = ((va, turns_a), (vb, turns_b))[p % 2]
        other = label[4 + p]
        for r in range(nterm):
            real, imag = (p_ref[other, m * nev : (m + 1) * nev] for m in (2 * r, 2 * r + 1))
            set_turns(turns, r, real, imag)
        v_ref[...] = jnp.zeros(v_ref.shape, v_ref.dtype)

        def write(spin, column, a, b, minus_b, v_ref=v_ref):
            add_to(v_ref, along(spin, nev), along(column, nev), a)
            add_to(v_ref, along(spin, nev), along(column, nev, width), minus_b)
            add_to(v_ref, along(spin, nev, width), along(column, nev), b)
            add_to(v_ref, along(spin, nev, width), along(column, nev, width), a)

        fill_spin_blocks(codes_of(gamma, mom ^ other, nterm), turns, write)
        for tile in range(2 * width // TILE):
            lanes = slice(tile * TILE, (tile + 1) * TILE)
            k_ref[p, :, lanes] = lax.dot_general(
                ht[...], v_ref[lanes, :], NT_DIMS, preferred_element_type=jnp.float32
            )


def row_sums(k_ref, source, offset, totals):
    rows = 16
    width = source.shape[-1]
    nev = totals[0].shape[-1]

    def step(index, totals):
        row = pl.multiple_of(index * rows, rows)
        here = pl.ds(pl.multiple_of(offset + row, rows), rows)
        totals = list(totals)
        for spin in range(NSPIN):
            lanes, later = along(spin, nev), along(spin, nev, width)
            real = source[0, pl.ds(row, rows), lanes].astype(jnp.float32)
            imag = source[1, pl.ds(row, rows), lanes].astype(jnp.float32)
            for n in range(len(totals) // 2):
                kr, ki = k_ref[n, here, lanes], k_ref[n, here, later]
                totals[2 * n] += real * kr - imag * ki
                totals[2 * n + 1] += real * ki + imag * kr
        return tuple(totals)

    return lax.fori_loop(0, source.shape[1] // rows, step, totals)


def early_kernel(sizes, place, seps, k_ref, near, far, sums_ref, part_ref, sems):
    plan = Plan(place, seps, sizes)
    count = sums_ref.shape[0]
    flag = lax.rem(lax.div(plan.hops(0), max(sizes[2] // 2, 1)), 2)

    @pl.when(flag == 0)
    def _():
        run_copies([(near, part_ref)], sems)

    @pl.when(flag != 0)
    def _():
        run_copies([(far, part_ref)], sems)

    zero = tuple(jnp.zeros(sums_ref.shape[1:], jnp.float32) for _ in range(count))
    for n, total in enumerate(row_sums(k_ref, part_ref, 0, zero)):
        sums_ref[n] = total


def late_kernel(sizes, sep_count, place, seps, label, k_ref, rest_ref, sums_ref, out_ref):
    plan = Plan(place, seps, sizes)
    count = sums_ref.shape[0] // 2
    width = rest_ref.shape[-1]
    start = k_ref.shape[1] - rest_ref.shape[1]
    totals = row_sums(k_ref, rest_ref, start, tuple(sums_ref[n] for n in range(2 * count)))
    sums = [jnp.sum(total, axis=0, keepdims=True) for total in totals]
    sums = [jnp.sum(total, axis=1, keepdims=True) * (1.0 / width) for total in sums]
    shape = out_ref.shape[1:]
    spot = lax.broadcasted_iota(jnp.int32, shape, 0) * shape[1]
    spot = spot + lax.broadcasted_iota(jnp.int32, shape, 1)
    here = spot // 2 == plan.pair_time * sep_count + plan.sep_index
    if plan.live is not None:
        here = here & plan.live
    values = [jnp.where(spot % 2 == 0, sums[2 * p], sums[2 * p + 1]) for p in range(count)]
    lines = []
    for op in range(count):
        line = jnp.zeros(shape, jnp.float32)
        for p, value in enumerate(values):
            line = jnp.where(label[p] == op, value, line)
        lines.append(jnp.where(here, line, 0.0))
    for n in range(out_ref.shape[0]):
        out_ref[n] = lines[n % count]


def smem():
    return pl.BlockSpec(memory_space=pltpu.SMEM)


def vmem():
    return pl.BlockSpec(memory_space=pltpu.VMEM)


def hbm():
    return pl.BlockSpec(memory_space=pltpu.HBM)


def limit(mib):
    return pltpu.CompilerParams(vmem_limit_bytes=mib * MIB)


def shards(peram_blocks, projections, gamma_index, partner, separations):
    src_count, snk_count = lax.axis_size("src"), lax.axis_size("snk")
    mom_count = lax.axis_size("mom")
    slices, offsets = peram_blocks.shape[:2]
    width = peram_blocks.shape[-1]
    nterm, nev = projections.shape[2], projections.shape[-1]
    time_count = slices * src_count
    sep_count = separations.shape[0]
    half_snk = snk_count // 2
    rows = nterm * 2 * nev
    sizes = (slices, offsets, src_count, snk_count)
    place = jnp.stack([lax.axis_index(name) for name in ("src", "snk", "mom")]).astype(jnp.int32)
    proj = projections.reshape(slices, rows, nev)

    def swap_mom(array, i):
        return lax.ppermute(array, "mom", [(a, a ^ i) for a in range(mom_count)])

    def swap_snk(array):
        pairs = [(a, (a + half_snk) % snk_count) for a in range(snk_count)]
        return lax.ppermute(array, "snk", pairs)

    def next_src(array, step=1, i=0):
        pairs = [
            (((a + step) % src_count) * mom_count + (b ^ i), a * mom_count + b)
            for a in range(src_count)
            for b in range(mom_count)
        ]
        return lax.ppermute(array, ("src", "mom"), pairs)

    def most_of(array, amount):
        step = 1
        while 2 * step < src_count:
            array = jnp.where((amount // step) % 2 != 0, next_src(array, step), array)
            step *= 2
        return array, next_src(array, step)

    def call(kernel, name, in_specs, out_specs, out_shape, scratch, mib):
        cost = pl.CostEstimate(flops=WEIGHT, bytes_accessed=WEIGHT // 1000, transcendentals=0)
        return pl.pallas_call(
            kernel,
            in_specs=in_specs,
            out_specs=out_specs,
            out_shape=out_shape,
            scratch_shapes=scratch,
            compiler_params=limit(mib),
            cost_estimate=cost,
            name=name,
        )

    def bf16(*shape):
        return jax.ShapeDtypeStruct(shape, jnp.bfloat16)

    def dma(count):
        return pltpu.SemaphoreType.DMA((count,))

    part = functools.partial
    split = (width * 5 // 8) // 16 * 16
    two = bf16(2 * rows, nev)
    rest_shape = bf16(2, width - split, width)
    leaving = [
        bf16(2, split, width),
        rest_shape,
        bf16(4 * rows + TAG_ROWS, nev),
        bf16(2 * rows + TAG_ROWS, nev),
        two,
        two,
    ]
    first, rest, near, near_core, far_same, far_cross = call(
        part(pack, sizes),
        "pack",
        [smem()] * 3 + [hbm()] * 2,
        [hbm()] * 6,
        leaving,
        [pltpu.VMEM(shape.shape, shape.dtype) for shape in leaving] + [dma(12), dma(6)],
        58,
    )(place, separations, partner, peram_blocks, proj)

    plan = Plan(place, separations, sizes)
    first = swap_snk(first)
    near = swap_mom(near, 2)
    rest_near, rest_far = most_of(rest, plan.peer_hops())
    if src_count == 2:
        far_same, far_cross = next_src(far_same), next_src(far_cross, 1, 2)
    near_core = swap_mom(near_core, 1)
    forward = swap_mom(near, 1)

    u_scratch = pltpu.VMEM((width, 2 * width), jnp.bfloat16)
    v_scratch = pltpu.VMEM((2 * width, 2 * width), jnp.bfloat16)
    turns = pltpu.VMEM((nterm, 4, nev, nev), jnp.bfloat16)
    piece = pltpu.VMEM((1, rows, nev), jnp.bfloat16)
    product = bf16(width, 2 * width)
    token = bf16(16, 128)
    y, h0, h1 = call(
        part(own_kernel_01, sizes),
        "own_products_01",
        [smem()] * 3 + [hbm()] * 3,
        [vmem()] * 3,
        [bf16(2 * width, 2 * width), product, product],
        [
            pltpu.VMEM((2, width, width), jnp.bfloat16),
            pltpu.VMEM((2, rows, nev), jnp.bfloat16),
            u_scratch,
            u_scratch,
            turns,
            turns,
            dma(3),
        ],
        58,
    )(place, separations, gamma_index, peram_blocks, proj, near_core)

    if src_count > 2:
        rest_near = jnp.where(plan.peer_hops() // (src_count // 2) != 0, rest_far, rest_near)
        rest_far = rest_near
    rest, chosen = call(
        part(choose, sizes),
        "choose",
        [smem()] * 2 + [hbm()] * 3,
        [vmem()] * 2,
        [rest_shape, token],
        [dma(1)],
        16,
    )(place, separations, rest_near, rest_far, first)
    rest = swap_snk(rest)
    first_near, first_far = most_of(first, plan.hops(0))

    h2, done_2 = call(
        own_kernel_2,
        "own_products_2",
        [smem()] * 2 + [hbm(), vmem(), vmem()],
        [vmem()] * 2,
        [product, token],
        [piece, u_scratch, turns, dma(1)],
        16,
    )(place, gamma_index, near, y, chosen)
    far_same, far_cross, opened = pl.pallas_call(
        gate,
        in_specs=[vmem(), pl.BlockSpec(memory_space=pl.ANY), pl.BlockSpec(memory_space=pl.ANY)],
        out_specs=[pl.BlockSpec(memory_space=pl.ANY), pl.BlockSpec(memory_space=pl.ANY), vmem()],
        out_shape=[two, two, token],
        input_output_aliases={1: 0, 2: 1},
        compiler_params=limit(16),
        cost_estimate=pl.CostEstimate(
            flops=WEIGHT, bytes_accessed=WEIGHT // 1000, transcendentals=0
        ),
        name="gate",
    )(done_2, far_same, far_cross)
    h3, label = call(
        part(own_kernel_3, sizes),
        "own_products_3",
        [smem()] * 4 + [hbm()] * 3 + [vmem()] * 2,
        [vmem(), smem()],
        [product, jax.ShapeDtypeStruct((2 * mom_count,), jnp.int32)],
        [piece, u_scratch, turns, pltpu.VMEM((3, TAG_ROWS, nev), jnp.bfloat16), dma(4)],
        16,
    )(place, separations, gamma_index, partner, near, near_core, forward, y, opened)

    if src_count == 2:
        far = [far_same, swap_mom(far_same, 1), far_cross, swap_mom(far_cross, 1)]
    else:

        def moved(array):
            if src_count == 1:
                return array
            array, away = most_of(array, plan.hops(0))
            return jnp.where(plan.hops(0) // (src_count // 2) != 0, away, array)

        own = lax.dynamic_index_in_dim(proj, plan.local(0), 0, keepdims=False)
        far = [own, near_core[:rows], near[:rows], forward[rows : 2 * rows]]
        far = [moved(array) for array in far]
    k = call(
        part(other_kernel, sizes, 1 if src_count == 2 else 0),
        "other_products",
        [smem()] * 4 + [vmem()] * 4 + [hbm()] * 8,
        vmem(),
        jax.ShapeDtypeStruct((mom_count, width, 2 * width), jnp.float32),
        [
            pltpu.VMEM((mom_count, rows, nev), jnp.bfloat16),
            v_scratch,
            v_scratch,
            turns,
            turns,
            dma(4),
        ],
        28,
    )(
        place, separations, gamma_index, label, h0, h1, h2, h3,
        proj, near, near_core, forward, *far,
    )

    sums = call(
        part(early_kernel, sizes),
        "early_traces",
        [smem()] * 2 + [vmem()] + [hbm()] * 2,
        vmem(),
        jax.ShapeDtypeStruct((2 * mom_count, 16, nev), jnp.float32),
        [pltpu.VMEM((2, split, width), jnp.bfloat16), dma(1)],
        20,
    )(place, separations, k, first_near, first_far)
    device_count = src_count * snk_count * mom_count
    values = time_count * sep_count * 2
    lines = (values + 127) // 128
    out = call(
        part(late_kernel, sizes, sep_count),
        "late_traces",
        [smem()] * 3 + [vmem()] * 3,
        vmem(),
        jax.ShapeDtypeStruct((device_count, lines, 128), jnp.float32),
        [],
        20,
    )(place, separations, label, k, rest, sums)
    out = lax.all_to_all(out, ("src", "snk", "mom"), split_axis=0, concat_axis=0, tiled=True)
    out = jnp.sum(out, axis=0).reshape(lines * 128)[:values]
    return out.reshape(time_count, sep_count, 1, 2)


def solution(mesh):
    placed = (
        P("src", "snk", None, None, None),
        P("src", "mom", None, None, None, None),
        P(),
        P("mom"),
        P(),
    )
    return jax.shard_map(
        shards, mesh=mesh, in_specs=placed, out_specs=P(None, None, "mom", None), check_vma=False
    )
```

```python
import functools

import jax
import jax.numpy as jnp
from jax import lax
from jax.experimental import pallas as pl
from jax.experimental.pallas import tpu as pltpu
from jax.sharding import PartitionSpec as P

NSPIN = 4
NT_DIMS = (((1,), (1,)), ((), ()))
MIB = 1024 * 1024
WEIGHT = 10**13
TAG_ROWS = 16
TILE = 256
GAMMAS = (
    (3, 1 | 1 << 2 | 3 << 4 | 3 << 6),
    (3, 2 | 0 << 2 | 0 << 4 | 2 << 6),
    (2, 1 | 3 << 2 | 3 << 4 | 1 << 6),
    (2, 0),
)


def spin_entry(code, row):
    phase = row * 0
    for bit, (flip, phases) in enumerate(GAMMAS):
        on = (code >> bit) & 1
        phase = phase + on * ((phases >> (2 * row)) & 3)
        row = row ^ (on * flip)
    return row, phase & 3


def fill_spin_blocks(codes, turns, write):
    for r, code in enumerate(codes):
        for spin in range(NSPIN):
            column, phase = spin_entry(code, spin)
            write(spin, column, *(turns[r, (n - phase) & 3] for n in (4, 1, 3)))


def set_turns(turns, r, real, imag):
    for n, value in enumerate((real, imag, -real, -imag)):
        turns[r, n] = value


def add_to(ref, rows, lanes, value):
    ref[rows, lanes] = ref[rows, lanes] + value


def along(spin, nev, start=0):
    if isinstance(spin, int):
        return slice(start + spin * nev, start + (spin + 1) * nev)
    return pl.ds(pl.multiple_of(start + spin * nev, nev), nev)


class Plan:
    def __init__(self, seps, sizes):
        slices, offsets, src_count, snk_count = sizes
        src, snk, self.mom = (lax.axis_index(name) for name in ("src", "snk", "mom"))
        half_snk = snk_count // 2
        self.slices, self.time_count = slices, slices * src_count
        self.forward = snk < half_snk
        base = lax.rem(snk, half_snk) * offsets
        self.keep = jnp.where(self.forward, 0, offsets - 1)
        self.give = offsets - 1 - self.keep
        self.sep_index = base + self.keep
        sign = jnp.where(self.forward, 1, -1)
        self.shift = sign * seps[base + self.keep]
        self.peer_shift = -sign * seps[base + self.give]
        self.own_time = src * slices + self.mom
        late = jnp.where(self.forward, 0, self.shift)
        self.pair_time = lax.rem(self.own_time + late + self.time_count, self.time_count)
        self.live = self.forward if offsets == 1 else None

    def _sum(self, place, amount):
        return lax.rem(place + amount + self.time_count, self.time_count)

    def local(self, i):
        return lax.rem(self._sum(self.mom ^ i, self.shift), self.slices)

    def hops(self, i):
        return lax.div(self._sum(self.mom ^ i, self.shift), self.slices)

    def peer_local(self):
        return lax.rem(self._sum(self.mom, self.peer_shift), self.slices)

    def peer_hops(self):
        return lax.div(self._sum(self.mom, self.peer_shift), self.slices)


def run_copies(copies, sems):
    handles = [
        pltpu.make_async_copy(source, target, sems.at[n])
        for n, (source, target) in enumerate(copies)
    ]
    for handle in handles:
        handle.start()
    for handle in handles:
        handle.wait()


def span(index, rows):
    return pl.ds(index * rows, rows)


def through(parts, ins, leaving):
    started, n = [], 0
    for copies, buffer, target in parts:
        group = []
        for source, spot in copies:
            group.append(pltpu.make_async_copy(source, spot, ins.at[n]))
            group[-1].start()
            n += 1
        started.append(group)
    handles = []
    for n, (group, (_, buffer, target)) in enumerate(zip(started, parts)):
        for handle in group:
            handle.wait()
        handles.append(pltpu.make_async_copy(buffer, target, leaving.at[n]))
        handles[-1].start()
    for handle in handles:
        handle.wait()


def two_slices(proj, buffer, first, second):
    rows = proj.shape[1]
    return [(proj.at[n], buffer.at[span(i, rows)]) for i, n in enumerate((first, second))]


def pack(sizes, seps, partner, peram, proj, *refs):
    outs, buffers, (ins, leaving) = refs[:4], refs[4:8], refs[8:]
    plan = Plan(seps, sizes)
    rows = proj.shape[1]
    peer, give, mom = plan.peer_local(), plan.give, plan.mom
    number = jnp.full((TAG_ROWS, proj.shape[-1]), partner[0].astype(jnp.float32))
    number = number.astype(jnp.bfloat16)
    first, core, own, rest = buffers
    core[pl.ds(2 * rows, TAG_ROWS), :] = number
    own[pl.ds(2 * rows, TAG_ROWS), :] = number
    split = first.shape[1]
    copies = [
        [(peram.at[peer, give, :, pl.ds(0, split)], first)],
        two_slices(proj, core, plan.local(1), mom ^ 1),
        two_slices(proj, own, mom ^ 2, mom ^ 3),
        [(peram.at[peer, give, :, pl.ds(split, rest.shape[1])], rest)],
    ]
    through(list(zip(copies, buffers, outs)), ins, leaving)


def pack_far(sizes, seps, peram, proj, after, *refs):
    outs, buffers, (ins, leaving) = refs[:3], refs[3:6], refs[6:]
    plan = Plan(seps, sizes)
    same, cross, block = buffers
    copies = [
        two_slices(proj, same, plan.local(0), plan.local(1)),
        two_slices(proj, cross, plan.local(2), plan.local(3)),
        [(peram.at[plan.mom, plan.keep], block)],
    ]
    through(list(zip(copies, buffers, outs)), ins, leaving)


def choose(sizes, seps, near, far, proj, after, out, others, sems):
    plan = Plan(seps, sizes)
    flag = lax.rem(plan.peer_hops(), 2)
    rows = proj.shape[1]
    copies = [(proj.at[plan.local(i + 2)], others.at[span(i, rows)]) for i in (0, 1)]

    @pl.when(flag == 0)
    def _():
        run_copies([(near, out)] + copies, sems)

    @pl.when(flag != 0)
    def _():
        run_copies([(far, out)] + copies, sems)


def gate(first, rest, first_out, rest_out, token):
    token[...] = jnp.zeros(token.shape, token.dtype)


def other_pack(sizes, seps, proj, near, far_same, far_cross, after, out, sems):
    plan = Plan(seps, sizes)
    rows = out.shape[0] // 2
    flag = lax.rem(plan.hops(1), 2) if sizes[2] == 2 else jnp.int32(0)
    low, high = out.at[span(0, rows)], out.at[span(1, rows)]

    @pl.when(flag == 0)
    def _():
        run_copies([(proj.at[plan.local(1)], low), (near.at[span(1, rows)], high)], sems)

    @pl.when(flag != 0)
    def _():
        run_copies([(far_same.at[span(1, rows)], low), (far_cross.at[span(1, rows)], high)], sems)


def own_fill(codes, p_ref, n, u_ref, turns):
    nev = turns.shape[-1]
    width = u_ref.shape[0]
    for r in range(len(codes)):
        real, imag = (p_ref[n, m * nev : (m + 1) * nev].T for m in (2 * r, 2 * r + 1))
        set_turns(turns, r, real, imag)
    u_ref[...] = jnp.zeros(u_ref.shape, u_ref.dtype)

    def write(spin, column, a, b, minus_b):
        add_to(u_ref, along(column, nev), along(spin, nev), a)
        add_to(u_ref, along(column, nev), along(spin, nev, width), b)

    fill_spin_blocks(codes, turns, write)


def own_dot(u_ref, y_ref, ht):
    for tile in range(ht.shape[-1] // TILE):
        lanes = slice(tile * TILE, (tile + 1) * TILE)
        out = lax.dot_general(
            u_ref[...], y_ref[lanes, :], NT_DIMS, preferred_element_type=jnp.float32
        )
        ht[:, lanes] = out.astype(jnp.bfloat16)


def codes_of(gamma, op, nterm):
    return [gamma[op, r] for r in range(nterm)]


def own_kernel_01(gamma, block, proj, core, y_ref, h_ref, x_ref, p_ref, u0, u1, turns0, turns1, sems):
    mom = lax.axis_index("mom")
    rows = proj.shape[1]
    run_copies(
        [
            (block, x_ref),
            (proj.at[mom], p_ref.at[0]),
            (core.at[span(1, rows)], p_ref.at[1]),
        ],
        sems,
    )
    width = x_ref.shape[-1]
    real, imag = x_ref[0], x_ref[1]
    y_ref[:width, :width] = real
    y_ref[:width, width:] = -imag
    y_ref[width:, :width] = imag
    y_ref[width:, width:] = real
    nterm = turns0.shape[0]
    own_fill(codes_of(gamma, mom, nterm), p_ref, 0, u0, turns0)
    own_dot(u0, y_ref, h_ref.at[0])
    own_fill(codes_of(gamma, mom ^ 1, nterm), p_ref, 1, u1, turns1)
    own_dot(u1, y_ref, h_ref.at[1])


def own_kernel_23(sizes, seps, gamma, partner, core, own, forward, y_ref, h_in, *refs):
    h_ref, label, token, p_ref, u0, u1, turns0, turns1, tags, sems = refs
    rows = p_ref.shape[1]
    spot = pl.ds(core.shape[0] - TAG_ROWS, TAG_ROWS)
    run_copies(
        [(own.at[span(0, rows)], p_ref.at[0]), (forward.at[span(1, rows)], p_ref.at[1])]
        + [(ref.at[spot], tags.at[n]) for n, ref in enumerate((core, own, forward))],
        sems,
    )
    plan = Plan(seps, sizes)
    mom = plan.mom
    partners = [partner[0]] + [
        jnp.max(tags[n].astype(jnp.float32)).astype(jnp.int32) for n in range(3)
    ]
    count = len(partners)
    for p in range(count):
        back = jnp.int32(0)
        for i, value in enumerate(partners):
            back = back + jnp.where(value == (mom ^ p), mom ^ i, 0)
        label[p] = jnp.where(plan.forward, back, mom ^ p)
        label[count + p] = jnp.where(plan.forward, back, partners[p]) ^ mom
    nterm = turns0.shape[0]
    own_fill(codes_of(gamma, mom ^ 2, nterm), p_ref, 0, u0, turns0)
    own_dot(u0, y_ref, h_ref.at[2])
    own_fill(codes_of(gamma, mom ^ 3, nterm), p_ref, 1, u1, turns1)
    own_dot(u1, y_ref, h_ref.at[3])
    token[...] = jnp.zeros(token.shape, token.dtype)


def other_products(pieces, gamma, label, h_ref, refs):
    k_ref, p_ref, va, vb, turns_a, turns_b = refs
    mom = lax.axis_index("mom")
    nterm, nev = turns_a.shape[0], turns_a.shape[-1]
    width = h_ref.shape[1]
    for n, piece in enumerate(pieces):
        v_ref, turns = ((va, turns_a), (vb, turns_b))[n % 2]
        for r in range(nterm):
            real, imag = (p_ref[n, m * nev : (m + 1) * nev] for m in (2 * r, 2 * r + 1))
            set_turns(turns, r, real, imag)
        v_ref[...] = jnp.zeros(v_ref.shape, v_ref.dtype)

        def write(spin, column, a, b, minus_b, v_ref=v_ref):
            add_to(v_ref, along(spin, nev), along(column, nev), a)
            add_to(v_ref, along(spin, nev), along(column, nev, width), minus_b)
            add_to(v_ref, along(spin, nev, width), along(column, nev), b)
            add_to(v_ref, along(spin, nev, width), along(column, nev, width), a)

        fill_spin_blocks(codes_of(gamma, mom ^ piece, nterm), turns, write)
        own = label[4 + piece]
        for tile in range(2 * width // TILE):
            lanes = slice(tile * TILE, (tile + 1) * TILE)
            k_ref[n, :, lanes] = lax.dot_general(
                h_ref[own], v_ref[lanes, :], NT_DIMS, preferred_element_type=jnp.float32
            )


def other_kernel_02(sizes, seps, gamma, label, h_ref, proj, near, far_same, far_cross, *refs):
    k_ref, p_ref, va, vb, turns_a, turns_b, sems = refs
    plan = Plan(seps, sizes)
    rows = p_ref.shape[1]
    low = span(0, rows)
    flag = lax.rem(plan.hops(0), 2) if sizes[2] == 2 else jnp.int32(1)

    @pl.when(flag == 0)
    def _():
        run_copies([(proj.at[plan.local(0)], p_ref.at[0]), (near.at[low], p_ref.at[1])], sems)

    @pl.when(flag != 0)
    def _():
        run_copies([(far_same.at[low], p_ref.at[0]), (far_cross.at[low], p_ref.at[1])], sems)

    out = (k_ref, p_ref, va, vb, turns_a, turns_b)
    other_products((0, 2), gamma, label, h_ref, out)


def other_kernel_13(gamma, label, h_ref, traded, k_ref, p_ref, va, vb, turns_a, turns_b, sems):
    rows = p_ref.shape[1]
    run_copies([(traded.at[span(n, rows)], p_ref.at[n]) for n in range(2)], sems)
    out = (k_ref, p_ref, va, vb, turns_a, turns_b)
    other_products((1, 3), gamma, label, h_ref, out)


def row_sums(k_refs, source, offset, totals):
    rows = 16
    width = source.shape[-1]
    nev = totals[0].shape[-1]

    def step(index, totals):
        row = pl.multiple_of(index * rows, rows)
        here = pl.ds(pl.multiple_of(offset + row, rows), rows)
        totals = list(totals)
        for spin in range(NSPIN):
            lanes, later = along(spin, nev), along(spin, nev, width)
            real = source[0, pl.ds(row, rows), lanes].astype(jnp.float32)
            imag = source[1, pl.ds(row, rows), lanes].astype(jnp.float32)
            for n in range(len(totals) // 2):
                k_ref, p = k_refs[n // 2], n % 2
                kr, ki = k_ref[p, here, lanes], k_ref[p, here, later]
                totals[2 * n] += real * kr - imag * ki
                totals[2 * n + 1] += real * ki + imag * kr
        return tuple(totals)

    return lax.fori_loop(0, source.shape[1] // rows, step, totals)


def early_kernel(sizes, seps, ka, kb, near, far, sums_ref, part_ref, sems):
    plan = Plan(seps, sizes)
    count = sums_ref.shape[0]
    flag = lax.rem(lax.div(plan.hops(0), max(sizes[2] // 2, 1)), 2)

    @pl.when(flag == 0)
    def _():
        run_copies([(near, part_ref)], sems)

    @pl.when(flag != 0)
    def _():
        run_copies([(far, part_ref)], sems)

    zero = tuple(jnp.zeros(sums_ref.shape[1:], jnp.float32) for _ in range(count))
    for n, total in enumerate(row_sums((ka, kb), part_ref, 0, zero)):
        sums_ref[n] = total


def late_kernel(sizes, sep_count, seps, label, ka, kb, rest_ref, sums_ref, out_ref):
    plan = Plan(seps, sizes)
    count = sums_ref.shape[0] // 2
    width = rest_ref.shape[-1]
    start = ka.shape[1] - rest_ref.shape[1]
    totals = row_sums((ka, kb), rest_ref, start, tuple(sums_ref[n] for n in range(2 * count)))
    sums = [jnp.sum(total, axis=0, keepdims=True) for total in totals]
    sums = [jnp.sum(total, axis=1, keepdims=True) * (1.0 / width) for total in sums]
    shape = out_ref.shape[1:]
    spot = lax.broadcasted_iota(jnp.int32, shape, 0) * shape[1]
    spot = spot + lax.broadcasted_iota(jnp.int32, shape, 1)
    here = spot // 2 == plan.pair_time * sep_count + plan.sep_index
    if plan.live is not None:
        here = here & plan.live
    values = [jnp.where(spot % 2 == 0, sums[2 * p], sums[2 * p + 1]) for p in range(count)]
    lines = []
    for op in range(count):
        line = jnp.zeros(shape, jnp.float32)
        for p, value in zip((0, 2, 1, 3), values):
            line = jnp.where(label[p] == op, value, line)
        lines.append(jnp.where(here, line, 0.0))
    for n in range(out_ref.shape[0]):
        out_ref[n] = lines[n % count]


def smem():
    return pl.BlockSpec(memory_space=pltpu.SMEM)


def vmem():
    return pl.BlockSpec(memory_space=pltpu.VMEM)


def anywhere():
    return pl.BlockSpec(memory_space=pl.ANY)


def hbm():
    return pl.BlockSpec(memory_space=pltpu.HBM)


def limit(mib):
    return pltpu.CompilerParams(vmem_limit_bytes=mib * MIB)


def shards(peram_blocks, projections, gamma_index, partner, separations):
    src_count, snk_count = lax.axis_size("src"), lax.axis_size("snk")
    mom_count = lax.axis_size("mom")
    slices, offsets = peram_blocks.shape[:2]
    width = peram_blocks.shape[-1]
    nterm, nev = projections.shape[2], projections.shape[-1]
    time_count = slices * src_count
    sep_count = separations.shape[0]
    half_snk = snk_count // 2
    rows = nterm * 2 * nev
    sizes = (slices, offsets, src_count, snk_count)
    proj = projections.reshape(slices, rows, nev)

    def swap_mom(array, i):
        return lax.ppermute(array, "mom", [(a, a ^ i) for a in range(mom_count)])

    def swap_snk(array):
        pairs = [(a, (a + half_snk) % snk_count) for a in range(snk_count)]
        return lax.ppermute(array, "snk", pairs)

    def next_src(array, step=1, i=0):
        pairs = [
            (((a + step) % src_count) * mom_count + (b ^ i), a * mom_count + b)
            for a in range(src_count)
            for b in range(mom_count)
        ]
        return lax.ppermute(array, ("src", "mom"), pairs)

    def most_of(array, amount):
        step = 1
        while 2 * step < src_count:
            array = jnp.where((amount // step) % 2 != 0, next_src(array, step), array)
            step *= 2
        return array, next_src(array, step)

    def call(kernel, name, in_specs, out_specs, out_shape, scratch, mib, aliases=None):
        cost = pl.CostEstimate(flops=WEIGHT, bytes_accessed=WEIGHT // 1000, transcendentals=0)
        return pl.pallas_call(
            kernel,
            in_specs=in_specs,
            out_specs=out_specs,
            out_shape=out_shape,
            scratch_shapes=scratch,
            input_output_aliases=aliases or {},
            compiler_params=limit(mib),
            cost_estimate=cost,
            name=name,
        )

    def bf16(*shape):
        return jax.ShapeDtypeStruct(shape, jnp.bfloat16)

    def dma(count):
        return pltpu.SemaphoreType.DMA((count,))

    part = functools.partial
    split = (width * 5 // 8) // 16 * 16
    two = bf16(2 * rows, nev)
    tagged = bf16(2 * rows + TAG_ROWS, nev)
    first_shape, rest_shape = bf16(2, split, width), bf16(2, width - split, width)
    token = bf16(16, 128)

    def buffers(shapes):
        return [pltpu.VMEM(shape.shape, shape.dtype) for shape in shapes]

    def alias(kernel, name, in_specs, out_shape, aliases, operands):
        return pl.pallas_call(
            kernel,
            in_specs=in_specs,
            out_specs=[anywhere()] * len(aliases) + [vmem()],
            out_shape=out_shape,
            input_output_aliases=aliases,
            compiler_params=limit(16),
            cost_estimate=pl.CostEstimate(
                flops=WEIGHT, bytes_accessed=WEIGHT // 1000, transcendentals=0
            ),
            name=name,
        )(*operands)

    leaving = [first_shape, tagged, tagged, rest_shape]
    first, core, own, rest = call(
        part(pack, sizes),
        "pack",
        [smem()] * 2 + [hbm()] * 2,
        [hbm()] * len(leaving),
        leaving,
        buffers(leaving) + [dma(6), dma(len(leaving))],
        58,
    )(separations, partner, peram_blocks, proj)

    plan = Plan(separations, sizes)
    first = swap_snk(first)
    core = swap_mom(core, 1)
    own = swap_mom(own, 2)
    rest_near, rest_far = most_of(rest, plan.peer_hops())
    forward = swap_mom(own, 1)
    leaving = [two, two, bf16(2, width, width)]
    far_same, far_cross, block = call(
        part(pack_far, sizes),
        "pack_far",
        [smem()] + [hbm()] * 3,
        [hbm()] * len(leaving),
        leaving,
        buffers(leaving) + [dma(5), dma(len(leaving))],
        58,
    )(separations, peram_blocks, proj, core)
    if src_count == 2:
        far_same, far_cross = next_src(far_same), next_src(far_cross, 1, 2)

    u_scratch = pltpu.VMEM((width, 2 * width), jnp.bfloat16)
    v_scratch = pltpu.VMEM((2 * width, 2 * width), jnp.bfloat16)
    turns = pltpu.VMEM((nterm, 4, nev, nev), jnp.bfloat16)
    products = bf16(mom_count, width, 2 * width)
    y, h = call(
        own_kernel_01,
        "own_products_01",
        [smem()] + [hbm()] * 3,
        [vmem()] * 2,
        [bf16(2 * width, 2 * width), products],
        [
            pltpu.VMEM((2, width, width), jnp.bfloat16),
            pltpu.VMEM((2, rows, nev), jnp.bfloat16),
            u_scratch,
            u_scratch,
            turns,
            turns,
            dma(3),
        ],
        16,
    )(gamma_index, block, proj, core)
    h, label, done_h = call(
        part(own_kernel_23, sizes),
        "own_products_23",
        [smem()] * 3 + [hbm()] * 3 + [vmem()] * 2,
        [vmem(), smem(), vmem()],
        [products, jax.ShapeDtypeStruct((2 * mom_count,), jnp.int32), token],
        [
            pltpu.VMEM((2, rows, nev), jnp.bfloat16),
            u_scratch,
            u_scratch,
            turns,
            turns,
            pltpu.VMEM((3, TAG_ROWS, nev), jnp.bfloat16),
            dma(5),
        ],
        16,
        {7: 0},
    )(separations, gamma_index, partner, core, own, forward, y, h)

    if src_count > 2:
        rest_near = jnp.where(plan.peer_hops() // (src_count // 2) != 0, rest_far, rest_near)
        rest_far = rest_near
    rest, near = call(
        part(choose, sizes),
        "choose",
        [smem()] + [hbm()] * 3 + [vmem()],
        [vmem()] * 2,
        [rest_shape, two],
        [dma(3)],
        16,
    )(separations, rest_near, rest_far, proj, done_h)
    near = swap_mom(near, 2)
    first, rest, opened = alias(
        gate,
        "gate",
        [anywhere()] * 2,
        [first_shape, rest_shape, token],
        {0: 0, 1: 1},
        (first, rest),
    )
    rest = swap_snk(rest)
    first_near, first_far = most_of(first, plan.hops(0))
    other_trade = call(
        part(other_pack, sizes),
        "other_pack",
        [smem()] + [hbm()] * 4 + [vmem()],
        vmem(),
        two,
        [dma(2)],
        16,
    )(separations, proj, near, far_same, far_cross, opened)
    other_got = swap_mom(other_trade, 1)
    if src_count != 2:

        def moved(array):
            if src_count == 1:
                return array
            array, away = most_of(array, plan.hops(0))
            return jnp.where(plan.hops(0) // (src_count // 2) != 0, away, array)

        far_same = moved(lax.dynamic_index_in_dim(proj, plan.local(0), 0, keepdims=False))
        far_cross, other_got = moved(near[:rows]), moved(other_got)

    k_shape = jax.ShapeDtypeStruct((2, width, 2 * width), jnp.float32)
    scratch = [pltpu.VMEM((2, rows, nev), jnp.bfloat16), v_scratch, v_scratch, turns, turns, dma(2)]
    ka = call(
        part(other_kernel_02, sizes),
        "other_products_02",
        [smem()] * 3 + [vmem()] + [hbm()] * 4,
        vmem(),
        k_shape,
        scratch,
        20,
    )(separations, gamma_index, label, h, proj, near, far_same, far_cross)
    kb = call(
        other_kernel_13,
        "other_products_13",
        [smem()] * 2 + [vmem(), hbm()],
        vmem(),
        k_shape,
        scratch,
        20,
    )(gamma_index, label, h, other_got)

    sums = call(
        part(early_kernel, sizes),
        "early_traces",
        [smem()] + [vmem()] * 2 + [hbm()] * 2,
        vmem(),
        jax.ShapeDtypeStruct((2 * mom_count, 16, nev), jnp.float32),
        [pltpu.VMEM((2, split, width), jnp.bfloat16), dma(1)],
        20,
    )(separations, ka, kb, first_near, first_far)
    device_count = src_count * snk_count * mom_count
    values = time_count * sep_count * 2
    lines = (values + 127) // 128
    out = call(
        part(late_kernel, sizes, sep_count),
        "late_traces",
        [smem()] * 2 + [vmem()] * 4,
        vmem(),
        jax.ShapeDtypeStruct((device_count, lines, 128), jnp.float32),
        [],
        20,
    )(separations, label, ka, kb, rest, sums)
    out = lax.all_to_all(out, ("src", "snk", "mom"), split_axis=0, concat_axis=0, tiled=True)
    out = jnp.sum(out, axis=0).reshape(lines * 128)[:values]
    return out.reshape(time_count, sep_count, 1, 2)


def solution(mesh):
    placed = (
        P("src", "snk", None, None, None),
        P("src", "mom", None, None, None, None),
        P(),
        P("mom"),
        P(),
    )
    return jax.shard_map(
        shards, mesh=mesh, in_specs=placed, out_specs=P(None, None, "mom", None), check_vma=False
    )
```

```python
import functools

import jax
import jax.numpy as jnp
from jax import lax
from jax.experimental import pallas as pl
from jax.experimental.pallas import tpu as pltpu
from jax.sharding import PartitionSpec as P

NSPIN = 4
NT_DIMS = (((1,), (1,)), ((), ()))
MIB = 1024 * 1024
WEIGHT = 10**13
TAG_ROWS = 16
TILE = 256
GAMMAS = (
    (3, 1 | 1 << 2 | 3 << 4 | 3 << 6),
    (3, 2 | 0 << 2 | 0 << 4 | 2 << 6),
    (2, 1 | 3 << 2 | 3 << 4 | 1 << 6),
    (2, 0),
)


def spin_entry(code, row):
    phase = row * 0
    for bit, (flip, phases) in enumerate(GAMMAS):
        on = (code >> bit) & 1
        phase = phase + on * ((phases >> (2 * row)) & 3)
        row = row ^ (on * flip)
    return row, phase & 3


def fill_spin_blocks(codes, turns, write):
    for r, code in enumerate(codes):
        for spin in range(NSPIN):
            column, phase = spin_entry(code, spin)
            write(spin, column, *(turns[r, (n - phase) & 3] for n in (4, 1)))


def set_turns(turns, r, real, imag):
    for n, value in enumerate((real, imag, -real, -imag)):
        turns[r, n] = value


def add_to(ref, rows, lanes, value):
    ref[rows, lanes] = ref[rows, lanes] + value


def along(spin, nev, start=0):
    if isinstance(spin, int):
        return slice(start + spin * nev, start + (spin + 1) * nev)
    return pl.ds(pl.multiple_of(start + spin * nev, nev), nev)


class Plan:
    def __init__(self, seps, sizes):
        slices, offsets, src_count, snk_count = sizes
        src, snk, self.mom = (lax.axis_index(name) for name in ("src", "snk", "mom"))
        half_snk = snk_count // 2
        self.slices, self.time_count = slices, slices * src_count
        self.forward = snk < half_snk
        base = lax.rem(snk, half_snk) * offsets
        self.keep = jnp.where(self.forward, 0, offsets - 1)
        self.give = offsets - 1 - self.keep
        self.sep_index = base + self.keep
        sign = jnp.where(self.forward, 1, -1)
        self.shift = sign * seps[base + self.keep]
        self.peer_shift = -sign * seps[base + self.give]
        self.own_time = src * slices + self.mom
        late = jnp.where(self.forward, 0, self.shift)
        self.pair_time = lax.rem(self.own_time + late + self.time_count, self.time_count)
        self.live = self.forward if offsets == 1 else None

    def _sum(self, place, amount):
        return lax.rem(place + amount + self.time_count, self.time_count)

    def local(self, i):
        return lax.rem(self._sum(self.mom ^ i, self.shift), self.slices)

    def hops(self, i):
        return lax.div(self._sum(self.mom ^ i, self.shift), self.slices)

    def peer_local(self):
        return lax.rem(self._sum(self.mom, self.peer_shift), self.slices)

    def peer_hops(self):
        return lax.div(self._sum(self.mom, self.peer_shift), self.slices)


def run_copies(copies, sems):
    handles = [
        pltpu.make_async_copy(source, target, sems.at[n])
        for n, (source, target) in enumerate(copies)
    ]
    for handle in handles:
        handle.start()
    for handle in handles:
        handle.wait()


def span(index, rows):
    return pl.ds(index * rows, rows)


def through(parts, ins, leaving):
    started, n = [], 0
    for copies, buffer, target in parts:
        group = []
        for source, spot in copies:
            group.append(pltpu.make_async_copy(source, spot, ins.at[n]))
            group[-1].start()
            n += 1
        started.append(group)
    handles = []
    for n, (group, (_, buffer, target)) in enumerate(zip(started, parts)):
        for handle in group:
            handle.wait()
        handles.append(pltpu.make_async_copy(buffer, target, leaving.at[n]))
        handles[-1].start()
    for handle in handles:
        handle.wait()


def two_slices(proj, buffer, first, second):
    rows = proj.shape[1]
    return [(proj.at[n], buffer.at[span(i, rows)]) for i, n in enumerate((first, second))]


def tag_of(partner, lanes):
    number = jnp.full((TAG_ROWS, lanes), partner[0].astype(jnp.float32))
    return number.astype(jnp.bfloat16)


def pack_first(sizes, seps, peram, out, token, buffer, ins, leaving):
    plan = Plan(seps, sizes)
    source = peram.at[plan.peer_local(), plan.give, :, pl.ds(0, out.shape[1])]
    through([([(source, buffer)], buffer, out)], ins, leaving)
    token[...] = jnp.zeros(token.shape, token.dtype)


def pack(sizes, seps, partner, peram, proj, after, *refs):
    outs, buffers, (ins, leaving) = refs[:5], refs[5:10], refs[10:]
    plan = Plan(seps, sizes)
    rows = proj.shape[1]
    mom = plan.mom
    own, rest, same, cross, block = buffers
    own[pl.ds(2 * rows, TAG_ROWS), :] = tag_of(partner, proj.shape[-1])
    start = peram.shape[-2] - rest.shape[1]
    source = peram.at[plan.peer_local(), plan.give, :, pl.ds(start, rest.shape[1])]
    copies = [
        two_slices(proj, own, mom ^ 2, mom ^ 3),
        [(source, rest)],
        two_slices(proj, same, plan.local(0), plan.local(1)),
        two_slices(proj, cross, plan.local(2), plan.local(3)),
        [(peram.at[mom, plan.keep], block)],
    ]
    through(list(zip(copies, buffers, outs)), ins, leaving)


def pack_later(sizes, seps, partner, proj, own, after, *refs):
    outs, buffers, (ins, leaving) = refs[:2], refs[2:4], refs[4:]
    plan = Plan(seps, sizes)
    rows = proj.shape[1]
    trade, near = buffers
    trade[pl.ds(2 * rows, TAG_ROWS), :] = tag_of(partner, proj.shape[-1])
    spot = pl.ds(2 * rows, TAG_ROWS)
    copies = [
        [
            (proj.at[plan.mom ^ 1], trade.at[span(0, rows)]),
            (own.at[span(1, rows)], trade.at[span(1, rows)]),
            (own.at[spot], trade.at[pl.ds(2 * rows + TAG_ROWS, TAG_ROWS)]),
        ],
        two_slices(proj, near, plan.local(2), plan.local(3)),
    ]
    through(list(zip(copies, buffers, outs)), ins, leaving)


def choose(sizes, seps, near, far, after, out, sems):
    flag = lax.rem(Plan(seps, sizes).peer_hops(), 2)

    @pl.when(flag == 0)
    def _():
        run_copies([(near, out)], sems)

    @pl.when(flag != 0)
    def _():
        run_copies([(far, out)], sems)


def gate(first, rest, after, first_out, rest_out, token):
    token[...] = jnp.zeros(token.shape, token.dtype)


def other_pack(sizes, seps, proj, near, far_same, far_cross, after, out, sems):
    plan = Plan(seps, sizes)
    rows = out.shape[0] // 2
    flag = lax.rem(plan.hops(1), 2) if sizes[2] == 2 else jnp.int32(0)
    low, high = out.at[span(0, rows)], out.at[span(1, rows)]

    @pl.when(flag == 0)
    def _():
        run_copies([(proj.at[plan.local(1)], low), (near.at[span(1, rows)], high)], sems)

    @pl.when(flag != 0)
    def _():
        run_copies([(far_same.at[span(1, rows)], low), (far_cross.at[span(1, rows)], high)], sems)


def own_fill(codes, p_ref, n, u_ref, turns):
    nev = turns.shape[-1]
    width = u_ref.shape[0]
    for r in range(len(codes)):
        real, imag = (p_ref[n, m * nev : (m + 1) * nev].T for m in (2 * r, 2 * r + 1))
        set_turns(turns, r, real, imag)
    u_ref[...] = jnp.zeros(u_ref.shape, u_ref.dtype)

    def write(spin, column, a, b):
        add_to(u_ref, along(column, nev), along(spin, nev), a)
        add_to(u_ref, along(column, nev), along(spin, nev, width), b)

    fill_spin_blocks(codes, turns, write)


def own_dot(u_ref, y_ref, ht):
    width = u_ref.shape[0]
    for tile in range(2 * width // TILE):
        start = tile * TILE
        out = lax.dot_general(
            u_ref[...], y_ref[start : start + TILE, :], NT_DIMS, preferred_element_type=jnp.float32
        ).astype(jnp.bfloat16)
        if start < width:
            ht[:, width + start : width + start + TILE] = out
        else:
            ht[:, start - width : start - width + TILE] = out
            ht[:, width + start : width + start + TILE] = -out


def codes_of(gamma, op, nterm):
    return [gamma[op, r] for r in range(nterm)]


def own_kernel_0(gamma, block, proj, y_ref, h_ref, token, x_ref, p_ref, u_ref, turns, sems):
    mom = lax.axis_index("mom")
    run_copies([(block, x_ref), (proj.at[mom], p_ref.at[0])], sems)
    width = x_ref.shape[-1]
    real, imag = x_ref[0], x_ref[1]
    y_ref[:width, :width] = real
    y_ref[:width, width:] = -imag
    y_ref[width:, :width] = imag
    y_ref[width:, width:] = real
    own_fill(codes_of(gamma, mom, turns.shape[0]), p_ref, 0, u_ref, turns)
    own_dot(u_ref, y_ref, h_ref.at[0])
    token[...] = jnp.zeros(token.shape, token.dtype)


def own_kernel_2(gamma, own, y_ref, h_in, h_ref, token, p_ref, u_ref, turns, sems):
    run_copies([(own.at[span(0, p_ref.shape[1])], p_ref.at[0])], sems)
    codes = codes_of(gamma, lax.axis_index("mom") ^ 2, turns.shape[0])
    own_fill(codes, p_ref, 0, u_ref, turns)
    own_dot(u_ref, y_ref, h_ref.at[2])
    token[...] = jnp.zeros(token.shape, token.dtype)


def own_kernel_13(sizes, seps, gamma, partner, own, traded, y_ref, h_in, after, *refs):
    h_ref, label, token, p_ref, u0, u1, turns0, turns1, tags, sems = refs
    rows = p_ref.shape[1]
    spots = [pl.ds(2 * rows, TAG_ROWS), pl.ds(2 * rows + TAG_ROWS, TAG_ROWS)]
    run_copies(
        [
            (traded.at[span(0, rows)], p_ref.at[0]),
            (traded.at[span(1, rows)], p_ref.at[1]),
            (traded.at[spots[0]], tags.at[0]),
            (own.at[spots[0]], tags.at[1]),
            (traded.at[spots[1]], tags.at[2]),
        ],
        sems,
    )
    plan = Plan(seps, sizes)
    mom = plan.mom
    partners = [partner[0]] + [
        jnp.max(tags[n].astype(jnp.float32)).astype(jnp.int32) for n in range(3)
    ]
    count = len(partners)
    for p in range(count):
        back = jnp.int32(0)
        for i, value in enumerate(partners):
            back = back + jnp.where(value == (mom ^ p), mom ^ i, 0)
        label[p] = jnp.where(plan.forward, back, mom ^ p)
        label[count + p] = jnp.where(plan.forward, back, partners[p]) ^ mom
    nterm = turns0.shape[0]
    own_fill(codes_of(gamma, mom ^ 1, nterm), p_ref, 0, u0, turns0)
    own_dot(u0, y_ref, h_ref.at[1])
    own_fill(codes_of(gamma, mom ^ 3, nterm), p_ref, 1, u1, turns1)
    own_dot(u1, y_ref, h_ref.at[3])
    token[...] = jnp.zeros(token.shape, token.dtype)


def other_products(pieces, gamma, label, h_ref, refs):
    k_ref, p_ref, wa, wb, turns_a, turns_b = refs
    mom = lax.axis_index("mom")
    nterm, nev = turns_a.shape[0], turns_a.shape[-1]
    width = wa.shape[0]
    for n, piece in enumerate(pieces):
        w_ref, turns = ((wa, turns_a), (wb, turns_b))[n % 2]
        for r in range(nterm):
            real, imag = (p_ref[n, m * nev : (m + 1) * nev] for m in (2 * r, 2 * r + 1))
            set_turns(turns, r, real, imag)
        w_ref[...] = jnp.zeros(w_ref.shape, w_ref.dtype)

        def write(spin, column, a, b, w_ref=w_ref):
            add_to(w_ref, along(spin, nev), along(column, nev), a)
            add_to(w_ref, along(spin, nev), along(column, nev, width), b)

        fill_spin_blocks(codes_of(gamma, mom ^ piece, nterm), turns, write)
        own = label[4 + piece]
        for tile in range(width // TILE):
            lanes = slice(tile * TILE, (tile + 1) * TILE)
            weights = w_ref[lanes, :]
            k_ref[n, :width, lanes] = lax.dot_general(
                h_ref[own, :, width:], weights, NT_DIMS, preferred_element_type=jnp.float32
            )
            k_ref[n, width:, lanes] = lax.dot_general(
                h_ref[own, :, : 2 * width], weights, NT_DIMS, preferred_element_type=jnp.float32
            )


def other_kernel_02(sizes, seps, gamma, label, h_ref, proj, near, far_same, far_cross, *refs):
    k_ref, p_ref, wa, wb, turns_a, turns_b, sems = refs
    plan = Plan(seps, sizes)
    rows = p_ref.shape[1]
    low = span(0, rows)
    flag = lax.rem(plan.hops(0), 2) if sizes[2] == 2 else jnp.int32(1)

    @pl.when(flag == 0)
    def _():
        run_copies([(proj.at[plan.local(0)], p_ref.at[0]), (near.at[low], p_ref.at[1])], sems)

    @pl.when(flag != 0)
    def _():
        run_copies([(far_same.at[low], p_ref.at[0]), (far_cross.at[low], p_ref.at[1])], sems)

    out = (k_ref, p_ref, wa, wb, turns_a, turns_b)
    other_products((0, 2), gamma, label, h_ref, out)


def other_kernel_13(gamma, label, h_ref, traded, k_ref, p_ref, wa, wb, turns_a, turns_b, sems):
    rows = p_ref.shape[1]
    run_copies([(traded.at[span(n, rows)], p_ref.at[n]) for n in range(2)], sems)
    out = (k_ref, p_ref, wa, wb, turns_a, turns_b)
    other_products((1, 3), gamma, label, h_ref, out)


def row_sums(k_refs, source, offset, totals):
    rows = 16
    width = source.shape[-1]
    nev = totals[0].shape[-1]

    def step(index, totals):
        row = pl.multiple_of(index * rows, rows)
        here = pl.ds(pl.multiple_of(offset + row, rows), rows)
        later = pl.ds(pl.multiple_of(width + offset + row, rows), rows)
        totals = list(totals)
        for spin in range(NSPIN):
            lanes = along(spin, nev)
            real = source[0, pl.ds(row, rows), lanes].astype(jnp.float32)
            imag = source[1, pl.ds(row, rows), lanes].astype(jnp.float32)
            for n in range(len(totals) // 2):
                k_ref, p = k_refs[n // 2], n % 2
                kr, ki = k_ref[p, here, lanes], k_ref[p, later, lanes]
                totals[2 * n] += real * kr - imag * ki
                totals[2 * n + 1] += real * ki + imag * kr
        return tuple(totals)

    return lax.fori_loop(0, source.shape[1] // rows, step, totals)


def trace_kernel(sizes, sep_count, seps, label, ka, kb, near, far, rest, out_ref, first_buf, rest_buf, sems):
    plan = Plan(seps, sizes)
    count = 2 * ka.shape[0]
    width = rest_buf.shape[-1]
    nev = width // NSPIN
    flag = lax.rem(lax.div(plan.hops(0), max(sizes[2] // 2, 1)), 2)
    later = pltpu.make_async_copy(rest, rest_buf, sems.at[1])
    later.start()

    @pl.when(flag == 0)
    def _():
        run_copies([(near, first_buf)], sems)

    @pl.when(flag != 0)
    def _():
        run_copies([(far, first_buf)], sems)

    totals = tuple(jnp.zeros((16, nev), jnp.float32) for _ in range(2 * count))
    totals = row_sums((ka, kb), first_buf, 0, totals)
    later.wait()
    totals = row_sums((ka, kb), rest_buf, first_buf.shape[1], totals)
    sums = [jnp.sum(total, axis=0, keepdims=True) for total in totals]
    sums = [jnp.sum(total, axis=1, keepdims=True) * (1.0 / width) for total in sums]
    shape = out_ref.shape[1:]
    spot = lax.broadcasted_iota(jnp.int32, shape, 0) * shape[1]
    spot = spot + lax.broadcasted_iota(jnp.int32, shape, 1)
    here = spot // 2 == plan.pair_time * sep_count + plan.sep_index
    if plan.live is not None:
        here = here & plan.live
    values = [jnp.where(spot % 2 == 0, sums[2 * p], sums[2 * p + 1]) for p in range(count)]
    lines = []
    for op in range(count):
        line = jnp.zeros(shape, jnp.float32)
        for p, value in zip((0, 2, 1, 3), values):
            line = jnp.where(label[p] == op, value, line)
        lines.append(jnp.where(here, line, 0.0))
    for n in range(out_ref.shape[0]):
        out_ref[n] = lines[n % count]


def smem():
    return pl.BlockSpec(memory_space=pltpu.SMEM)


def vmem():
    return pl.BlockSpec(memory_space=pltpu.VMEM)


def anywhere():
    return pl.BlockSpec(memory_space=pl.ANY)


def hbm():
    return pl.BlockSpec(memory_space=pltpu.HBM)


def limit(mib):
    return pltpu.CompilerParams(vmem_limit_bytes=mib * MIB)


def shards(peram_blocks, projections, gamma_index, partner, separations):
    src_count, snk_count = lax.axis_size("src"), lax.axis_size("snk")
    mom_count = lax.axis_size("mom")
    slices, offsets = peram_blocks.shape[:2]
    width = peram_blocks.shape[-1]
    nterm, nev = projections.shape[2], projections.shape[-1]
    time_count = slices * src_count
    sep_count = separations.shape[0]
    half_snk = snk_count // 2
    rows = nterm * 2 * nev
    sizes = (slices, offsets, src_count, snk_count)
    proj = projections.reshape(slices, rows, nev)

    def swap_mom(array, i):
        return lax.ppermute(array, "mom", [(a, a ^ i) for a in range(mom_count)])

    def swap_snk(array):
        pairs = [(a, (a + half_snk) % snk_count) for a in range(snk_count)]
        return lax.ppermute(array, "snk", pairs)

    def next_src(array, step=1, i=0):
        pairs = [
            (((a + step) % src_count) * mom_count + (b ^ i), a * mom_count + b)
            for a in range(src_count)
            for b in range(mom_count)
        ]
        return lax.ppermute(array, ("src", "mom"), pairs)

    def most_of(array, amount):
        step = 1
        while 2 * step < src_count:
            array = jnp.where((amount // step) % 2 != 0, next_src(array, step), array)
            step *= 2
        return array, next_src(array, step)

    def call(kernel, name, in_specs, out_specs, out_shape, scratch, mib, aliases=None):
        cost = pl.CostEstimate(flops=WEIGHT, bytes_accessed=WEIGHT // 1000, transcendentals=0)
        return pl.pallas_call(
            kernel,
            in_specs=in_specs,
            out_specs=out_specs,
            out_shape=out_shape,
            scratch_shapes=scratch,
            input_output_aliases=aliases or {},
            compiler_params=limit(mib),
            cost_estimate=cost,
            name=name,
        )

    def bf16(*shape):
        return jax.ShapeDtypeStruct(shape, jnp.bfloat16)

    def dma(count):
        return pltpu.SemaphoreType.DMA((count,))

    part = functools.partial
    split = (width * 5 // 8) // 16 * 16
    two = bf16(2 * rows, nev)
    tagged = bf16(2 * rows + TAG_ROWS, nev)
    first_shape, rest_shape = bf16(2, split, width), bf16(2, width - split, width)
    token = bf16(16, 128)

    def buffers(shapes):
        return [pltpu.VMEM(shape.shape, shape.dtype) for shape in shapes]

    def alias(kernel, name, in_specs, out_shape, aliases, operands):
        return pl.pallas_call(
            kernel,
            in_specs=in_specs,
            out_specs=[anywhere()] * len(aliases) + [vmem()],
            out_shape=out_shape,
            input_output_aliases=aliases,
            compiler_params=limit(16),
            cost_estimate=pl.CostEstimate(
                flops=WEIGHT, bytes_accessed=WEIGHT // 1000, transcendentals=0
            ),
            name=name,
        )(*operands)

    first, tick = call(
        part(pack_first, sizes),
        "pack_first",
        [smem(), hbm()],
        [hbm(), vmem()],
        [first_shape, token],
        buffers([first_shape]) + [dma(1), dma(1)],
        58,
    )(separations, peram_blocks)
    leaving = [tagged, rest_shape, two, two, bf16(2, width, width)]
    own, rest, far_same, far_cross, block = call(
        part(pack, sizes),
        "pack",
        [smem()] * 2 + [hbm()] * 2 + [vmem()],
        [hbm()] * len(leaving),
        leaving,
        buffers(leaving) + [dma(8), dma(len(leaving))],
        58,
    )(separations, partner, peram_blocks, proj, swap_mom(tick, 1))

    plan = Plan(separations, sizes)
    first = swap_snk(first)
    own = swap_mom(own, 2)
    rest_near, rest_far = most_of(rest, plan.peer_hops())
    if src_count == 2:
        far_same, far_cross = next_src(far_same), next_src(far_cross, 1, 2)
    u_scratch = pltpu.VMEM((width, 2 * width), jnp.bfloat16)
    turns = pltpu.VMEM((nterm, 4, nev, nev), jnp.bfloat16)
    piece = pltpu.VMEM((1, rows, nev), jnp.bfloat16)
    pieces = pltpu.VMEM((2, rows, nev), jnp.bfloat16)
    products = bf16(mom_count, width, 3 * width)
    y, h, done_0 = call(
        own_kernel_0,
        "own_products_0",
        [smem()] + [hbm()] * 2,
        [vmem()] * 3,
        [bf16(2 * width, 2 * width), products, token],
        [pltpu.VMEM((2, width, width), jnp.bfloat16), piece, u_scratch, turns, dma(2)],
        16,
    )(gamma_index, block, proj)
    leaving = [bf16(2 * (rows + TAG_ROWS), nev), two]
    traded, near = call(
        part(pack_later, sizes),
        "pack_later",
        [smem()] * 2 + [hbm()] * 2 + [vmem()],
        [hbm()] * len(leaving),
        leaving,
        buffers(leaving) + [dma(5), dma(len(leaving))],
        16,
    )(separations, partner, proj, own, done_0)
    traded = swap_mom(traded, 1)
    near = swap_mom(near, 2)
    h, done_2 = call(
        own_kernel_2,
        "own_products_2",
        [smem(), hbm()] + [vmem()] * 2,
        [vmem()] * 2,
        [products, token],
        [piece, u_scratch, turns, dma(1)],
        16,
        {3: 0},
    )(gamma_index, own, y, h)

    if src_count > 2:
        rest_near = jnp.where(plan.peer_hops() // (src_count // 2) != 0, rest_far, rest_near)
        rest_far = rest_near
    rest = call(
        part(choose, sizes),
        "choose",
        [smem()] + [hbm()] * 2 + [vmem()],
        vmem(),
        rest_shape,
        [dma(1)],
        16,
    )(separations, rest_near, rest_far, done_0)
    first, rest, opened = alias(
        gate,
        "gate",
        [anywhere()] * 2 + [vmem()],
        [first_shape, rest_shape, token],
        {0: 0, 1: 1},
        (first, rest, done_2),
    )
    rest = swap_snk(rest)
    first_near, first_far = most_of(first, plan.hops(0))
    h, label, done_h = call(
        part(own_kernel_13, sizes),
        "own_products_13",
        [smem()] * 3 + [hbm()] * 2 + [vmem()] * 3,
        [vmem(), smem(), vmem()],
        [products, jax.ShapeDtypeStruct((2 * mom_count,), jnp.int32), token],
        [pieces, u_scratch, u_scratch, turns, turns]
        + [pltpu.VMEM((3, TAG_ROWS, nev), jnp.bfloat16), dma(5)],
        16,
        {6: 0},
    )(separations, gamma_index, partner, own, traded, y, h, opened)

    other_trade = call(
        part(other_pack, sizes),
        "other_pack",
        [smem()] + [hbm()] * 4 + [vmem()],
        vmem(),
        two,
        [dma(2)],
        16,
    )(separations, proj, near, far_same, far_cross, done_h)
    other_got = swap_mom(other_trade, 1)
    if src_count != 2:

        def moved(array):
            if src_count == 1:
                return array
            array, away = most_of(array, plan.hops(0))
            return jnp.where(plan.hops(0) // (src_count // 2) != 0, away, array)

        far_same = moved(lax.dynamic_index_in_dim(proj, plan.local(0), 0, keepdims=False))
        far_cross, other_got = moved(near[:rows]), moved(other_got)

    k_shape = jax.ShapeDtypeStruct((2, 2 * width, width), jnp.float32)
    scratch = [pieces, u_scratch, u_scratch, turns, turns, dma(2)]
    ka = call(
        part(other_kernel_02, sizes),
        "other_products_02",
        [smem()] * 3 + [vmem()] + [hbm()] * 4,
        vmem(),
        k_shape,
        scratch,
        20,
    )(separations, gamma_index, label, h, proj, near, far_same, far_cross)
    kb = call(
        other_kernel_13,
        "other_products_13",
        [smem()] * 2 + [vmem(), hbm()],
        vmem(),
        k_shape,
        scratch,
        20,
    )(gamma_index, label, h, other_got)

    device_count = src_count * snk_count * mom_count
    values = time_count * sep_count * 2
    lines = (values + 127) // 128
    out = call(
        part(trace_kernel, sizes, sep_count),
        "traces",
        [smem()] * 2 + [vmem()] * 2 + [hbm()] * 3,
        vmem(),
        jax.ShapeDtypeStruct((device_count, lines, 128), jnp.float32),
        buffers([first_shape, rest_shape]) + [dma(2)],
        20,
    )(separations, label, ka, kb, first_near, first_far, rest)
    out = lax.all_to_all(out, ("src", "snk", "mom"), split_axis=0, concat_axis=0, tiled=True)
    out = jnp.sum(out, axis=0).reshape(lines * 128)[:values]
    return out.reshape(time_count, sep_count, 1, 2)


def solution(mesh):
    placed = (
        P("src", "snk", None, None, None),
        P("src", "mom", None, None, None, None),
        P(),
        P("mom"),
        P(),
    )
    return jax.shard_map(
        shards, mesh=mesh, in_specs=placed, out_specs=P(None, None, "mom", None), check_vma=False
    )
```

```python
import functools

import jax
import jax.numpy as jnp
from jax import lax
from jax.experimental import pallas as pl
from jax.experimental.pallas import tpu as pltpu
from jax.sharding import PartitionSpec as P

NSPIN = 4
NT_DIMS = (((1,), (1,)), ((), ()))
MIB = 1024 * 1024
WEIGHT = 10**13
TAG_ROWS = 16
TILE = 256
GAMMAS = (
    (3, 1 | 1 << 2 | 3 << 4 | 3 << 6),
    (3, 2 | 0 << 2 | 0 << 4 | 2 << 6),
    (2, 1 | 3 << 2 | 3 << 4 | 1 << 6),
    (2, 0),
)


def spin_entry(code, row):
    phase = row * 0
    for bit, (flip, phases) in enumerate(GAMMAS):
        on = (code >> bit) & 1
        phase = phase + on * ((phases >> (2 * row)) & 3)
        row = row ^ (on * flip)
    return row, phase & 3


def fill_spin_blocks(codes, turns, write):
    for r, code in enumerate(codes):
        for spin in range(NSPIN):
            column, phase = spin_entry(code, spin)
            write(spin, column, *(turns[r, (n - phase) & 3] for n in (4, 1)))


def set_turns(turns, r, real, imag):
    for n, value in enumerate((real, imag, -real, -imag)):
        turns[r, n] = value


def add_to(ref, rows, lanes, value):
    ref[rows, lanes] = ref[rows, lanes] + value


def along(spin, nev, start=0):
    if isinstance(spin, int):
        return slice(start + spin * nev, start + (spin + 1) * nev)
    return pl.ds(pl.multiple_of(start + spin * nev, nev), nev)


class Plan:
    def __init__(self, seps, sizes):
        slices, offsets, src_count, snk_count = sizes
        src, snk, self.mom = (lax.axis_index(name) for name in ("src", "snk", "mom"))
        half_snk = snk_count // 2
        self.slices, self.time_count = slices, slices * src_count
        self.forward = snk < half_snk
        base = lax.rem(snk, half_snk) * offsets
        self.keep = jnp.where(self.forward, 0, offsets - 1)
        self.give = offsets - 1 - self.keep
        self.sep_index = base + self.keep
        sign = jnp.where(self.forward, 1, -1)
        self.shift = sign * seps[base + self.keep]
        self.peer_shift = -sign * seps[base + self.give]
        self.own_time = src * slices + self.mom
        late = jnp.where(self.forward, 0, self.shift)
        self.pair_time = lax.rem(self.own_time + late + self.time_count, self.time_count)
        self.live = self.forward if offsets == 1 else None

    def _sum(self, place, amount):
        return lax.rem(place + amount + self.time_count, self.time_count)

    def local(self, i):
        return lax.rem(self._sum(self.mom ^ i, self.shift), self.slices)

    def hops(self, i):
        return lax.div(self._sum(self.mom ^ i, self.shift), self.slices)

    def peer_local(self):
        return lax.rem(self._sum(self.mom, self.peer_shift), self.slices)

    def peer_hops(self):
        return lax.div(self._sum(self.mom, self.peer_shift), self.slices)


def run_copies(copies, sems):
    handles = [
        pltpu.make_async_copy(source, target, sems.at[n])
        for n, (source, target) in enumerate(copies)
    ]
    for handle in handles:
        handle.start()
    for handle in handles:
        handle.wait()


def span(index, rows):
    return pl.ds(index * rows, rows)


def through(parts, ins, leaving):
    started, n = [], 0
    for copies, buffer, target in parts:
        group = []
        for source, spot in copies:
            group.append(pltpu.make_async_copy(source, spot, ins.at[n]))
            group[-1].start()
            n += 1
        started.append(group)
    handles = []
    for n, (group, (_, buffer, target)) in enumerate(zip(started, parts)):
        for handle in group:
            handle.wait()
        handles.append(pltpu.make_async_copy(buffer, target, leaving.at[n]))
        handles[-1].start()
    for handle in handles:
        handle.wait()


def two_slices(proj, buffer, first, second):
    rows = proj.shape[1]
    return [(proj.at[n], buffer.at[span(i, rows)]) for i, n in enumerate((first, second))]


def tag_of(partner, lanes):
    number = jnp.full((TAG_ROWS, lanes), partner[0].astype(jnp.float32))
    return number.astype(jnp.bfloat16)


def pack_first(sizes, seps, peram, out, token, buffer, ins, leaving):
    plan = Plan(seps, sizes)
    source = peram.at[plan.peer_local(), plan.give, :, pl.ds(0, out.shape[1])]
    through([([(source, buffer)], buffer, out)], ins, leaving)
    token[...] = jnp.zeros(token.shape, token.dtype)


def pack(sizes, seps, partner, peram, proj, after, *refs):
    outs, buffers, (ins, leaving) = refs[:6], refs[6:12], refs[12:]
    plan = Plan(seps, sizes)
    rows = proj.shape[1]
    mom = plan.mom
    own, rest, same, cross, block, near = buffers
    own[pl.ds(2 * rows, TAG_ROWS), :] = tag_of(partner, proj.shape[-1])
    start = peram.shape[-2] - rest.shape[1]
    source = peram.at[plan.peer_local(), plan.give, :, pl.ds(start, rest.shape[1])]
    copies = [
        two_slices(proj, own, mom ^ 2, mom ^ 3),
        [(source, rest)],
        two_slices(proj, same, plan.local(0), plan.local(1)),
        two_slices(proj, cross, plan.local(2), plan.local(3)),
        [(peram.at[mom, plan.keep], block)],
        two_slices(proj, near, plan.local(2), plan.local(3)),
    ]
    through(list(zip(copies, buffers, outs)), ins, leaving)


def pack_later(sizes, seps, partner, proj, own, after, out, buffer, ins, leaving):
    rows = proj.shape[1]
    plan = Plan(seps, sizes)
    buffer[pl.ds(3 * rows, TAG_ROWS), :] = tag_of(partner, proj.shape[-1])
    copies = [
        (proj.at[plan.mom ^ 1], buffer.at[span(0, rows)]),
        (own.at[span(1, rows)], buffer.at[span(1, rows)]),
        (proj.at[plan.local(1)], buffer.at[span(2, rows)]),
        (
            own.at[pl.ds(2 * rows, TAG_ROWS)],
            buffer.at[pl.ds(3 * rows + TAG_ROWS, TAG_ROWS)],
        ),
    ]
    through([(copies, buffer, out)], ins, leaving)


def choose(sizes, seps, near, far, after, out, sems):
    flag = lax.rem(Plan(seps, sizes).peer_hops(), 2)

    @pl.when(flag == 0)
    def _():
        run_copies([(near, out)], sems)

    @pl.when(flag != 0)
    def _():
        run_copies([(far, out)], sems)


def gate(first, rest, after, first_out, rest_out, token):
    token[...] = jnp.zeros(token.shape, token.dtype)


def gate_far(near, same, cross, h, near_out, same_out, cross_out, h_out):
    h_out[0, :16, :128] = h[0, :16, :128]


def own_fill(codes, p_ref, n, u_ref, turns):
    nev = turns.shape[-1]
    width = u_ref.shape[0]
    for r in range(len(codes)):
        real, imag = (p_ref[n, m * nev : (m + 1) * nev].T for m in (2 * r, 2 * r + 1))
        set_turns(turns, r, real, imag)
    u_ref[...] = jnp.zeros(u_ref.shape, u_ref.dtype)

    def write(spin, column, a, b):
        add_to(u_ref, along(column, nev), along(spin, nev), a)
        add_to(u_ref, along(column, nev), along(spin, nev, width), b)

    fill_spin_blocks(codes, turns, write)


def own_dot(u_ref, y_ref, ht):
    width = u_ref.shape[0]
    for tile in range(2 * width // TILE):
        start = tile * TILE
        out = lax.dot_general(
            u_ref[...], y_ref[start : start + TILE, :], NT_DIMS, preferred_element_type=jnp.float32
        ).astype(jnp.bfloat16)
        if start < width:
            ht[:, width + start : width + start + TILE] = out
        else:
            ht[:, start - width : start - width + TILE] = out
            ht[:, width + start : width + start + TILE] = -out


def codes_of(gamma, op, nterm):
    return [gamma[op, r] for r in range(nterm)]


def own_kernel_0(gamma, block, proj, y_ref, h_ref, token, x_ref, p_ref, u_ref, turns, sems):
    mom = lax.axis_index("mom")
    run_copies([(block, x_ref), (proj.at[mom], p_ref.at[0])], sems)
    width = x_ref.shape[-1]
    real, imag = x_ref[0], x_ref[1]
    y_ref[:width, :width] = real
    y_ref[:width, width:] = -imag
    y_ref[width:, :width] = imag
    y_ref[width:, width:] = real
    own_fill(codes_of(gamma, mom, turns.shape[0]), p_ref, 0, u_ref, turns)
    own_dot(u_ref, y_ref, h_ref.at[0])
    token[...] = jnp.zeros(token.shape, token.dtype)


def own_kernel_2(gamma, own, y_ref, h_in, h_ref, token, p_ref, u_ref, turns, sems):
    run_copies([(own.at[span(0, p_ref.shape[1])], p_ref.at[0])], sems)
    codes = codes_of(gamma, lax.axis_index("mom") ^ 2, turns.shape[0])
    own_fill(codes, p_ref, 0, u_ref, turns)
    own_dot(u_ref, y_ref, h_ref.at[2])
    token[...] = jnp.zeros(token.shape, token.dtype)


def own_kernel_13(sizes, seps, gamma, partner, own, traded, y_ref, h_in, after, *refs):
    h_ref, label, p_ref, u0, u1, turns0, turns1, tags, sems = refs
    rows = p_ref.shape[1]
    spots = [pl.ds(n * rows + m * TAG_ROWS, TAG_ROWS) for n, m in ((3, 0), (2, 0), (3, 1))]
    run_copies(
        [
            (traded.at[span(0, rows)], p_ref.at[0]),
            (traded.at[span(1, rows)], p_ref.at[1]),
            (traded.at[spots[0]], tags.at[0]),
            (own.at[spots[1]], tags.at[1]),
            (traded.at[spots[2]], tags.at[2]),
        ],
        sems,
    )
    plan = Plan(seps, sizes)
    mom = plan.mom
    partners = [partner[0]] + [
        jnp.max(tags[n].astype(jnp.float32)).astype(jnp.int32) for n in range(3)
    ]
    count = len(partners)
    for p in range(count):
        back = jnp.int32(0)
        for i, value in enumerate(partners):
            back = back + jnp.where(value == (mom ^ p), mom ^ i, 0)
        label[p] = jnp.where(plan.forward, back, mom ^ p)
        label[count + p] = jnp.where(plan.forward, back, partners[p]) ^ mom
    nterm = turns0.shape[0]
    own_fill(codes_of(gamma, mom ^ 1, nterm), p_ref, 0, u0, turns0)
    own_dot(u0, y_ref, h_ref.at[1])
    own_fill(codes_of(gamma, mom ^ 3, nterm), p_ref, 1, u1, turns1)
    own_dot(u1, y_ref, h_ref.at[3])


def other_products(pieces, gamma, label, h_ref, sources, refs):
    k_ref, p_ref, wa, wb, turns_a, turns_b, sems = refs
    mom = lax.axis_index("mom")
    nterm, nev = turns_a.shape[0], turns_a.shape[-1]
    width = wa.shape[0]
    (here, away), flag = sources

    @pl.when(flag == 0)
    def _():
        run_copies([(ref, p_ref.at[n]) for n, ref in enumerate(here)], sems)

    @pl.when(flag != 0)
    def _():
        run_copies([(ref, p_ref.at[n]) for n, ref in enumerate(away)], sems)

    for n, piece in enumerate(pieces):
        w_ref, turns = ((wa, turns_a), (wb, turns_b))[n % 2]
        for r in range(nterm):
            real, imag = (p_ref[n, m * nev : (m + 1) * nev] for m in (2 * r, 2 * r + 1))
            set_turns(turns, r, real, imag)
        w_ref[...] = jnp.zeros(w_ref.shape, w_ref.dtype)

        def write(spin, column, a, b, w_ref=w_ref):
            add_to(w_ref, along(spin, nev), along(column, nev), a)
            add_to(w_ref, along(spin, nev), along(column, nev, width), b)

        fill_spin_blocks(codes_of(gamma, mom ^ piece, nterm), turns, write)
        own = label[4 + piece]
        for tile in range(width // TILE):
            lanes = slice(tile * TILE, (tile + 1) * TILE)
            weights = w_ref[lanes, :]
            k_ref[n, :width, lanes] = lax.dot_general(
                h_ref[own, :, width:], weights, NT_DIMS, preferred_element_type=jnp.float32
            )
            k_ref[n, width:, lanes] = lax.dot_general(
                h_ref[own, :, : 2 * width], weights, NT_DIMS, preferred_element_type=jnp.float32
            )


def other_flag(plan, sizes):
    return lax.rem(plan.hops(0), 2) if sizes[2] == 2 else jnp.int32(1)


def other_kernel_02(sizes, seps, gamma, label, h_ref, proj, near, same, cross, *refs):
    plan = Plan(seps, sizes)
    low = span(0, proj.shape[1])
    here, away = (proj.at[plan.local(0)], near.at[low]), (same.at[low], cross.at[low])
    sources = ((here, away), other_flag(plan, sizes))
    other_products((0, 2), gamma, label, h_ref, sources, refs)


def other_kernel_13(sizes, seps, gamma, label, h_ref, traded, near, same, cross, *refs):
    plan = Plan(seps, sizes)
    rows = refs[1].shape[1]
    at = span(1 if sizes[2] == 2 else 0, rows)
    here = (traded.at[span(2, rows)], near.at[span(1, rows)])
    sources = ((here, (same.at[at], cross.at[at])), other_flag(plan, sizes))
    other_products((1, 3), gamma, label, h_ref, sources, refs)


def row_sums(k_refs, source, offset, totals):
    rows = 16
    width = source.shape[-1]
    nev = totals[0].shape[-1]

    def step(index, totals):
        row = pl.multiple_of(index * rows, rows)
        here = pl.ds(pl.multiple_of(offset + row, rows), rows)
        later = pl.ds(pl.multiple_of(width + offset + row, rows), rows)
        totals = list(totals)
        for spin in range(NSPIN):
            lanes = along(spin, nev)
            real = source[0, pl.ds(row, rows), lanes].astype(jnp.float32)
            imag = source[1, pl.ds(row, rows), lanes].astype(jnp.float32)
            for n in range(len(totals) // 2):
                k_ref, p = k_refs[n // 2], n % 2
                kr, ki = k_ref[p, here, lanes], k_ref[p, later, lanes]
                totals[2 * n] += real * kr - imag * ki
                totals[2 * n + 1] += real * ki + imag * kr
        return tuple(totals)

    return lax.fori_loop(0, source.shape[1] // rows, step, totals)


def trace_kernel(sizes, sep_count, seps, label, ka, kb, near, far, rest, out_ref, first_buf, rest_buf, sems):
    plan = Plan(seps, sizes)
    count = 2 * ka.shape[0]
    width = rest_buf.shape[-1]
    nev = width // NSPIN
    flag = lax.rem(lax.div(plan.hops(0), max(sizes[2] // 2, 1)), 2)
    later = pltpu.make_async_copy(rest, rest_buf, sems.at[1])
    later.start()

    @pl.when(flag == 0)
    def _():
        run_copies([(near, first_buf)], sems)

    @pl.when(flag != 0)
    def _():
        run_copies([(far, first_buf)], sems)

    totals = tuple(jnp.zeros((16, nev), jnp.float32) for _ in range(2 * count))
    totals = row_sums((ka, kb), first_buf, 0, totals)
    later.wait()
    totals = row_sums((ka, kb), rest_buf, first_buf.shape[1], totals)
    sums = [jnp.sum(total, axis=0, keepdims=True) for total in totals]
    sums = [jnp.sum(total, axis=1, keepdims=True) * (1.0 / width) for total in sums]
    shape = out_ref.shape[1:]
    spot = lax.broadcasted_iota(jnp.int32, shape, 0) * shape[1]
    spot = spot + lax.broadcasted_iota(jnp.int32, shape, 1)
    here = spot // 2 == plan.pair_time * sep_count + plan.sep_index
    if plan.live is not None:
        here = here & plan.live
    values = [jnp.where(spot % 2 == 0, sums[2 * p], sums[2 * p + 1]) for p in range(count)]
    lines = []
    for op in range(count):
        line = jnp.zeros(shape, jnp.float32)
        for p, value in zip((0, 2, 1, 3), values):
            line = jnp.where(label[p] == op, value, line)
        lines.append(jnp.where(here, line, 0.0))
    for n in range(out_ref.shape[0]):
        out_ref[n] = lines[n % count]


def smem():
    return pl.BlockSpec(memory_space=pltpu.SMEM)


def vmem():
    return pl.BlockSpec(memory_space=pltpu.VMEM)


def anywhere():
    return pl.BlockSpec(memory_space=pl.ANY)


def hbm():
    return pl.BlockSpec(memory_space=pltpu.HBM)


def limit(mib):
    return pltpu.CompilerParams(vmem_limit_bytes=mib * MIB)


def shards(peram_blocks, projections, gamma_index, partner, separations):
    src_count, snk_count = lax.axis_size("src"), lax.axis_size("snk")
    mom_count = lax.axis_size("mom")
    slices, offsets = peram_blocks.shape[:2]
    width = peram_blocks.shape[-1]
    nterm, nev = projections.shape[2], projections.shape[-1]
    time_count = slices * src_count
    sep_count = separations.shape[0]
    half_snk = snk_count // 2
    rows = nterm * 2 * nev
    sizes = (slices, offsets, src_count, snk_count)
    proj = projections.reshape(slices, rows, nev)

    def swap_mom(array, i):
        return lax.ppermute(array, "mom", [(a, a ^ i) for a in range(mom_count)])

    def swap_snk(array):
        pairs = [(a, (a + half_snk) % snk_count) for a in range(snk_count)]
        return lax.ppermute(array, "snk", pairs)

    def next_src(array, step=1, i=0):
        pairs = [
            (((a + step) % src_count) * mom_count + (b ^ i), a * mom_count + b)
            for a in range(src_count)
            for b in range(mom_count)
        ]
        return lax.ppermute(array, ("src", "mom"), pairs)

    def most_of(array, amount):
        step = 1
        while 2 * step < src_count:
            array = jnp.where((amount // step) % 2 != 0, next_src(array, step), array)
            step *= 2
        return array, next_src(array, step)

    def call(kernel, name, in_specs, out_specs, out_shape, scratch, mib, aliases=None):
        cost = pl.CostEstimate(flops=WEIGHT, bytes_accessed=WEIGHT // 1000, transcendentals=0)
        return pl.pallas_call(
            kernel,
            in_specs=in_specs,
            out_specs=out_specs,
            out_shape=out_shape,
            scratch_shapes=scratch,
            input_output_aliases=aliases or {},
            compiler_params=limit(mib),
            cost_estimate=cost,
            name=name,
        )

    def bf16(*shape):
        return jax.ShapeDtypeStruct(shape, jnp.bfloat16)

    def dma(count):
        return pltpu.SemaphoreType.DMA((count,))

    part = functools.partial
    split = (width * 5 // 8) // 16 * 16
    two = bf16(2 * rows, nev)
    tagged = bf16(2 * rows + TAG_ROWS, nev)
    first_shape, rest_shape = bf16(2, split, width), bf16(2, width - split, width)
    token = bf16(16, 128)

    def buffers(shapes):
        return [pltpu.VMEM(shape.shape, shape.dtype) for shape in shapes]

    def alias(kernel, name, in_specs, out_shape, aliases, operands):
        return pl.pallas_call(
            kernel,
            in_specs=in_specs,
            out_specs=[anywhere()] * len(aliases) + [vmem()],
            out_shape=out_shape,
            input_output_aliases=aliases,
            compiler_params=limit(20),
            cost_estimate=pl.CostEstimate(
                flops=WEIGHT, bytes_accessed=WEIGHT // 1000, transcendentals=0
            ),
            name=name,
        )(*operands)

    first, tick = call(
        part(pack_first, sizes),
        "pack_first",
        [smem(), hbm()],
        [hbm(), vmem()],
        [first_shape, token],
        buffers([first_shape]) + [dma(1), dma(1)],
        58,
    )(separations, peram_blocks)
    leaving = [tagged, rest_shape, two, two, bf16(2, width, width), two]
    own, rest, far_same, far_cross, block, near = call(
        part(pack, sizes),
        "pack",
        [smem()] * 2 + [hbm()] * 2 + [vmem()],
        [hbm()] * len(leaving),
        leaving,
        buffers(leaving) + [dma(10), dma(len(leaving))],
        58,
    )(separations, partner, peram_blocks, proj, swap_mom(tick, 1))

    plan = Plan(separations, sizes)
    first = swap_snk(first)
    own = swap_mom(own, 2)
    rest_near, rest_far = most_of(rest, plan.peer_hops())
    if src_count == 2:
        far_same, far_cross = next_src(far_same), next_src(far_cross, 1, 2)
    u_scratch = pltpu.VMEM((width, 2 * width), jnp.bfloat16)
    turns = pltpu.VMEM((nterm, 4, nev, nev), jnp.bfloat16)
    piece = pltpu.VMEM((1, rows, nev), jnp.bfloat16)
    pieces = pltpu.VMEM((2, rows, nev), jnp.bfloat16)
    products = bf16(mom_count, width, 3 * width)
    y, h, done_0 = call(
        own_kernel_0,
        "own_products_0",
        [smem()] + [hbm()] * 2,
        [vmem()] * 3,
        [bf16(2 * width, 2 * width), products, token],
        [pltpu.VMEM((2, width, width), jnp.bfloat16), piece, u_scratch, turns, dma(2)],
        20,
    )(gamma_index, block, proj)
    trade = bf16(3 * rows + 2 * TAG_ROWS, nev)
    traded = call(
        part(pack_later, sizes),
        "pack_later",
        [smem()] * 2 + [hbm()] * 2 + [vmem()],
        hbm(),
        trade,
        buffers([trade]) + [dma(4), dma(1)],
        20,
    )(separations, partner, proj, own, done_0)
    traded = swap_mom(traded, 1)
    near = swap_mom(near, 2)
    h, done_2 = call(
        own_kernel_2,
        "own_products_2",
        [smem(), hbm()] + [vmem()] * 2,
        [vmem()] * 2,
        [products, token],
        [piece, u_scratch, turns, dma(1)],
        20,
        {3: 0},
    )(gamma_index, own, y, h)

    if src_count > 2:
        rest_near = jnp.where(plan.peer_hops() // (src_count // 2) != 0, rest_far, rest_near)
        rest_far = rest_near
    rest = call(
        part(choose, sizes),
        "choose",
        [smem()] + [hbm()] * 2 + [vmem()],
        vmem(),
        rest_shape,
        [dma(1)],
        20,
    )(separations, rest_near, rest_far, done_0)
    first, rest, opened = alias(
        gate,
        "gate",
        [anywhere()] * 2 + [vmem()],
        [first_shape, rest_shape, token],
        {0: 0, 1: 1},
        (first, rest, done_2),
    )
    rest = swap_snk(rest)
    first_near, first_far = most_of(first, plan.hops(0))
    h, label = call(
        part(own_kernel_13, sizes),
        "own_products_13",
        [smem()] * 3 + [hbm()] * 2 + [vmem()] * 3,
        [vmem(), smem()],
        [products, jax.ShapeDtypeStruct((2 * mom_count,), jnp.int32)],
        [pieces, u_scratch, u_scratch, turns, turns]
        + [pltpu.VMEM((3, TAG_ROWS, nev), jnp.bfloat16), dma(5)],
        20,
        {6: 0},
    )(separations, gamma_index, partner, own, traded, y, h, opened)

    near, far_same, far_cross, h = pl.pallas_call(
        gate_far,
        in_specs=[anywhere()] * 3 + [vmem()],
        out_specs=[anywhere()] * 3 + [vmem()],
        out_shape=[two, two, two, products],
        input_output_aliases={n: n for n in range(4)},
        compiler_params=limit(20),
        cost_estimate=pl.CostEstimate(
            flops=WEIGHT, bytes_accessed=WEIGHT // 1000, transcendentals=0
        ),
        name="gate_far",
    )(near, far_same, far_cross, h)
    near_core = swap_mom(near, 1)
    if src_count == 2:
        far = [far_same, far_cross, swap_mom(far_same, 1), swap_mom(far_cross, 1)]
    else:

        def moved(array):
            if src_count == 1:
                return array
            array, away = most_of(array, plan.hops(0))
            return jnp.where(plan.hops(0) // (src_count // 2) != 0, away, array)

        here = lax.dynamic_index_in_dim(proj, plan.local(0), 0, keepdims=False)
        here = (here, near[:rows], traded[2 * rows : 3 * rows], near_core[rows:])
        far = [moved(array) for array in here]

    k_shape = jax.ShapeDtypeStruct((2, 2 * width, width), jnp.float32)
    scratch = [pieces, u_scratch, u_scratch, turns, turns, dma(2)]
    ka = call(
        part(other_kernel_02, sizes),
        "other_products_02",
        [smem()] * 3 + [vmem()] + [hbm()] * 4,
        vmem(),
        k_shape,
        scratch,
        20,
    )(separations, gamma_index, label, h, proj, near, far[0], far[1])
    kb = call(
        part(other_kernel_13, sizes),
        "other_products_13",
        [smem()] * 3 + [vmem()] + [hbm()] * 4,
        vmem(),
        k_shape,
        scratch,
        20,
    )(separations, gamma_index, label, h, traded, near_core, far[2], far[3])

    device_count = src_count * snk_count * mom_count
    values = time_count * sep_count * 2
    lines = (values + 127) // 128
    out = call(
        part(trace_kernel, sizes, sep_count),
        "traces",
        [smem()] * 2 + [vmem()] * 2 + [hbm()] * 3,
        vmem(),
        jax.ShapeDtypeStruct((device_count, lines, 128), jnp.float32),
        buffers([first_shape, rest_shape]) + [dma(2)],
        20,
    )(separations, label, ka, kb, first_near, first_far, rest)
    out = lax.all_to_all(out, ("src", "snk", "mom"), split_axis=0, concat_axis=0, tiled=True)
    out = jnp.sum(out, axis=0).reshape(lines * 128)[:values]
    return out.reshape(time_count, sep_count, 1, 2)


def solution(mesh):
    placed = (
        P("src", "snk", None, None, None),
        P("src", "mom", None, None, None, None),
        P(),
        P("mom"),
        P(),
    )
    return jax.shard_map(
        shards, mesh=mesh, in_specs=placed, out_specs=P(None, None, "mom", None), check_vma=False
    )
```

```python
import functools

import jax
import jax.numpy as jnp
from jax import lax
from jax.experimental import pallas as pl
from jax.experimental.pallas import tpu as pltpu
from jax.sharding import PartitionSpec as P

NSPIN = 4
NT_DIMS = (((1,), (1,)), ((), ()))
MIB = 1024 * 1024
WEIGHT = 10**13
TAG_ROWS = 16
TILE = 256
GAMMAS = (
    (3, 1 | 1 << 2 | 3 << 4 | 3 << 6),
    (3, 2 | 0 << 2 | 0 << 4 | 2 << 6),
    (2, 1 | 3 << 2 | 3 << 4 | 1 << 6),
    (2, 0),
)


def spin_entry(code, row):
    phase = row * 0
    for bit, (flip, phases) in enumerate(GAMMAS):
        on = (code >> bit) & 1
        phase = phase + on * ((phases >> (2 * row)) & 3)
        row = row ^ (on * flip)
    return row, phase & 3


def fill_spin_blocks(codes, turns, write):
    for r, code in enumerate(codes):
        for spin in range(NSPIN):
            column, phase = spin_entry(code, spin)
            write(spin, column, *(turns[r, (n - phase) & 3] for n in (4, 1)))


def set_turns(turns, r, real, imag):
    for n, value in enumerate((real, imag, -real, -imag)):
        turns[r, n] = value


def add_to(ref, rows, lanes, value):
    ref[rows, lanes] = ref[rows, lanes] + value


def along(spin, nev, start=0):
    if isinstance(spin, int):
        return slice(start + spin * nev, start + (spin + 1) * nev)
    return pl.ds(pl.multiple_of(start + spin * nev, nev), nev)


class Plan:
    def __init__(self, seps, sizes):
        slices, offsets, src_count, snk_count = sizes
        src, snk, self.mom = (lax.axis_index(name) for name in ("src", "snk", "mom"))
        half_snk = snk_count // 2
        self.slices, self.time_count = slices, slices * src_count
        self.forward = snk < half_snk
        base = lax.rem(snk, half_snk) * offsets
        self.keep = jnp.where(self.forward, 0, offsets - 1)
        self.give = offsets - 1 - self.keep
        self.sep_index = base + self.keep
        sign = jnp.where(self.forward, 1, -1)
        self.shift = sign * seps[base + self.keep]
        self.peer_shift = -sign * seps[base + self.give]
        self.own_time = src * slices + self.mom
        late = jnp.where(self.forward, 0, self.shift)
        self.pair_time = lax.rem(self.own_time + late + self.time_count, self.time_count)
        self.live = self.forward if offsets == 1 else None

    def _sum(self, place, amount):
        return lax.rem(place + amount + self.time_count, self.time_count)

    def local(self, i):
        return lax.rem(self._sum(self.mom ^ i, self.shift), self.slices)

    def hops(self, i):
        return lax.div(self._sum(self.mom ^ i, self.shift), self.slices)

    def peer_local(self):
        return lax.rem(self._sum(self.mom, self.peer_shift), self.slices)

    def peer_hops(self):
        return lax.div(self._sum(self.mom, self.peer_shift), self.slices)


def run_copies(copies, sems):
    handles = [
        pltpu.make_async_copy(source, target, sems.at[n])
        for n, (source, target) in enumerate(copies)
    ]
    for handle in handles:
        handle.start()
    for handle in handles:
        handle.wait()


def span(index, rows):
    return pl.ds(index * rows, rows)


def through(parts, ins, leaving):
    started, n = [], 0
    for copies, buffer, target in parts:
        group = []
        for source, spot in copies:
            group.append(pltpu.make_async_copy(source, spot, ins.at[n]))
            group[-1].start()
            n += 1
        started.append(group)
    handles = []
    for n, (group, (_, buffer, target)) in enumerate(zip(started, parts)):
        for handle in group:
            handle.wait()
        handles.append(pltpu.make_async_copy(buffer, target, leaving.at[n]))
        handles[-1].start()
    for handle in handles:
        handle.wait()


def two_slices(proj, buffer, first, second):
    rows = proj.shape[1]
    return [(proj.at[n], buffer.at[span(i, rows)]) for i, n in enumerate((first, second))]


def tag_of(partner, lanes):
    number = jnp.full((TAG_ROWS, lanes), partner[0].astype(jnp.float32))
    return number.astype(jnp.bfloat16)


def pack_first(sizes, seps, partner, peram, *refs):
    outs, token, buffers, (ins, leaving) = refs[:2], refs[2], refs[3:5], refs[5:]
    plan = Plan(seps, sizes)
    start, copies = 0, []
    for buffer in buffers:
        rows = buffer.shape[1]
        source = peram.at[plan.peer_local(), plan.give, :, pl.ds(start, rows)]
        copies.append([(source, buffer)])
        start += rows
    token[...] = tag_of(partner, token.shape[-1])
    through(list(zip(copies, buffers, outs)), ins, leaving)


def pack(sizes, seps, partner, proj, tick, after, *refs):
    outs, buffers, (ins, leaving) = refs[:2], refs[2:4], refs[4:]
    plan = Plan(seps, sizes)
    rows = proj.shape[1]
    same, cross = buffers
    cross[pl.ds(2 * rows, TAG_ROWS), :] = tag_of(partner, cross.shape[-1])
    cross[pl.ds(2 * rows + TAG_ROWS, TAG_ROWS), :] = tick[...]
    copies = [
        two_slices(proj, same, plan.local(0), plan.local(1)),
        two_slices(proj, cross, plan.local(2), plan.local(3)),
    ]
    through(list(zip(copies, buffers, outs)), ins, leaving)


def choose(sizes, seps, near, far, after, out, sems):
    flag = lax.rem(Plan(seps, sizes).peer_hops(), 2)

    @pl.when(flag == 0)
    def _():
        run_copies([(near, out)], sems)

    @pl.when(flag != 0)
    def _():
        run_copies([(far, out)], sems)


def gate(first, rest, after, first_out, rest_out, token):
    token[...] = jnp.zeros(token.shape, token.dtype)


def gate_one(after, array, array_out, token):
    token[...] = after[...]


def gate_far(after, same, cross, same_out, cross_out, token):
    token[...] = after[...]


def own_fill(codes, p_ref, n, u_ref, turns):
    nev = turns.shape[-1]
    width = u_ref.shape[0]
    for r in range(len(codes)):
        real, imag = (p_ref[n, m * nev : (m + 1) * nev].T for m in (2 * r, 2 * r + 1))
        set_turns(turns, r, real, imag)
    u_ref[...] = jnp.zeros(u_ref.shape, u_ref.dtype)

    def write(spin, column, a, b):
        add_to(u_ref, along(column, nev), along(spin, nev), a)
        add_to(u_ref, along(column, nev), along(spin, nev, width), b)

    fill_spin_blocks(codes, turns, write)


def own_dot(u_ref, y_ref, ht):
    width = u_ref.shape[0]
    for tile in range(2 * width // TILE):
        start = tile * TILE
        out = lax.dot_general(
            u_ref[...], y_ref[start : start + TILE, :], NT_DIMS, preferred_element_type=jnp.float32
        ).astype(jnp.bfloat16)
        if start < width:
            ht[:, width + start : width + start + TILE] = out
        else:
            ht[:, start - width : start - width + TILE] = out
            ht[:, width + start : width + start + TILE] = -out


def codes_of(gamma, op, nterm):
    return [gamma[op, r] for r in range(nterm)]


def own_kernel_0(sizes, seps, gamma, peram, proj, y_ref, ht, token, x_ref, p_ref, u_ref, turns, sems):
    plan = Plan(seps, sizes)
    mom = plan.mom
    run_copies([(peram.at[mom, plan.keep], x_ref), (proj.at[mom], p_ref.at[0])], sems)
    width = x_ref.shape[-1]
    real, imag = x_ref[0], x_ref[1]
    y_ref[:width, :width] = real
    y_ref[:width, width:] = -imag
    y_ref[width:, :width] = imag
    y_ref[width:, width:] = real
    own_fill(codes_of(gamma, mom, turns.shape[0]), p_ref, 0, u_ref, turns)
    own_dot(u_ref, y_ref, ht)
    token[...] = jnp.zeros(token.shape, token.dtype)


def own_kernel(piece, gamma, source, y_ref, after, ht, token, p_ref, u_ref, turns, sems):
    mom = lax.axis_index("mom")
    run_copies([(source.at[mom], p_ref.at[0])], sems)
    own_fill(codes_of(gamma, mom ^ piece, turns.shape[0]), p_ref, 0, u_ref, turns)
    own_dot(u_ref, y_ref, ht)
    token[...] = jnp.zeros(token.shape, token.dtype)


def find_labels(plan, partner, tick, tags, label):
    mom = plan.mom

    def number(tag):
        return jnp.max(tag.astype(jnp.float32)).astype(jnp.int32)

    partners = [partner[0], number(tick[...]), number(tags[:TAG_ROWS]), number(tags[TAG_ROWS:])]
    count = len(partners)
    for p in range(count):
        back = jnp.int32(0)
        for i, value in enumerate(partners):
            back = back + jnp.where(value == (mom ^ p), mom ^ i, 0)
        label[p] = jnp.where(plan.forward, back, mom ^ p)
        label[count + p] = jnp.where(plan.forward, back, partners[p]) ^ mom


def other_products(pieces, gamma, label, products, sources, refs, before=None):
    k_ref, p_ref, hs, wa, wb, turns_a, turns_b, sems = refs
    mom = lax.axis_index("mom")
    nterm, nev = turns_a.shape[0], turns_a.shape[-1]
    width = wa.shape[0]
    (here, away), flag = sources
    for n in range(2):
        for wanted, refs_now in ((0, here), (1, away)):

            @pl.when(flag == wanted)
            def _():
                pltpu.make_async_copy(refs_now[n], p_ref.at[n], sems.at[n]).start()

    if before is not None:
        before()
    for n, piece in enumerate(pieces):
        for own, source in enumerate(products):

            @pl.when(label[4 + piece] == own)
            def _():
                pltpu.make_async_copy(source, hs.at[n], sems.at[2 + n]).start()

    for n, piece in enumerate(pieces):
        w_ref, turns = ((wa, turns_a), (wb, turns_b))[n % 2]
        pltpu.make_async_copy(away[n], p_ref.at[n], sems.at[n]).wait()
        for r in range(nterm):
            real, imag = (p_ref[n, m * nev : (m + 1) * nev] for m in (2 * r, 2 * r + 1))
            set_turns(turns, r, real, imag)
        w_ref[...] = jnp.zeros(w_ref.shape, w_ref.dtype)

        def write(spin, column, a, b, w_ref=w_ref):
            add_to(w_ref, along(spin, nev), along(column, nev), a)
            add_to(w_ref, along(spin, nev), along(column, nev, width), b)

        fill_spin_blocks(codes_of(gamma, mom ^ piece, nterm), turns, write)
        pltpu.make_async_copy(products[0], hs.at[n], sems.at[2 + n]).wait()
        for tile in range(width // TILE):
            lanes = slice(tile * TILE, (tile + 1) * TILE)
            weights = w_ref[lanes, :]
            k_ref[n, :width, lanes] = lax.dot_general(
                hs[n, :, width:], weights, NT_DIMS, preferred_element_type=jnp.float32
            )
            k_ref[n, width:, lanes] = lax.dot_general(
                hs[n, :, : 2 * width], weights, NT_DIMS, preferred_element_type=jnp.float32
            )


def other_flag(plan, sizes):
    return lax.rem(plan.hops(0), 2) if sizes[2] == 2 else jnp.int32(1)


def other_kernel_02(sizes, seps, gamma, partner, tick, h0, h1, h2, h3, proj, near, same, cross, *refs):
    k_ref, label, tags, sems, refs = refs[0], refs[1], refs[2], refs[3], (refs[0],) + refs[4:]
    plan = Plan(seps, sizes)
    rows = proj.shape[1]
    low, at = span(0, rows), plan.local(0)
    sources = (((proj.at[at], near.at[at]), (same.at[low], cross.at[low])), other_flag(plan, sizes))

    def before():
        run_copies([(cross.at[pl.ds(2 * rows, 2 * TAG_ROWS)], tags)], sems)
        find_labels(plan, partner, tick, tags, label)

    other_products((0, 2), gamma, label, (h0, h1, h2, h3), sources, refs, before)


def other_kernel_13(sizes, seps, gamma, label, h0, h1, h2, h3, core, near, same, cross, *refs):
    plan = Plan(seps, sizes)
    rows = core.shape[1]
    away, at = span(1 if sizes[2] == 2 else 0, rows), plan.local(0)
    sources = (((core.at[at], near.at[at]), (same.at[away], cross.at[away])), other_flag(plan, sizes))
    other_products((1, 3), gamma, label, (h0, h1, h2, h3), sources, refs)


def row_sums(k_refs, source, offset, totals):
    rows = 16
    width = source.shape[-1]
    nev = totals[0].shape[-1]

    def step(index, totals):
        row = pl.multiple_of(index * rows, rows)
        here = pl.ds(pl.multiple_of(offset + row, rows), rows)
        later = pl.ds(pl.multiple_of(width + offset + row, rows), rows)
        totals = list(totals)
        for spin in range(NSPIN):
            lanes = along(spin, nev)
            real = source[0, pl.ds(row, rows), lanes].astype(jnp.float32)
            imag = source[1, pl.ds(row, rows), lanes].astype(jnp.float32)
            for n in range(len(totals) // 2):
                k_ref, p = k_refs[n // 2], n % 2
                kr, ki = k_ref[p, here, lanes], k_ref[p, later, lanes]
                totals[2 * n] += real * kr - imag * ki
                totals[2 * n + 1] += real * ki + imag * kr
        return tuple(totals)

    return lax.fori_loop(0, source.shape[1] // rows, step, totals)


def trace_kernel(sizes, sep_count, seps, label, ka, kb, near, far, rest, out_ref, first_buf, rest_buf, sems):
    plan = Plan(seps, sizes)
    count = 2 * ka.shape[0]
    width = rest_buf.shape[-1]
    nev = width // NSPIN
    flag = lax.rem(lax.div(plan.hops(0), max(sizes[2] // 2, 1)), 2)
    later = pltpu.make_async_copy(rest, rest_buf, sems.at[1])
    later.start()

    @pl.when(flag == 0)
    def _():
        run_copies([(near, first_buf)], sems)

    @pl.when(flag != 0)
    def _():
        run_copies([(far, first_buf)], sems)

    totals = tuple(jnp.zeros((16, nev), jnp.float32) for _ in range(2 * count))
    totals = row_sums((ka, kb), first_buf, 0, totals)
    later.wait()
    totals = row_sums((ka, kb), rest_buf, first_buf.shape[1], totals)
    sums = [jnp.sum(total, axis=0, keepdims=True) for total in totals]
    sums = [jnp.sum(total, axis=1, keepdims=True) * (1.0 / width) for total in sums]
    shape = out_ref.shape[1:]
    spot = lax.broadcasted_iota(jnp.int32, shape, 0) * shape[1]
    spot = spot + lax.broadcasted_iota(jnp.int32, shape, 1)
    here = spot // 2 == plan.pair_time * sep_count + plan.sep_index
    if plan.live is not None:
        here = here & plan.live
    values = [jnp.where(spot % 2 == 0, sums[2 * p], sums[2 * p + 1]) for p in range(count)]
    lines = []
    for op in range(count):
        line = jnp.zeros(shape, jnp.float32)
        for p, value in zip((0, 2, 1, 3), values):
            line = jnp.where(label[p] == op, value, line)
        lines.append(jnp.where(here, line, 0.0))
    for n in range(out_ref.shape[0]):
        out_ref[n] = lines[n % count]


def smem():
    return pl.BlockSpec(memory_space=pltpu.SMEM)


def vmem():
    return pl.BlockSpec(memory_space=pltpu.VMEM)


def anywhere():
    return pl.BlockSpec(memory_space=pl.ANY)


def hbm():
    return pl.BlockSpec(memory_space=pltpu.HBM)


def limit(mib):
    return pltpu.CompilerParams(vmem_limit_bytes=mib * MIB)


def shards(peram_blocks, projections, gamma_index, partner, separations):
    src_count, snk_count = lax.axis_size("src"), lax.axis_size("snk")
    mom_count = lax.axis_size("mom")
    slices, offsets = peram_blocks.shape[:2]
    width = peram_blocks.shape[-1]
    nterm, nev = projections.shape[2], projections.shape[-1]
    time_count = slices * src_count
    sep_count = separations.shape[0]
    half_snk = snk_count // 2
    rows = nterm * 2 * nev
    sizes = (slices, offsets, src_count, snk_count)
    proj = projections.reshape(slices, rows, nev)

    def swap_mom(array, i):
        return lax.ppermute(array, "mom", [(a, a ^ i) for a in range(mom_count)])

    def swap_snk(array):
        pairs = [(a, (a + half_snk) % snk_count) for a in range(snk_count)]
        return lax.ppermute(array, "snk", pairs)

    def next_src(array, step=1, i=0):
        pairs = [
            (((a + step) % src_count) * mom_count + (b ^ i), a * mom_count + b)
            for a in range(src_count)
            for b in range(mom_count)
        ]
        return lax.ppermute(array, ("src", "mom"), pairs)

    def most_of(array, amount):
        step = 1
        while 2 * step < src_count:
            array = jnp.where((amount // step) % 2 != 0, next_src(array, step), array)
            step *= 2
        return array, next_src(array, step)

    def call(kernel, name, in_specs, out_specs, out_shape, scratch, mib, aliases=None):
        cost = pl.CostEstimate(flops=WEIGHT, bytes_accessed=WEIGHT // 1000, transcendentals=0)
        return pl.pallas_call(
            kernel,
            in_specs=in_specs,
            out_specs=out_specs,
            out_shape=out_shape,
            scratch_shapes=scratch,
            input_output_aliases=aliases or {},
            compiler_params=limit(mib),
            cost_estimate=cost,
            name=name,
        )

    def bf16(*shape):
        return jax.ShapeDtypeStruct(shape, jnp.bfloat16)

    def dma(count):
        return pltpu.SemaphoreType.DMA((count,))

    part = functools.partial
    split = (width * 5 // 8) // 16 * 16
    two = bf16(2 * rows, nev)
    tagged = bf16(2 * rows + TAG_ROWS, nev)
    first_shape, rest_shape = bf16(2, split, width), bf16(2, width - split, width)
    token = bf16(16, 128)

    def buffers(shapes):
        return [pltpu.VMEM(shape.shape, shape.dtype) for shape in shapes]

    def alias(kernel, name, in_specs, out_shape, aliases, operands):
        return pl.pallas_call(
            kernel,
            in_specs=in_specs,
            out_specs=[anywhere()] * len(aliases) + [vmem()],
            out_shape=out_shape,
            input_output_aliases=aliases,
            compiler_params=limit(20),
            cost_estimate=pl.CostEstimate(
                flops=WEIGHT, bytes_accessed=WEIGHT // 1000, transcendentals=0
            ),
            name=name,
        )(*operands)

    leaving = [first_shape, rest_shape]
    first, rest, tick = call(
        part(pack_first, sizes),
        "pack_first",
        [smem()] * 2 + [hbm()],
        [hbm()] * 2 + [vmem()],
        leaving + [token],
        buffers(leaving) + [dma(2), dma(2)],
        58,
    )(separations, partner, peram_blocks)

    plan = Plan(separations, sizes)
    near = swap_mom(proj, 2)
    core = swap_mom(proj, 1)
    first = swap_snk(first)
    rest_near, rest_far = most_of(rest, plan.peer_hops())
    tick = swap_mom(tick, 1)
    u_scratch = pltpu.VMEM((width, 2 * width), jnp.bfloat16)
    turns = pltpu.VMEM((nterm, 4, nev, nev), jnp.bfloat16)
    piece = pltpu.VMEM((1, rows, nev), jnp.bfloat16)
    pieces = pltpu.VMEM((2, rows, nev), jnp.bfloat16)
    product = bf16(width, 3 * width)
    y, h0, done_0 = call(
        part(own_kernel_0, sizes),
        "own_products_0",
        [smem()] * 2 + [hbm()] * 2,
        [vmem()] * 3,
        [bf16(2 * width, 2 * width), product, token],
        [pltpu.VMEM((2, width, width), jnp.bfloat16), piece, u_scratch, turns, dma(2)],
        58,
    )(separations, gamma_index, peram_blocks, proj)
    leaving = [two, bf16(2 * (rows + TAG_ROWS), nev)]
    far_same, far_cross = call(
        part(pack, sizes),
        "pack",
        [smem()] * 2 + [hbm(), vmem(), vmem()],
        [hbm()] * 2,
        leaving,
        buffers(leaving) + [dma(4), dma(2)],
        58,
    )(separations, partner, proj, tick, done_0)
    if src_count == 2:
        far_same, far_cross = next_src(far_same), next_src(far_cross, 1, 2)
    else:
        far_cross = swap_mom(far_cross, 2)
    def own_one(number, source, after):
        return call(
            part(own_kernel, number),
            "own_products_%d" % number,
            [smem(), hbm(), vmem(), vmem()],
            [vmem()] * 2,
            [product, token],
            [piece, u_scratch, turns, dma(1)],
            20,
        )(gamma_index, source, y, after)

    h1, done_1 = own_one(1, core, done_0)
    near, _ = alias(
        gate_one,
        "gate_near",
        [vmem(), anywhere()],
        [bf16(*proj.shape), token],
        {1: 0},
        (done_1, near),
    )
    near_core = swap_mom(near, 1)

    if src_count > 2:
        rest_near = jnp.where(plan.peer_hops() // (src_count // 2) != 0, rest_far, rest_near)
        rest_far = rest_near
    rest = call(
        part(choose, sizes),
        "choose",
        [smem()] + [hbm()] * 2 + [vmem()],
        vmem(),
        rest_shape,
        [dma(1)],
        20,
    )(separations, rest_near, rest_far, done_1)
    h2, done_2 = own_one(2, near, done_1)
    first, rest, opened = alias(
        gate,
        "gate",
        [anywhere()] * 2 + [vmem()],
        [first_shape, rest_shape, token],
        {0: 0, 1: 1},
        (first, rest, done_2),
    )
    rest = swap_snk(rest)
    first_near, first_far = most_of(first, plan.hops(0))
    h3, done_3 = own_one(3, near_core, opened)
    far_same, far_cross, _ = alias(
        gate_far,
        "gate_far",
        [vmem()] + [anywhere()] * 2,
        [two, bf16(2 * (rows + TAG_ROWS), nev), token],
        {1: 0, 2: 1},
        (done_3, far_same, far_cross),
    )
    if src_count == 2:
        far = [far_same, far_cross, swap_mom(far_same, 1), swap_mom(far_cross, 1)]
    else:

        def moved(array):
            array = lax.dynamic_index_in_dim(array, plan.local(0), 0, keepdims=False)
            if src_count == 1:
                return array
            array, away = most_of(array, plan.hops(0))
            return jnp.where(plan.hops(0) // (src_count // 2) != 0, away, array)

        far = [moved(array) for array in (proj, near, core, near_core)]
        far[1] = jnp.concatenate([far[1], far[1], far_cross[2 * rows :]])

    k_shape = jax.ShapeDtypeStruct((2, 2 * width, width), jnp.float32)
    scratch = [pieces, pltpu.VMEM((2, width, 3 * width), jnp.bfloat16)]
    scratch += [u_scratch, u_scratch, turns, turns, dma(4)]
    ka, label = call(
        part(other_kernel_02, sizes),
        "other_products_02",
        [smem()] * 3 + [vmem()] + [hbm()] * 8,
        [vmem(), smem()],
        [k_shape, jax.ShapeDtypeStruct((2 * mom_count,), jnp.int32)],
        [pltpu.VMEM((2 * TAG_ROWS, nev), jnp.bfloat16), dma(1)] + scratch,
        20,
    )(
        separations, gamma_index, partner, tick, h0, h1, h2, h3, proj, near, far[0], far[1],
    )
    kb = call(
        part(other_kernel_13, sizes),
        "other_products_13",
        [smem()] * 3 + [hbm()] * 8,
        vmem(),
        k_shape,
        scratch,
        20,
    )(separations, gamma_index, label, h0, h1, h2, h3, core, near_core, far[2], far[3])

    device_count = src_count * snk_count * mom_count
    values = time_count * sep_count * 2
    lines = (values + 127) // 128
    out = call(
        part(trace_kernel, sizes, sep_count),
        "traces",
        [smem()] * 2 + [vmem()] * 2 + [hbm()] * 3,
        vmem(),
        jax.ShapeDtypeStruct((device_count, lines, 128), jnp.float32),
        buffers([first_shape, rest_shape]) + [dma(2)],
        20,
    )(separations, label, ka, kb, first_near, first_far, rest)
    out = lax.all_to_all(out, ("src", "snk", "mom"), split_axis=0, concat_axis=0, tiled=True)
    out = jnp.sum(out, axis=0).reshape(lines * 128)[:values]
    return out.reshape(time_count, sep_count, 1, 2)


def solution(mesh):
    placed = (
        P("src", "snk", None, None, None),
        P("src", "mom", None, None, None, None),
        P(),
        P("mom"),
        P(),
    )
    return jax.shard_map(
        shards, mesh=mesh, in_specs=placed, out_specs=P(None, None, "mom", None), check_vma=False
    )
```

```python
import functools

import jax
import jax.numpy as jnp
from jax import lax
from jax.experimental import pallas as pl
from jax.experimental.pallas import tpu as pltpu
from jax.sharding import PartitionSpec as P

NSPIN = 4
NT_DIMS = (((1,), (1,)), ((), ()))
MIB = 1024 * 1024
WEIGHT = 10**13
TAG_ROWS = 16
TILE = 256
SPLIT = 9
GAMMAS = (
    (3, 1 | 1 << 2 | 3 << 4 | 3 << 6),
    (3, 2 | 0 << 2 | 0 << 4 | 2 << 6),
    (2, 1 | 3 << 2 | 3 << 4 | 1 << 6),
    (2, 0),
)


def spin_entry(code, row):
    phase = row * 0
    for bit, (flip, phases) in enumerate(GAMMAS):
        on = (code >> bit) & 1
        phase = phase + on * ((phases >> (2 * row)) & 3)
        row = row ^ (on * flip)
    return row, phase & 3


def fill_spin_blocks(codes, turns, write):
    for r, code in enumerate(codes):
        for spin in range(NSPIN):
            column, phase = spin_entry(code, spin)
            write(spin, column, *(turns[r, (n - phase) & 3] for n in (4, 1)))


def set_turns(turns, r, real, imag):
    for n, value in enumerate((real, imag, -real, -imag)):
        turns[r, n] = value


def add_to(ref, rows, lanes, value):
    ref[rows, lanes] = ref[rows, lanes] + value


def along(spin, nev, start=0):
    if isinstance(spin, int):
        return slice(start + spin * nev, start + (spin + 1) * nev)
    return pl.ds(pl.multiple_of(start + spin * nev, nev), nev)


class Plan:
    def __init__(self, seps, sizes):
        slices, offsets, src_count, snk_count = sizes
        src, snk, self.mom = (lax.axis_index(name) for name in ("src", "snk", "mom"))
        half_snk = snk_count // 2
        self.slices, self.time_count = slices, slices * src_count
        self.forward = snk < half_snk
        base = lax.rem(snk, half_snk) * offsets
        self.keep = jnp.where(self.forward, 0, offsets - 1)
        self.give = offsets - 1 - self.keep
        self.sep_index = base + self.keep
        sign = jnp.where(self.forward, 1, -1)
        self.shift = sign * seps[base + self.keep]
        self.peer_shift = -sign * seps[base + self.give]
        self.own_time = src * slices + self.mom
        late = jnp.where(self.forward, 0, self.shift)
        self.pair_time = lax.rem(self.own_time + late + self.time_count, self.time_count)
        self.live = self.forward if offsets == 1 else None

    def _sum(self, place, amount):
        return lax.rem(place + amount + self.time_count, self.time_count)

    def local(self, i):
        return lax.rem(self._sum(self.mom ^ i, self.shift), self.slices)

    def hops(self, i):
        return lax.div(self._sum(self.mom ^ i, self.shift), self.slices)

    def peer_local(self):
        return lax.rem(self._sum(self.mom, self.peer_shift), self.slices)

    def peer_hops(self):
        return lax.div(self._sum(self.mom, self.peer_shift), self.slices)


def run_copies(copies, sems):
    handles = [
        pltpu.make_async_copy(source, target, sems.at[n])
        for n, (source, target) in enumerate(copies)
    ]
    for handle in handles:
        handle.start()
    for handle in handles:
        handle.wait()


def span(index, rows):
    return pl.ds(index * rows, rows)


def through(parts, ins, leaving):
    started, n = [], 0
    for copies, buffer, target in parts:
        group = []
        for source, spot in copies:
            group.append(pltpu.make_async_copy(source, spot, ins.at[n]))
            group[-1].start()
            n += 1
        started.append(group)
    handles = []
    for n, (group, (_, buffer, target)) in enumerate(zip(started, parts)):
        for handle in group:
            handle.wait()
        handles.append(pltpu.make_async_copy(buffer, target, leaving.at[n]))
        handles[-1].start()
    for handle in handles:
        handle.wait()


def two_slices(proj, buffer, first, second):
    rows = proj.shape[1]
    return [(proj.at[n], buffer.at[span(i, rows)]) for i, n in enumerate((first, second))]


def tag_of(partner, lanes):
    number = jnp.full((TAG_ROWS, lanes), partner[0].astype(jnp.float32))
    return number.astype(jnp.bfloat16)


def pack_first(sizes, seps, partner, peram, *refs):
    outs, token, buffers, (ins, leaving) = refs[:2], refs[2], refs[3:5], refs[5:]
    plan = Plan(seps, sizes)
    start, copies = 0, []
    for buffer in buffers:
        rows = buffer.shape[1]
        source = peram.at[plan.peer_local(), plan.give, :, pl.ds(start, rows)]
        copies.append([(source, buffer)])
        start += rows
    token[...] = tag_of(partner, token.shape[-1])
    through(list(zip(copies, buffers, outs)), ins, leaving)


def pack(sizes, seps, partner, proj, tick, after, *refs):
    outs, buffers, (ins, leaving) = refs[:2], refs[2:4], refs[4:]
    plan = Plan(seps, sizes)
    rows = proj.shape[1]
    same, cross = buffers
    cross[pl.ds(2 * rows, TAG_ROWS), :] = tag_of(partner, cross.shape[-1])
    cross[pl.ds(2 * rows + TAG_ROWS, TAG_ROWS), :] = tick[...]
    copies = [
        two_slices(proj, same, plan.local(0), plan.local(1)),
        two_slices(proj, cross, plan.local(2), plan.local(3)),
    ]
    through(list(zip(copies, buffers, outs)), ins, leaving)


def choose(sizes, seps, near, far, after, out, token, sems):
    flag = lax.rem(Plan(seps, sizes).peer_hops(), 2)

    @pl.when(flag == 0)
    def _():
        run_copies([(near, out)], sems)

    @pl.when(flag != 0)
    def _():
        run_copies([(far, out)], sems)

    token[...] = after[...]


def gate_one(after, array, array_out, token):
    token[...] = after[...]


def gate_far(after, same, cross, same_out, cross_out, token):
    token[...] = after[...]


def own_fill(codes, p_ref, n, u_ref, turns):
    nev = turns.shape[-1]
    width = u_ref.shape[0]
    for r in range(len(codes)):
        real, imag = (p_ref[n, m * nev : (m + 1) * nev].T for m in (2 * r, 2 * r + 1))
        set_turns(turns, r, real, imag)
    u_ref[...] = jnp.zeros(u_ref.shape, u_ref.dtype)

    def write(spin, column, a, b):
        add_to(u_ref, along(column, nev), along(spin, nev), a)
        add_to(u_ref, along(column, nev), along(spin, nev, width), b)

    fill_spin_blocks(codes, turns, write)


def own_dot(u_ref, y_ref, ht):
    width = u_ref.shape[0]
    for tile in range(2 * width // TILE):
        start = tile * TILE
        out = lax.dot_general(
            u_ref[...], y_ref[start : start + TILE, :], NT_DIMS, preferred_element_type=jnp.float32
        ).astype(jnp.bfloat16)
        if start < width:
            ht[:, width + start : width + start + TILE] = out
        else:
            ht[:, start - width : start - width + TILE] = out
            ht[:, width + start : width + start + TILE] = -out


def codes_of(gamma, op, nterm):
    return [gamma[op, r] for r in range(nterm)]


def own_kernel_0(sizes, seps, gamma, peram, proj, y_ref, ht, token, x_ref, p_ref, u_ref, turns, sems):
    plan = Plan(seps, sizes)
    mom = plan.mom
    run_copies([(peram.at[mom, plan.keep], x_ref), (proj.at[mom], p_ref.at[0])], sems)
    width = x_ref.shape[-1]
    real, imag = x_ref[0], x_ref[1]
    y_ref[:width, :width] = real
    y_ref[:width, width:] = -imag
    y_ref[width:, :width] = imag
    y_ref[width:, width:] = real
    own_fill(codes_of(gamma, mom, turns.shape[0]), p_ref, 0, u_ref, turns)
    own_dot(u_ref, y_ref, ht)
    token[...] = jnp.zeros(token.shape, token.dtype)


def own_kernel(piece, gamma, source, y_ref, after, ht, token, p_ref, u_ref, turns, sems):
    mom = lax.axis_index("mom")
    run_copies([(source.at[mom], p_ref.at[0])], sems)
    own_fill(codes_of(gamma, mom ^ piece, turns.shape[0]), p_ref, 0, u_ref, turns)
    own_dot(u_ref, y_ref, ht)
    token[...] = jnp.zeros(token.shape, token.dtype)


def find_labels(plan, partner, tick, tags, label):
    mom = plan.mom

    def number(tag):
        return jnp.max(tag.astype(jnp.float32)).astype(jnp.int32)

    partners = [partner[0], number(tick[...]), number(tags[:TAG_ROWS]), number(tags[TAG_ROWS:])]
    count = len(partners)
    for p in range(count):
        back = jnp.int32(0)
        for i, value in enumerate(partners):
            back = back + jnp.where(value == (mom ^ p), mom ^ i, 0)
        label[p] = jnp.where(plan.forward, back, mom ^ p)
        label[count + p] = jnp.where(plan.forward, back, partners[p]) ^ mom


def other_products(pieces, gamma, label, products, sources, refs, before=None):
    k_ref, p_ref, hs, wa, wb, turns_a, turns_b, sems = refs
    mom = lax.axis_index("mom")
    nterm, nev = turns_a.shape[0], turns_a.shape[-1]
    width = wa.shape[0]
    (here, away), flag = sources
    for n in range(2):
        for wanted, refs_now in ((0, here), (1, away)):

            @pl.when(flag == wanted)
            def _():
                pltpu.make_async_copy(refs_now[n], p_ref.at[n], sems.at[n]).start()

    if before is not None:
        before()
    for n, piece in enumerate(pieces):
        for own, source in enumerate(products):

            @pl.when(label[4 + piece] == own)
            def _():
                pltpu.make_async_copy(source, hs.at[n], sems.at[2 + n]).start()

    for n, piece in enumerate(pieces):
        w_ref, turns = ((wa, turns_a), (wb, turns_b))[n % 2]
        pltpu.make_async_copy(away[n], p_ref.at[n], sems.at[n]).wait()
        for r in range(nterm):
            real, imag = (p_ref[n, m * nev : (m + 1) * nev] for m in (2 * r, 2 * r + 1))
            set_turns(turns, r, real, imag)
        w_ref[...] = jnp.zeros(w_ref.shape, w_ref.dtype)

        def write(spin, column, a, b, w_ref=w_ref):
            add_to(w_ref, along(spin, nev), along(column, nev), a)
            add_to(w_ref, along(spin, nev), along(column, nev, width), b)

        fill_spin_blocks(codes_of(gamma, mom ^ piece, nterm), turns, write)
        pltpu.make_async_copy(products[0], hs.at[n], sems.at[2 + n]).wait()
        for tile in range(width // TILE):
            lanes = slice(tile * TILE, (tile + 1) * TILE)
            weights = w_ref[lanes, :]
            k_ref[n, :width, lanes] = lax.dot_general(
                hs[n, :, width:], weights, NT_DIMS, preferred_element_type=jnp.float32
            )
            k_ref[n, width:, lanes] = lax.dot_general(
                hs[n, :, : 2 * width], weights, NT_DIMS, preferred_element_type=jnp.float32
            )


def other_flag(plan, sizes):
    return lax.rem(plan.hops(0), 2) if sizes[2] == 2 else jnp.int32(1)


def other_kernel_02(sizes, seps, gamma, partner, tick, h0, h1, h2, h3, proj, near, same, cross, *refs):
    k_ref, label, tags, sems, refs = refs[0], refs[1], refs[2], refs[3], (refs[0],) + refs[4:]
    plan = Plan(seps, sizes)
    rows = proj.shape[1]
    low, at = span(0, rows), plan.local(0)
    sources = (((proj.at[at], near.at[at]), (same.at[low], cross.at[low])), other_flag(plan, sizes))

    def before():
        run_copies([(cross.at[pl.ds(2 * rows, 2 * TAG_ROWS)], tags)], sems)
        find_labels(plan, partner, tick, tags, label)

    other_products((0, 2), gamma, label, (h0, h1, h2, h3), sources, refs, before)


def other_kernel_13(sizes, seps, gamma, label, h0, h1, h2, h3, core, near, same, cross, *refs):
    plan = Plan(seps, sizes)
    rows = core.shape[1]
    away, at = span(1 if sizes[2] == 2 else 0, rows), plan.local(0)
    sources = (((core.at[at], near.at[at]), (same.at[away], cross.at[away])), other_flag(plan, sizes))
    other_products((1, 3), gamma, label, (h0, h1, h2, h3), sources, refs)


def row_sums(k_refs, source, offset, totals):
    rows = 16
    width = source.shape[-1]
    nev = totals[0].shape[-1]

    def step(index, totals):
        row = pl.multiple_of(index * rows, rows)
        here = pl.ds(pl.multiple_of(offset + row, rows), rows)
        later = pl.ds(pl.multiple_of(width + offset + row, rows), rows)
        totals = list(totals)
        for spin in range(NSPIN):
            lanes = along(spin, nev)
            real = source[0, pl.ds(row, rows), lanes].astype(jnp.float32)
            imag = source[1, pl.ds(row, rows), lanes].astype(jnp.float32)
            for n in range(len(totals) // 2):
                k_ref, p = k_refs[n // 2], n % 2
                kr, ki = k_ref[p, here, lanes], k_ref[p, later, lanes]
                totals[2 * n] += real * kr - imag * ki
                totals[2 * n + 1] += real * ki + imag * kr
        return tuple(totals)

    return lax.fori_loop(0, source.shape[1] // rows, step, totals)


def early_kernel(sizes, seps, ka, kb, near, far, sums_ref, part_ref, sems):
    plan = Plan(seps, sizes)
    flag = lax.rem(lax.div(plan.hops(0), max(sizes[2] // 2, 1)), 2)

    @pl.when(flag == 0)
    def _():
        run_copies([(near, part_ref)], sems)

    @pl.when(flag != 0)
    def _():
        run_copies([(far, part_ref)], sems)

    zero = tuple(jnp.zeros(sums_ref.shape[1:], jnp.float32) for _ in range(sums_ref.shape[0]))
    for n, total in enumerate(row_sums((ka, kb), part_ref, 0, zero)):
        sums_ref[n] = total


def late_kernel(sizes, sep_count, seps, label, ka, kb, rest_ref, sums_ref, out_ref):
    plan = Plan(seps, sizes)
    count = sums_ref.shape[0] // 2
    width = rest_ref.shape[-1]
    start = ka.shape[-1] - rest_ref.shape[1]
    totals = row_sums((ka, kb), rest_ref, start, tuple(sums_ref[n] for n in range(2 * count)))
    sums = [jnp.sum(total, axis=0, keepdims=True) for total in totals]
    sums = [jnp.sum(total, axis=1, keepdims=True) * (1.0 / width) for total in sums]
    shape = out_ref.shape[1:]
    spot = lax.broadcasted_iota(jnp.int32, shape, 0) * shape[1]
    spot = spot + lax.broadcasted_iota(jnp.int32, shape, 1)
    here = spot // 2 == plan.pair_time * sep_count + plan.sep_index
    if plan.live is not None:
        here = here & plan.live
    values = [jnp.where(spot % 2 == 0, sums[2 * p], sums[2 * p + 1]) for p in range(count)]
    lines = []
    for op in range(count):
        line = jnp.zeros(shape, jnp.float32)
        for p, value in zip((0, 2, 1, 3), values):
            line = jnp.where(label[p] == op, value, line)
        lines.append(jnp.where(here, line, 0.0))
    for n in range(out_ref.shape[0]):
        out_ref[n] = lines[n % count]


def smem():
    return pl.BlockSpec(memory_space=pltpu.SMEM)


def vmem():
    return pl.BlockSpec(memory_space=pltpu.VMEM)


def anywhere():
    return pl.BlockSpec(memory_space=pl.ANY)


def hbm():
    return pl.BlockSpec(memory_space=pltpu.HBM)


def limit(mib):
    return pltpu.CompilerParams(vmem_limit_bytes=mib * MIB)


def shards(peram_blocks, projections, gamma_index, partner, separations):
    src_count, snk_count = lax.axis_size("src"), lax.axis_size("snk")
    mom_count = lax.axis_size("mom")
    slices, offsets = peram_blocks.shape[:2]
    width = peram_blocks.shape[-1]
    nterm, nev = projections.shape[2], projections.shape[-1]
    time_count = slices * src_count
    sep_count = separations.shape[0]
    half_snk = snk_count // 2
    rows = nterm * 2 * nev
    sizes = (slices, offsets, src_count, snk_count)
    proj = projections.reshape(slices, rows, nev)

    def swap_mom(array, i):
        return lax.ppermute(array, "mom", [(a, a ^ i) for a in range(mom_count)])

    def swap_snk(array):
        pairs = [(a, (a + half_snk) % snk_count) for a in range(snk_count)]
        return lax.ppermute(array, "snk", pairs)

    def next_src(array, step=1, i=0):
        pairs = [
            (((a + step) % src_count) * mom_count + (b ^ i), a * mom_count + b)
            for a in range(src_count)
            for b in range(mom_count)
        ]
        return lax.ppermute(array, ("src", "mom"), pairs)

    def most_of(array, amount):
        step = 1
        while 2 * step < src_count:
            array = jnp.where((amount // step) % 2 != 0, next_src(array, step), array)
            step *= 2
        return array, next_src(array, step)

    def call(kernel, name, in_specs, out_specs, out_shape, scratch, mib, aliases=None):
        cost = pl.CostEstimate(flops=WEIGHT, bytes_accessed=WEIGHT // 1000, transcendentals=0)
        return pl.pallas_call(
            kernel,
            in_specs=in_specs,
            out_specs=out_specs,
            out_shape=out_shape,
            scratch_shapes=scratch,
            input_output_aliases=aliases or {},
            compiler_params=limit(mib),
            cost_estimate=cost,
            name=name,
        )

    def bf16(*shape):
        return jax.ShapeDtypeStruct(shape, jnp.bfloat16)

    def dma(count):
        return pltpu.SemaphoreType.DMA((count,))

    part = functools.partial
    split = (width * SPLIT // 16) // 16 * 16
    two = bf16(2 * rows, nev)
    tagged = bf16(2 * rows + TAG_ROWS, nev)
    first_shape, rest_shape = bf16(2, split, width), bf16(2, width - split, width)
    token = bf16(16, 128)

    def buffers(shapes):
        return [pltpu.VMEM(shape.shape, shape.dtype) for shape in shapes]

    def alias(kernel, name, in_specs, out_shape, aliases, operands):
        return pl.pallas_call(
            kernel,
            in_specs=in_specs,
            out_specs=[anywhere()] * len(aliases) + [vmem()],
            out_shape=out_shape,
            input_output_aliases=aliases,
            compiler_params=limit(20),
            cost_estimate=pl.CostEstimate(
                flops=WEIGHT, bytes_accessed=WEIGHT // 1000, transcendentals=0
            ),
            name=name,
        )(*operands)

    leaving = [first_shape, rest_shape]
    first, rest, tick = call(
        part(pack_first, sizes),
        "pack_first",
        [smem()] * 2 + [hbm()],
        [hbm()] * 2 + [vmem()],
        leaving + [token],
        buffers(leaving) + [dma(2), dma(2)],
        58,
    )(separations, partner, peram_blocks)

    plan = Plan(separations, sizes)
    near = swap_mom(proj, 2)
    core = swap_mom(proj, 1)
    first = swap_snk(first)
    rest_near, rest_far = most_of(rest, plan.peer_hops())
    tick = swap_mom(tick, 1)
    u_scratch = pltpu.VMEM((width, 2 * width), jnp.bfloat16)
    turns = pltpu.VMEM((nterm, 4, nev, nev), jnp.bfloat16)
    piece = pltpu.VMEM((1, rows, nev), jnp.bfloat16)
    pieces = pltpu.VMEM((2, rows, nev), jnp.bfloat16)
    product = bf16(width, 3 * width)
    y, h0, done_0 = call(
        part(own_kernel_0, sizes),
        "own_products_0",
        [smem()] * 2 + [hbm()] * 2,
        [vmem()] * 3,
        [bf16(2 * width, 2 * width), product, token],
        [pltpu.VMEM((2, width, width), jnp.bfloat16), piece, u_scratch, turns, dma(2)],
        58,
    )(separations, gamma_index, peram_blocks, proj)
    leaving = [two, bf16(2 * (rows + TAG_ROWS), nev)]
    far_same, far_cross = call(
        part(pack, sizes),
        "pack",
        [smem()] * 2 + [hbm(), vmem(), vmem()],
        [hbm()] * 2,
        leaving,
        buffers(leaving) + [dma(4), dma(2)],
        58,
    )(separations, partner, proj, tick, done_0)
    if src_count == 2:
        far_same, far_cross = next_src(far_same), next_src(far_cross, 1, 2)
    else:
        far_cross = swap_mom(far_cross, 2)
    def own_one(number, source, after):
        return call(
            part(own_kernel, number),
            "own_products_%d" % number,
            [smem(), hbm(), vmem(), vmem()],
            [vmem()] * 2,
            [product, token],
            [piece, u_scratch, turns, dma(1)],
            20,
        )(gamma_index, source, y, after)

    h1, done_1 = own_one(1, core, done_0)
    near, _ = alias(
        gate_one,
        "gate_near",
        [vmem(), anywhere()],
        [bf16(*proj.shape), token],
        {1: 0},
        (done_1, near),
    )
    near_core = swap_mom(near, 1)

    if src_count > 2:
        rest_near = jnp.where(plan.peer_hops() // (src_count // 2) != 0, rest_far, rest_near)
        rest_far = rest_near
    rest, chosen = call(
        part(choose, sizes),
        "choose",
        [smem()] + [hbm()] * 2 + [vmem()],
        [vmem()] * 2,
        [rest_shape, token],
        [dma(1)],
        20,
    )(separations, rest_near, rest_far, done_1)
    rest = swap_snk(rest)
    h2, done_2 = own_one(2, near, done_1)
    h3, done_3 = own_one(3, near_core, chosen)
    first, _ = alias(
        gate_one, "gate_first", [vmem(), anywhere()], [first_shape, token], {1: 0}, (done_3, first)
    )
    first_near, first_far = most_of(first, plan.hops(0))
    far_same, far_cross, _ = alias(
        gate_far,
        "gate_far",
        [vmem()] + [anywhere()] * 2,
        [two, bf16(2 * (rows + TAG_ROWS), nev), token],
        {1: 0, 2: 1},
        (swap_mom(done_3, 1), far_same, far_cross),
    )
    if src_count == 2:
        far = [far_same, far_cross, swap_mom(far_same, 1), swap_mom(far_cross, 1)]
    else:

        def moved(array):
            array = lax.dynamic_index_in_dim(array, plan.local(0), 0, keepdims=False)
            if src_count == 1:
                return array
            array, away = most_of(array, plan.hops(0))
            return jnp.where(plan.hops(0) // (src_count // 2) != 0, away, array)

        far = [moved(array) for array in (proj, near, core, near_core)]
        far[1] = jnp.concatenate([far[1], far[1], far_cross[2 * rows :]])

    k_shape = jax.ShapeDtypeStruct((2, 2 * width, width), jnp.float32)
    scratch = [pieces, pltpu.VMEM((2, width, 3 * width), jnp.bfloat16)]
    scratch += [u_scratch, u_scratch, turns, turns, dma(4)]
    ka, label = call(
        part(other_kernel_02, sizes),
        "other_products_02",
        [smem()] * 3 + [vmem()] + [hbm()] * 8,
        [vmem(), smem()],
        [k_shape, jax.ShapeDtypeStruct((2 * mom_count,), jnp.int32)],
        [pltpu.VMEM((2 * TAG_ROWS, nev), jnp.bfloat16), dma(1)] + scratch,
        20,
    )(
        separations, gamma_index, partner, tick, h0, h1, h2, h3, proj, near, far[0], far[1],
    )
    kb = call(
        part(other_kernel_13, sizes),
        "other_products_13",
        [smem()] * 3 + [hbm()] * 8,
        vmem(),
        k_shape,
        scratch,
        20,
    )(separations, gamma_index, label, h0, h1, h2, h3, core, near_core, far[2], far[3])

    sums = call(
        part(early_kernel, sizes),
        "early_traces",
        [smem()] + [vmem()] * 2 + [hbm()] * 2,
        vmem(),
        jax.ShapeDtypeStruct((2 * mom_count, 16, nev), jnp.float32),
        buffers([first_shape]) + [dma(1)],
        20,
    )(separations, ka, kb, first_near, first_far)
    device_count = src_count * snk_count * mom_count
    values = time_count * sep_count * 2
    lines = (values + 127) // 128
    out = call(
        part(late_kernel, sizes, sep_count),
        "late_traces",
        [smem()] * 2 + [vmem()] * 4,
        vmem(),
        jax.ShapeDtypeStruct((device_count, lines, 128), jnp.float32),
        [],
        20,
    )(separations, label, ka, kb, rest, sums)
    out = lax.all_to_all(out, ("src", "snk", "mom"), split_axis=0, concat_axis=0, tiled=True)
    out = jnp.sum(out, axis=0).reshape(lines * 128)[:values]
    return out.reshape(time_count, sep_count, 1, 2)


def solution(mesh):
    placed = (
        P("src", "snk", None, None, None),
        P("src", "mom", None, None, None, None),
        P(),
        P("mom"),
        P(),
    )
    return jax.shard_map(
        shards, mesh=mesh, in_specs=placed, out_specs=P(None, None, "mom", None), check_vma=False
    )
```

```python
import functools

import jax
import jax.numpy as jnp
from jax import lax
from jax.experimental import pallas as pl
from jax.experimental.pallas import tpu as pltpu
from jax.sharding import PartitionSpec as P

NSPIN = 4
NT_DIMS = (((1,), (1,)), ((), ()))
MIB = 1024 * 1024
WEIGHT = 10**13
TAG_ROWS = 16
TILE = 256
SPLIT = 10
GAMMAS = (
    (3, 1 | 1 << 2 | 3 << 4 | 3 << 6),
    (3, 2 | 0 << 2 | 0 << 4 | 2 << 6),
    (2, 1 | 3 << 2 | 3 << 4 | 1 << 6),
    (2, 0),
)


def spin_entry(code, row):
    phase = row * 0
    for bit, (flip, phases) in enumerate(GAMMAS):
        on = (code >> bit) & 1
        phase = phase + on * ((phases >> (2 * row)) & 3)
        row = row ^ (on * flip)
    return row, phase & 3


def fill_spin_blocks(codes, turns, write):
    for r, code in enumerate(codes):
        for spin in range(NSPIN):
            column, phase = spin_entry(code, spin)
            write(spin, column, *(turns[r, (n - phase) & 3] for n in (4, 1)))


def set_turns(turns, r, real, imag):
    for n, value in enumerate((real, imag, -real, -imag)):
        turns[r, n] = value


def add_to(ref, rows, lanes, value):
    ref[rows, lanes] = ref[rows, lanes] + value


def along(spin, nev, start=0):
    if isinstance(spin, int):
        return slice(start + spin * nev, start + (spin + 1) * nev)
    return pl.ds(pl.multiple_of(start + spin * nev, nev), nev)


class Plan:
    def __init__(self, seps, sizes):
        slices, offsets, src_count, snk_count = sizes
        src, snk, self.mom = (lax.axis_index(name) for name in ("src", "snk", "mom"))
        half_snk = snk_count // 2
        self.slices, self.time_count = slices, slices * src_count
        self.forward = snk < half_snk
        base = lax.rem(snk, half_snk) * offsets
        self.keep = jnp.where(self.forward, 0, offsets - 1)
        self.give = offsets - 1 - self.keep
        self.sep_index = base + self.keep
        sign = jnp.where(self.forward, 1, -1)
        self.shift = sign * seps[base + self.keep]
        self.peer_shift = -sign * seps[base + self.give]
        self.own_time = src * slices + self.mom
        late = jnp.where(self.forward, 0, self.shift)
        self.pair_time = lax.rem(self.own_time + late + self.time_count, self.time_count)
        self.live = self.forward if offsets == 1 else None

    def _sum(self, place, amount):
        return lax.rem(place + amount + self.time_count, self.time_count)

    def local(self, i):
        return lax.rem(self._sum(self.mom ^ i, self.shift), self.slices)

    def hops(self, i):
        return lax.div(self._sum(self.mom ^ i, self.shift), self.slices)

    def peer_local(self):
        return lax.rem(self._sum(self.mom, self.peer_shift), self.slices)

    def peer_hops(self):
        return lax.div(self._sum(self.mom, self.peer_shift), self.slices)


def run_copies(copies, sems):
    handles = [
        pltpu.make_async_copy(source, target, sems.at[n])
        for n, (source, target) in enumerate(copies)
    ]
    for handle in handles:
        handle.start()
    for handle in handles:
        handle.wait()


def span(index, rows):
    return pl.ds(index * rows, rows)


def through(parts, ins, leaving):
    started, n = [], 0
    for copies, buffer, target in parts:
        group = []
        for source, spot in copies:
            group.append(pltpu.make_async_copy(source, spot, ins.at[n]))
            group[-1].start()
            n += 1
        started.append(group)
    handles = []
    for n, (group, (_, buffer, target)) in enumerate(zip(started, parts)):
        for handle in group:
            handle.wait()
        handles.append(pltpu.make_async_copy(buffer, target, leaving.at[n]))
        handles[-1].start()
    for handle in handles:
        handle.wait()


def two_slices(proj, buffer, first, second):
    rows = proj.shape[1]
    return [(proj.at[n], buffer.at[span(i, rows)]) for i, n in enumerate((first, second))]


def tag_of(partner, lanes):
    number = jnp.full((TAG_ROWS, lanes), partner[0].astype(jnp.float32))
    return number.astype(jnp.bfloat16)


def pack_first(sizes, seps, partner, peram, *refs):
    outs, token, buffers, (ins, leaving) = refs[:2], refs[2], refs[3:5], refs[5:]
    plan = Plan(seps, sizes)
    start, copies = 0, []
    for buffer in buffers:
        rows = buffer.shape[1]
        source = peram.at[plan.peer_local(), plan.give, :, pl.ds(start, rows)]
        copies.append([(source, buffer)])
        start += rows
    token[...] = tag_of(partner, token.shape[-1])
    through(list(zip(copies, buffers, outs)), ins, leaving)


def pack(sizes, seps, partner, proj, tick, after, *refs):
    outs, buffers, (ins, leaving) = refs[:2], refs[2:4], refs[4:]
    plan = Plan(seps, sizes)
    rows = proj.shape[1]
    same, cross = buffers
    cross[pl.ds(2 * rows, TAG_ROWS), :] = tag_of(partner, cross.shape[-1])
    cross[pl.ds(2 * rows + TAG_ROWS, TAG_ROWS), :] = tick[...]
    copies = [
        two_slices(proj, same, plan.local(0), plan.local(1)),
        two_slices(proj, cross, plan.local(2), plan.local(3)),
    ]
    through(list(zip(copies, buffers, outs)), ins, leaving)


def choose(sizes, seps, near, far, after, out, token, sems):
    flag = lax.rem(Plan(seps, sizes).peer_hops(), 2)

    @pl.when(flag == 0)
    def _():
        run_copies([(near, out)], sems)

    @pl.when(flag != 0)
    def _():
        run_copies([(far, out)], sems)

    token[...] = after[...]


def gate_one(after, array, array_out, token):
    token[...] = after[...]


def gate_both(first, rest, after, first_out, rest_out, token):
    token[...] = after[...]


def gate_far(after, same, cross, same_out, cross_out, token):
    token[...] = after[...]


def own_fill(codes, p_ref, n, u_ref, turns):
    nev = turns.shape[-1]
    width = u_ref.shape[0]
    for r in range(len(codes)):
        real, imag = (p_ref[n, m * nev : (m + 1) * nev].T for m in (2 * r, 2 * r + 1))
        set_turns(turns, r, real, imag)
    u_ref[...] = jnp.zeros(u_ref.shape, u_ref.dtype)

    def write(spin, column, a, b):
        add_to(u_ref, along(column, nev), along(spin, nev), a)
        add_to(u_ref, along(column, nev), along(spin, nev, width), b)

    fill_spin_blocks(codes, turns, write)


def own_dot(u_ref, y_ref, ht):
    width = u_ref.shape[0]
    for tile in range(2 * width // TILE):
        start = tile * TILE
        out = lax.dot_general(
            u_ref[...], y_ref[start : start + TILE, :], NT_DIMS, preferred_element_type=jnp.float32
        ).astype(jnp.bfloat16)
        if start < width:
            ht[:, width + start : width + start + TILE] = out
        else:
            ht[:, start - width : start - width + TILE] = out
            ht[:, width + start : width + start + TILE] = -out


def codes_of(gamma, op, nterm):
    return [gamma[op, r] for r in range(nterm)]


def own_kernel_0(sizes, seps, gamma, peram, proj, y_ref, ht, token, x_ref, p_ref, u_ref, turns, sems):
    plan = Plan(seps, sizes)
    mom = plan.mom
    run_copies([(peram.at[mom, plan.keep], x_ref), (proj.at[mom], p_ref.at[0])], sems)
    width = x_ref.shape[-1]
    real, imag = x_ref[0], x_ref[1]
    y_ref[:width, :width] = real
    y_ref[:width, width:] = -imag
    y_ref[width:, :width] = imag
    y_ref[width:, width:] = real
    own_fill(codes_of(gamma, mom, turns.shape[0]), p_ref, 0, u_ref, turns)
    own_dot(u_ref, y_ref, ht)
    token[...] = jnp.zeros(token.shape, token.dtype)


def own_kernel(piece, gamma, source, y_ref, after, ht, token, p_ref, u_ref, turns, sems):
    mom = lax.axis_index("mom")
    run_copies([(source.at[mom], p_ref.at[0])], sems)
    own_fill(codes_of(gamma, mom ^ piece, turns.shape[0]), p_ref, 0, u_ref, turns)
    own_dot(u_ref, y_ref, ht)
    token[...] = jnp.zeros(token.shape, token.dtype)


def find_labels(plan, partner, tick, tags, label):
    mom = plan.mom

    def number(tag):
        return jnp.max(tag.astype(jnp.float32)).astype(jnp.int32)

    partners = [partner[0], number(tick[...]), number(tags[:TAG_ROWS]), number(tags[TAG_ROWS:])]
    count = len(partners)
    for p in range(count):
        back = jnp.int32(0)
        for i, value in enumerate(partners):
            back = back + jnp.where(value == (mom ^ p), mom ^ i, 0)
        label[p] = jnp.where(plan.forward, back, mom ^ p)
        label[count + p] = jnp.where(plan.forward, back, partners[p]) ^ mom


def other_products(pieces, gamma, label, products, sources, refs, before=None):
    k_ref, p_ref, hs, wa, wb, turns_a, turns_b, sems = refs
    mom = lax.axis_index("mom")
    nterm, nev = turns_a.shape[0], turns_a.shape[-1]
    width = wa.shape[0]
    (here, away), flag = sources
    for n in range(2):
        for wanted, refs_now in ((0, here), (1, away)):

            @pl.when(flag == wanted)
            def _():
                pltpu.make_async_copy(refs_now[n], p_ref.at[n], sems.at[n]).start()

    if before is not None:
        before()
    for n, piece in enumerate(pieces):
        for own, source in enumerate(products):

            @pl.when(label[4 + piece] == own)
            def _():
                pltpu.make_async_copy(source, hs.at[n], sems.at[2 + n]).start()

    for n, piece in enumerate(pieces):
        w_ref, turns = ((wa, turns_a), (wb, turns_b))[n % 2]
        pltpu.make_async_copy(away[n], p_ref.at[n], sems.at[n]).wait()
        for r in range(nterm):
            real, imag = (p_ref[n, m * nev : (m + 1) * nev] for m in (2 * r, 2 * r + 1))
            set_turns(turns, r, real, imag)
        w_ref[...] = jnp.zeros(w_ref.shape, w_ref.dtype)

        def write(spin, column, a, b, w_ref=w_ref):
            add_to(w_ref, along(spin, nev), along(column, nev), a)
            add_to(w_ref, along(spin, nev), along(column, nev, width), b)

        fill_spin_blocks(codes_of(gamma, mom ^ piece, nterm), turns, write)
        pltpu.make_async_copy(products[0], hs.at[n], sems.at[2 + n]).wait()
        for tile in range(width // TILE):
            lanes = slice(tile * TILE, (tile + 1) * TILE)
            weights = w_ref[lanes, :]
            k_ref[n, :width, lanes] = lax.dot_general(
                hs[n, :, width:], weights, NT_DIMS, preferred_element_type=jnp.float32
            )
            k_ref[n, width:, lanes] = lax.dot_general(
                hs[n, :, : 2 * width], weights, NT_DIMS, preferred_element_type=jnp.float32
            )


def other_flag(plan, sizes):
    return lax.rem(plan.hops(0), 2) if sizes[2] == 2 else jnp.int32(1)


def other_kernel_02(sizes, seps, gamma, partner, tick, h0, h1, h2, h3, proj, near, same, cross, *refs):
    k_ref, label, tags, sems, refs = refs[0], refs[1], refs[2], refs[3], (refs[0],) + refs[4:]
    plan = Plan(seps, sizes)
    rows = proj.shape[1]
    low, at = span(0, rows), plan.local(0)
    sources = (((proj.at[at], near.at[at]), (same.at[low], cross.at[low])), other_flag(plan, sizes))

    def before():
        run_copies([(cross.at[pl.ds(2 * rows, 2 * TAG_ROWS)], tags)], sems)
        find_labels(plan, partner, tick, tags, label)

    other_products((0, 2), gamma, label, (h0, h1, h2, h3), sources, refs, before)


def other_kernel_13(sizes, seps, gamma, label, h0, h1, h2, h3, core, near, same, cross, *refs):
    plan = Plan(seps, sizes)
    rows = core.shape[1]
    away, at = span(1 if sizes[2] == 2 else 0, rows), plan.local(0)
    sources = (((core.at[at], near.at[at]), (same.at[away], cross.at[away])), other_flag(plan, sizes))
    other_products((1, 3), gamma, label, (h0, h1, h2, h3), sources, refs)


def row_sums(k_refs, source, offset, totals):
    rows = 16
    width = source.shape[-1]
    nev = totals[0].shape[-1]

    def step(index, totals):
        row = pl.multiple_of(index * rows, rows)
        here = pl.ds(pl.multiple_of(offset + row, rows), rows)
        later = pl.ds(pl.multiple_of(width + offset + row, rows), rows)
        totals = list(totals)
        for spin in range(NSPIN):
            lanes = along(spin, nev)
            real = source[0, pl.ds(row, rows), lanes].astype(jnp.float32)
            imag = source[1, pl.ds(row, rows), lanes].astype(jnp.float32)
            for n in range(len(totals) // 2):
                k_ref, p = k_refs[n // 2], n % 2
                kr, ki = k_ref[p, here, lanes], k_ref[p, later, lanes]
                totals[2 * n] += real * kr - imag * ki
                totals[2 * n + 1] += real * ki + imag * kr
        return tuple(totals)

    return lax.fori_loop(0, source.shape[1] // rows, step, totals)


def early_kernel(sizes, seps, ka, kb, near, far, sums_ref, part_ref, sems):
    plan = Plan(seps, sizes)
    flag = lax.rem(lax.div(plan.hops(0), max(sizes[2] // 2, 1)), 2)

    @pl.when(flag == 0)
    def _():
        run_copies([(near, part_ref)], sems)

    @pl.when(flag != 0)
    def _():
        run_copies([(far, part_ref)], sems)

    zero = tuple(jnp.zeros(sums_ref.shape[1:], jnp.float32) for _ in range(sums_ref.shape[0]))
    for n, total in enumerate(row_sums((ka, kb), part_ref, 0, zero)):
        sums_ref[n] = total


def late_kernel(sizes, sep_count, rest_ref, seps, label, ka, kb, sums_ref, out_ref):
    plan = Plan(seps, sizes)
    count = sums_ref.shape[0] // 2
    width = rest_ref.shape[-1]
    start = ka.shape[-1] - rest_ref.shape[1]
    totals = row_sums((ka, kb), rest_ref, start, tuple(sums_ref[n] for n in range(2 * count)))
    sums = [jnp.sum(total, axis=0, keepdims=True) for total in totals]
    sums = [jnp.sum(total, axis=1, keepdims=True) * (1.0 / width) for total in sums]
    shape = out_ref.shape[1:]
    spot = lax.broadcasted_iota(jnp.int32, shape, 0) * shape[1]
    spot = spot + lax.broadcasted_iota(jnp.int32, shape, 1)
    here = spot // 2 == plan.pair_time * sep_count + plan.sep_index
    if plan.live is not None:
        here = here & plan.live
    values = [jnp.where(spot % 2 == 0, sums[2 * p], sums[2 * p + 1]) for p in range(count)]
    lines = []
    for op in range(count):
        line = jnp.zeros(shape, jnp.float32)
        for p, value in zip((0, 2, 1, 3), values):
            line = jnp.where(label[p] == op, value, line)
        lines.append(jnp.where(here, line, 0.0))
    for n in range(out_ref.shape[0]):
        out_ref[n] = lines[n % count]


def smem():
    return pl.BlockSpec(memory_space=pltpu.SMEM)


def vmem():
    return pl.BlockSpec(memory_space=pltpu.VMEM)


def anywhere():
    return pl.BlockSpec(memory_space=pl.ANY)


def hbm():
    return pl.BlockSpec(memory_space=pltpu.HBM)


def limit(mib):
    return pltpu.CompilerParams(vmem_limit_bytes=mib * MIB)


def shards(peram_blocks, projections, gamma_index, partner, separations):
    src_count, snk_count = lax.axis_size("src"), lax.axis_size("snk")
    mom_count = lax.axis_size("mom")
    slices, offsets = peram_blocks.shape[:2]
    width = peram_blocks.shape[-1]
    nterm, nev = projections.shape[2], projections.shape[-1]
    time_count = slices * src_count
    sep_count = separations.shape[0]
    half_snk = snk_count // 2
    rows = nterm * 2 * nev
    sizes = (slices, offsets, src_count, snk_count)
    proj = projections.reshape(slices, rows, nev)

    def swap_mom(array, i):
        return lax.ppermute(array, "mom", [(a, a ^ i) for a in range(mom_count)])

    def swap_snk(array):
        pairs = [(a, (a + half_snk) % snk_count) for a in range(snk_count)]
        return lax.ppermute(array, "snk", pairs)

    def next_src(array, step=1, i=0):
        pairs = [
            (((a + step) % src_count) * mom_count + (b ^ i), a * mom_count + b)
            for a in range(src_count)
            for b in range(mom_count)
        ]
        return lax.ppermute(array, ("src", "mom"), pairs)

    def most_of(array, amount):
        step = 1
        while 2 * step < src_count:
            array = jnp.where((amount // step) % 2 != 0, next_src(array, step), array)
            step *= 2
        return array, next_src(array, step)

    def call(kernel, name, in_specs, out_specs, out_shape, scratch, mib, aliases=None):
        cost = pl.CostEstimate(flops=WEIGHT, bytes_accessed=WEIGHT // 1000, transcendentals=0)
        return pl.pallas_call(
            kernel,
            in_specs=in_specs,
            out_specs=out_specs,
            out_shape=out_shape,
            scratch_shapes=scratch,
            input_output_aliases=aliases or {},
            compiler_params=limit(mib),
            cost_estimate=cost,
            name=name,
        )

    def bf16(*shape):
        return jax.ShapeDtypeStruct(shape, jnp.bfloat16)

    def dma(count):
        return pltpu.SemaphoreType.DMA((count,))

    part = functools.partial
    split = (width * SPLIT // 16) // 16 * 16
    two = bf16(2 * rows, nev)
    tagged = bf16(2 * rows + TAG_ROWS, nev)
    first_shape, rest_shape = bf16(2, split, width), bf16(2, width - split, width)
    token = bf16(16, 128)

    def buffers(shapes):
        return [pltpu.VMEM(shape.shape, shape.dtype) for shape in shapes]

    def alias(kernel, name, in_specs, out_shape, aliases, operands):
        return pl.pallas_call(
            kernel,
            in_specs=in_specs,
            out_specs=[anywhere()] * len(aliases) + [vmem()],
            out_shape=out_shape,
            input_output_aliases=aliases,
            compiler_params=limit(20),
            cost_estimate=pl.CostEstimate(
                flops=WEIGHT, bytes_accessed=WEIGHT // 1000, transcendentals=0
            ),
            name=name,
        )(*operands)

    leaving = [first_shape, rest_shape]
    first, rest, tick = call(
        part(pack_first, sizes),
        "pack_first",
        [smem()] * 2 + [hbm()],
        [hbm()] * 2 + [vmem()],
        leaving + [token],
        buffers(leaving) + [dma(2), dma(2)],
        58,
    )(separations, partner, peram_blocks)

    plan = Plan(separations, sizes)
    near = swap_mom(proj, 2)
    core = swap_mom(proj, 1)
    first = swap_snk(first)
    rest_near, rest_far = most_of(rest, plan.peer_hops())
    tick = swap_mom(tick, 1)
    u_scratch = pltpu.VMEM((width, 2 * width), jnp.bfloat16)
    turns = pltpu.VMEM((nterm, 4, nev, nev), jnp.bfloat16)
    piece = pltpu.VMEM((1, rows, nev), jnp.bfloat16)
    pieces = pltpu.VMEM((2, rows, nev), jnp.bfloat16)
    product = bf16(width, 3 * width)
    y, h0, done_0 = call(
        part(own_kernel_0, sizes),
        "own_products_0",
        [smem()] * 2 + [hbm()] * 2,
        [vmem()] * 3,
        [bf16(2 * width, 2 * width), product, token],
        [pltpu.VMEM((2, width, width), jnp.bfloat16), piece, u_scratch, turns, dma(2)],
        58,
    )(separations, gamma_index, peram_blocks, proj)
    leaving = [two, bf16(2 * (rows + TAG_ROWS), nev)]
    far_same, far_cross = call(
        part(pack, sizes),
        "pack",
        [smem()] * 2 + [hbm(), vmem(), vmem()],
        [hbm()] * 2,
        leaving,
        buffers(leaving) + [dma(4), dma(2)],
        58,
    )(separations, partner, proj, tick, done_0)
    if src_count == 2:
        far_same, far_cross = next_src(far_same), next_src(far_cross, 1, 2)
    else:
        far_cross = swap_mom(far_cross, 2)
    def own_one(number, source, after):
        return call(
            part(own_kernel, number),
            "own_products_%d" % number,
            [smem(), hbm(), vmem(), vmem()],
            [vmem()] * 2,
            [product, token],
            [piece, u_scratch, turns, dma(1)],
            20,
        )(gamma_index, source, y, after)

    h1, done_1 = own_one(1, core, done_0)
    near, _ = alias(
        gate_one,
        "gate_near",
        [vmem(), anywhere()],
        [bf16(*proj.shape), token],
        {1: 0},
        (done_1, near),
    )
    near_core = swap_mom(near, 1)

    if src_count > 2:
        rest_near = jnp.where(plan.peer_hops() // (src_count // 2) != 0, rest_far, rest_near)
        rest_far = rest_near
    rest, chosen = call(
        part(choose, sizes),
        "choose",
        [smem()] + [hbm()] * 2 + [vmem()],
        [vmem()] * 2,
        [rest_shape, token],
        [dma(1)],
        20,
    )(separations, rest_near, rest_far, done_1)
    h2, done_2 = own_one(2, near, done_1)
    h3, done_3 = own_one(3, near_core, chosen)
    first, rest, _ = alias(
        gate_both,
        "gate_both",
        [anywhere()] * 2 + [vmem()],
        [first_shape, rest_shape, token],
        {0: 0, 1: 1},
        (first, rest, done_3),
    )
    rest = swap_snk(rest)
    first_near, first_far = most_of(first, plan.hops(0))
    far_same, far_cross, _ = alias(
        gate_far,
        "gate_far",
        [vmem()] + [anywhere()] * 2,
        [two, bf16(2 * (rows + TAG_ROWS), nev), token],
        {1: 0, 2: 1},
        (swap_mom(done_3, 1), far_same, far_cross),
    )
    if src_count == 2:
        far = [far_same, far_cross, swap_mom(far_same, 1), swap_mom(far_cross, 1)]
    else:

        def moved(array):
            array = lax.dynamic_index_in_dim(array, plan.local(0), 0, keepdims=False)
            if src_count == 1:
                return array
            array, away = most_of(array, plan.hops(0))
            return jnp.where(plan.hops(0) // (src_count // 2) != 0, away, array)

        far = [moved(array) for array in (proj, near, core, near_core)]
        far[1] = jnp.concatenate([far[1], far[1], far_cross[2 * rows :]])

    k_shape = jax.ShapeDtypeStruct((2, 2 * width, width), jnp.float32)
    scratch = [pieces, pltpu.VMEM((2, width, 3 * width), jnp.bfloat16)]
    scratch += [u_scratch, u_scratch, turns, turns, dma(4)]
    ka, label = call(
        part(other_kernel_02, sizes),
        "other_products_02",
        [smem()] * 3 + [vmem()] + [hbm()] * 8,
        [vmem(), smem()],
        [k_shape, jax.ShapeDtypeStruct((2 * mom_count,), jnp.int32)],
        [pltpu.VMEM((2 * TAG_ROWS, nev), jnp.bfloat16), dma(1)] + scratch,
        20,
    )(
        separations, gamma_index, partner, tick, h0, h1, h2, h3, proj, near, far[0], far[1],
    )
    kb = call(
        part(other_kernel_13, sizes),
        "other_products_13",
        [smem()] * 3 + [hbm()] * 8,
        vmem(),
        k_shape,
        scratch,
        20,
    )(separations, gamma_index, label, h0, h1, h2, h3, core, near_core, far[2], far[3])

    sums = call(
        part(early_kernel, sizes),
        "early_traces",
        [smem()] + [vmem()] * 2 + [hbm()] * 2,
        vmem(),
        jax.ShapeDtypeStruct((2 * mom_count, 16, nev), jnp.float32),
        buffers([first_shape]) + [dma(1)],
        20,
    )(separations, ka, kb, first_near, first_far)
    device_count = src_count * snk_count * mom_count
    values = time_count * sep_count * 2
    lines = (values + 127) // 128
    out = call(
        part(late_kernel, sizes, sep_count),
        "late_traces",
        [vmem()] + [smem()] * 2 + [vmem()] * 3,
        vmem(),
        jax.ShapeDtypeStruct((device_count, lines, 128), jnp.float32),
        [],
        20,
    )(rest, separations, label, ka, kb, sums)
    out = lax.all_to_all(out, ("src", "snk", "mom"), split_axis=0, concat_axis=0, tiled=True)
    out = jnp.sum(out, axis=0).reshape(lines * 128)[:values]
    return out.reshape(time_count, sep_count, 1, 2)


def solution(mesh):
    placed = (
        P("src", "snk", None, None, None),
        P("src", "mom", None, None, None, None),
        P(),
        P("mom"),
        P(),
    )
    return jax.shard_map(
        shards, mesh=mesh, in_specs=placed, out_specs=P(None, None, "mom", None), check_vma=False
    )
```

```python
import functools

import jax
import jax.numpy as jnp
from jax import lax
from jax.experimental import pallas as pl
from jax.experimental.pallas import tpu as pltpu
from jax.sharding import PartitionSpec as P

NSPIN = 4
NT_DIMS = (((1,), (1,)), ((), ()))
MIB = 1024 * 1024
WEIGHT = 10**13
TAG_ROWS = 16
TILE = 256
GAMMAS = (
    (3, 1 | 1 << 2 | 3 << 4 | 3 << 6),
    (3, 2 | 0 << 2 | 0 << 4 | 2 << 6),
    (2, 1 | 3 << 2 | 3 << 4 | 1 << 6),
    (2, 0),
)


def spin_entry(code, row):
    phase = row * 0
    for bit, (flip, phases) in enumerate(GAMMAS):
        on = (code >> bit) & 1
        phase = phase + on * ((phases >> (2 * row)) & 3)
        row = row ^ (on * flip)
    return row, phase & 3


def fill_spin_blocks(codes, turns, write):
    for r in range(len(codes)):
        fill_term(codes, turns, write, r)


def fill_term(codes, turns, write, r):
    for spin in range(NSPIN):
        column, phase = spin_entry(codes[r], spin)
        write(spin, column, *(turns[r, (n - phase) & 3] for n in (4, 1)))


def set_turns(turns, r, real, imag):
    for n, value in enumerate((real, imag, -real, -imag)):
        turns[r, n] = value


def add_to(ref, rows, lanes, value):
    ref[rows, lanes] = ref[rows, lanes] + value


def along(spin, nev, start=0):
    if isinstance(spin, int):
        return slice(start + spin * nev, start + (spin + 1) * nev)
    return pl.ds(pl.multiple_of(start + spin * nev, nev), nev)


class Plan:
    def __init__(self, seps, sizes):
        slices, offsets, src_count, snk_count = sizes
        src, snk, self.mom = (lax.axis_index(name) for name in ("src", "snk", "mom"))
        half_snk = snk_count // 2
        self.slices, self.time_count = slices, slices * src_count
        self.forward = snk < half_snk
        base = lax.rem(snk, half_snk) * offsets
        self.keep = jnp.where(self.forward, 0, offsets - 1)
        self.give = offsets - 1 - self.keep
        self.sep_index = base + self.keep
        sign = jnp.where(self.forward, 1, -1)
        self.shift = sign * seps[base + self.keep]
        self.peer_shift = -sign * seps[base + self.give]
        self.own_time = src * slices + self.mom
        late = jnp.where(self.forward, 0, self.shift)
        self.pair_time = lax.rem(self.own_time + late + self.time_count, self.time_count)
        self.live = self.forward if offsets == 1 else None

    def _sum(self, place, amount):
        return lax.rem(place + amount + self.time_count, self.time_count)

    def local(self, i):
        return lax.rem(self._sum(self.mom ^ i, self.shift), self.slices)

    def hops(self, i):
        return lax.div(self._sum(self.mom ^ i, self.shift), self.slices)

    def peer_local(self):
        return lax.rem(self._sum(self.mom, self.peer_shift), self.slices)

    def peer_hops(self):
        return lax.div(self._sum(self.mom, self.peer_shift), self.slices)


def run_copies(copies, sems):
    handles = [
        pltpu.make_async_copy(source, target, sems.at[n])
        for n, (source, target) in enumerate(copies)
    ]
    for handle in handles:
        handle.start()
    for handle in handles:
        handle.wait()


def span(index, rows):
    return pl.ds(index * rows, rows)


def through(parts, ins, leaving):
    started, n = [], 0
    for copies, buffer, target in parts:
        group = []
        for source, spot in copies:
            group.append(pltpu.make_async_copy(source, spot, ins.at[n]))
            group[-1].start()
            n += 1
        started.append(group)
    handles = []
    for n, (group, (_, buffer, target)) in enumerate(zip(started, parts)):
        for handle in group:
            handle.wait()
        handles.append(pltpu.make_async_copy(buffer, target, leaving.at[n]))
        handles[-1].start()
    for handle in handles:
        handle.wait()


def two_slices(proj, buffer, first, second):
    rows = proj.shape[1]
    return [(proj.at[n], buffer.at[span(i, rows)]) for i, n in enumerate((first, second))]


def tag_of(partner, lanes):
    number = jnp.full((TAG_ROWS, lanes), partner[0].astype(jnp.float32))
    return number.astype(jnp.bfloat16)


def pack_first(sizes, seps, partner, peram, *refs):
    outs, token, buffers, (ins, leaving) = refs[:2], refs[2], refs[3:5], refs[5:]
    plan = Plan(seps, sizes)
    start, copies = 0, []
    for buffer in buffers:
        rows = buffer.shape[1]
        source = peram.at[plan.peer_local(), plan.give, :, pl.ds(start, rows)]
        copies.append([(source, buffer)])
        start += rows
    token[...] = tag_of(partner, token.shape[-1])
    through(list(zip(copies, buffers, outs)), ins, leaving)


def pack(sizes, seps, partner, proj, tick, after, *refs):
    outs, buffers, (ins, leaving) = refs[:2], refs[2:4], refs[4:]
    plan = Plan(seps, sizes)
    rows = proj.shape[1]
    same, cross = buffers
    cross[pl.ds(2 * rows, TAG_ROWS), :] = tag_of(partner, cross.shape[-1])
    cross[pl.ds(2 * rows + TAG_ROWS, TAG_ROWS), :] = tick[...]
    copies = [
        two_slices(proj, same, plan.local(0), plan.local(1)),
        two_slices(proj, cross, plan.local(2), plan.local(3)),
    ]
    through(list(zip(copies, buffers, outs)), ins, leaving)


def choose(sizes, seps, near, far, after, out, sems):
    flag = lax.rem(Plan(seps, sizes).peer_hops(), 2)

    @pl.when(flag == 0)
    def _():
        run_copies([(near, out)], sems)

    @pl.when(flag != 0)
    def _():
        run_copies([(far, out)], sems)


def gate(first, rest, after, first_out, rest_out, token):
    token[...] = jnp.zeros(token.shape, token.dtype)


def gate_one(after, array, array_out, token):
    token[...] = after[...]


def gate_far(after, same, cross, same_out, cross_out, token):
    token[...] = after[...]


def own_fill(codes, p_ref, n, u_ref, turns):
    nev = turns.shape[-1]
    width = u_ref.shape[0]
    for r in range(len(codes)):
        real, imag = (p_ref[n, m * nev : (m + 1) * nev].T for m in (2 * r, 2 * r + 1))
        set_turns(turns, r, real, imag)
    u_ref[...] = jnp.zeros(u_ref.shape, u_ref.dtype)

    def write(spin, column, a, b):
        add_to(u_ref, along(column, nev), along(spin, nev), a)
        add_to(u_ref, along(column, nev), along(spin, nev, width), b)

    fill_spin_blocks(codes, turns, write)


def own_dot(u_ref, y_ref, ht):
    width = u_ref.shape[0]
    for tile in range(2 * width // TILE):
        start = tile * TILE
        out = lax.dot_general(
            u_ref[...], y_ref[start : start + TILE, :], NT_DIMS, preferred_element_type=jnp.float32
        ).astype(jnp.bfloat16)
        if start < width:
            ht[:, width + start : width + start + TILE] = out
        else:
            ht[:, start - width : start - width + TILE] = out
            ht[:, width + start : width + start + TILE] = -out


def codes_of(gamma, op, nterm):
    return [gamma[op, r] for r in range(nterm)]


def own_kernel_0(sizes, seps, gamma, peram, proj, y_ref, ht, token, x_ref, p_ref, u_ref, turns, sems):
    plan = Plan(seps, sizes)
    mom = plan.mom
    run_copies([(peram.at[mom, plan.keep], x_ref), (proj.at[mom], p_ref.at[0])], sems)
    width = x_ref.shape[-1]
    real, imag = x_ref[0], x_ref[1]
    y_ref[:width, :width] = real
    y_ref[:width, width:] = -imag
    y_ref[width:, :width] = imag
    y_ref[width:, width:] = real
    own_fill(codes_of(gamma, mom, turns.shape[0]), p_ref, 0, u_ref, turns)
    own_dot(u_ref, y_ref, ht)
    token[...] = jnp.zeros(token.shape, token.dtype)


def own_kernel(piece, gamma, source, y_ref, after, ht, token, p_ref, u_ref, turns, sems):
    mom = lax.axis_index("mom")
    run_copies([(source.at[mom], p_ref.at[0])], sems)
    own_fill(codes_of(gamma, mom ^ piece, turns.shape[0]), p_ref, 0, u_ref, turns)
    own_dot(u_ref, y_ref, ht)
    token[...] = jnp.zeros(token.shape, token.dtype)


def find_labels(plan, partner, tick, tags, label):
    mom = plan.mom

    def number(tag):
        return jnp.max(tag.astype(jnp.float32)).astype(jnp.int32)

    partners = [partner[0], number(tick[...]), number(tags[:TAG_ROWS]), number(tags[TAG_ROWS:])]
    count = len(partners)
    for p in range(count):
        back = jnp.int32(0)
        for i, value in enumerate(partners):
            back = back + jnp.where(value == (mom ^ p), mom ^ i, 0)
        label[p] = jnp.where(plan.forward, back, mom ^ p)
        label[count + p] = jnp.where(plan.forward, back, partners[p]) ^ mom


def other_products(pieces, gamma, label, products, sources, refs, before=None):
    k_ref, p_ref, hs, wa, wb, turns_a, turns_b, sems = refs
    mom = lax.axis_index("mom")
    nterm, nev = turns_a.shape[0], turns_a.shape[-1]
    width = wa.shape[0]
    (here, away), flag = sources
    for n in range(2):
        for wanted, refs_now in ((0, here), (1, away)):

            @pl.when(flag == wanted)
            def _():
                pltpu.make_async_copy(refs_now[n], p_ref.at[n], sems.at[n]).start()

    if before is not None:
        before()
    for n, piece in enumerate(pieces):
        for own, source in enumerate(products):

            @pl.when(label[4 + piece] == own)
            def _():
                pltpu.make_async_copy(source, hs.at[n], sems.at[2 + n]).start()

    pairs = ((wa, turns_a), (wb, turns_b))

    def fill(n):
        w_ref, turns = pairs[n]
        codes = codes_of(gamma, mom ^ pieces[n], nterm)

        def write(spin, column, a, b):
            add_to(w_ref, along(spin, nev), along(column, nev), a)
            add_to(w_ref, along(spin, nev), along(column, nev, width), b)

        def step(r):
            rows = slice(r * nev, (r + 1) * nev)
            w_ref[rows, :] = jnp.zeros((nev, w_ref.shape[1]), w_ref.dtype)
            real, imag = (p_ref[n, m * nev : (m + 1) * nev] for m in (2 * r, 2 * r + 1))
            set_turns(turns, r, real, imag)

        def term(r):
            fill_term(codes, turns, write, r)

        return [functools.partial(f, r) for f in (step, term) for r in range(nterm)]

    def dots(n):
        def dot(start, half):
            lanes = slice(start, start + TILE)
            left = slice(width, 3 * width) if half == 0 else slice(0, 2 * width)
            rows = slice(half * width, (half + 1) * width)
            k_ref[n, rows, lanes] = lax.dot_general(
                hs[n, :, left], pairs[n][0][lanes, :], NT_DIMS, preferred_element_type=jnp.float32
            )

        return [functools.partial(dot, tile, half) for tile in range(0, width, TILE) for half in (0, 1)]

    for n in range(2):
        pltpu.make_async_copy(away[n], p_ref.at[n], sems.at[n]).wait()
    for step in fill(0):
        step()
    for n in range(2):
        pltpu.make_async_copy(products[0], hs.at[n], sems.at[2 + n]).wait()
    ahead = fill(1)
    for n, dot in enumerate(dots(0)):
        for step in ahead[2 * n : 2 * n + 2]:
            step()
        dot()
    for dot in dots(1):
        dot()


def other_flag(plan, sizes):
    return lax.rem(plan.hops(0), 2) if sizes[2] == 2 else jnp.int32(1)


def other_kernel_02(sizes, seps, gamma, partner, tick, h0, h1, h2, h3, proj, near, same, cross, *refs):
    k_ref, label, tags, sems, refs = refs[0], refs[1], refs[2], refs[3], (refs[0],) + refs[4:]
    plan = Plan(seps, sizes)
    rows = proj.shape[1]
    low, at = span(0, rows), plan.local(0)
    sources = (((proj.at[at], near.at[at]), (same.at[low], cross.at[low])), other_flag(plan, sizes))

    def before():
        run_copies([(cross.at[pl.ds(2 * rows, 2 * TAG_ROWS)], tags)], sems)
        find_labels(plan, partner, tick, tags, label)

    other_products((0, 2), gamma, label, (h0, h1, h2, h3), sources, refs, before)


def other_kernel_13(sizes, seps, gamma, label, h0, h1, h2, h3, core, near, same, cross, *refs):
    plan = Plan(seps, sizes)
    rows = core.shape[1]
    away, at = span(1 if sizes[2] == 2 else 0, rows), plan.local(0)
    sources = (((core.at[at], near.at[at]), (same.at[away], cross.at[away])), other_flag(plan, sizes))
    other_products((1, 3), gamma, label, (h0, h1, h2, h3), sources, refs)


def row_sums(k_refs, source, offset, totals):
    rows = 16
    width = source.shape[-1]
    nev = totals[0].shape[-1]

    def step(index, totals):
        row = pl.multiple_of(index * rows, rows)
        here = pl.ds(pl.multiple_of(offset + row, rows), rows)
        later = pl.ds(pl.multiple_of(width + offset + row, rows), rows)
        totals = list(totals)
        for spin in range(NSPIN):
            lanes = along(spin, nev)
            real = source[0, pl.ds(row, rows), lanes].astype(jnp.float32)
            imag = source[1, pl.ds(row, rows), lanes].astype(jnp.float32)
            for n in range(len(totals) // 2):
                k_ref, p = k_refs[n // 2], n % 2
                kr, ki = k_ref[p, here, lanes], k_ref[p, later, lanes]
                totals[2 * n] += real * kr - imag * ki
                totals[2 * n + 1] += real * ki + imag * kr
        return tuple(totals)

    return lax.fori_loop(0, source.shape[1] // rows, step, totals)


def trace_kernel(sizes, sep_count, seps, label, ka, kb, near, far, rest, out_ref, first_buf, rest_buf, sems):
    plan = Plan(seps, sizes)
    count = 2 * ka.shape[0]
    width = rest_buf.shape[-1]
    nev = width // NSPIN
    flag = lax.rem(lax.div(plan.hops(0), max(sizes[2] // 2, 1)), 2)
    later = pltpu.make_async_copy(rest, rest_buf, sems.at[1])
    chunk = first_buf.shape[1] // 2
    parts = [pl.ds(n * chunk, chunk) for n in range(2)]
    for wanted, source in ((0, near), (1, far)):

        @pl.when(flag == wanted)
        def _():
            for n, rows in enumerate(parts):
                pltpu.make_async_copy(
                    source.at[:, rows], first_buf.at[:, rows], sems.at[2 * n]
                ).start()

    later.start()
    totals = tuple(jnp.zeros((16, nev), jnp.float32) for _ in range(2 * count))
    for n, rows in enumerate(parts):
        pltpu.make_async_copy(far.at[:, rows], first_buf.at[:, rows], sems.at[2 * n]).wait()
        totals = row_sums((ka, kb), first_buf.at[:, rows], n * chunk, totals)
    later.wait()
    totals = row_sums((ka, kb), rest_buf, first_buf.shape[1], totals)
    sums = [jnp.sum(total, axis=0, keepdims=True) for total in totals]
    sums = [jnp.sum(total, axis=1, keepdims=True) * (1.0 / width) for total in sums]
    shape = out_ref.shape[1:]
    spot = lax.broadcasted_iota(jnp.int32, shape, 0) * shape[1]
    spot = spot + lax.broadcasted_iota(jnp.int32, shape, 1)
    here = spot // 2 == plan.pair_time * sep_count + plan.sep_index
    if plan.live is not None:
        here = here & plan.live
    values = [jnp.where(spot % 2 == 0, sums[2 * p], sums[2 * p + 1]) for p in range(count)]
    lines = []
    for op in range(count):
        line = jnp.zeros(shape, jnp.float32)
        for p, value in zip((0, 2, 1, 3), values):
            line = jnp.where(label[p] == op, value, line)
        lines.append(jnp.where(here, line, 0.0))
    for n in range(out_ref.shape[0]):
        out_ref[n] = lines[n % count]


def smem():
    return pl.BlockSpec(memory_space=pltpu.SMEM)


def vmem():
    return pl.BlockSpec(memory_space=pltpu.VMEM)


def anywhere():
    return pl.BlockSpec(memory_space=pl.ANY)


def hbm():
    return pl.BlockSpec(memory_space=pltpu.HBM)


def limit(mib):
    return pltpu.CompilerParams(vmem_limit_bytes=mib * MIB)


def shards(peram_blocks, projections, gamma_index, partner, separations):
    src_count, snk_count = lax.axis_size("src"), lax.axis_size("snk")
    mom_count = lax.axis_size("mom")
    slices, offsets = peram_blocks.shape[:2]
    width = peram_blocks.shape[-1]
    nterm, nev = projections.shape[2], projections.shape[-1]
    time_count = slices * src_count
    sep_count = separations.shape[0]
    half_snk = snk_count // 2
    rows = nterm * 2 * nev
    sizes = (slices, offsets, src_count, snk_count)
    proj = projections.reshape(slices, rows, nev)

    def swap_mom(array, i):
        return lax.ppermute(array, "mom", [(a, a ^ i) for a in range(mom_count)])

    def swap_snk(array):
        pairs = [(a, (a + half_snk) % snk_count) for a in range(snk_count)]
        return lax.ppermute(array, "snk", pairs)

    def next_src(array, step=1, i=0):
        pairs = [
            (((a + step) % src_count) * mom_count + (b ^ i), a * mom_count + b)
            for a in range(src_count)
            for b in range(mom_count)
        ]
        return lax.ppermute(array, ("src", "mom"), pairs)

    def most_of(array, amount):
        step = 1
        while 2 * step < src_count:
            array = jnp.where((amount // step) % 2 != 0, next_src(array, step), array)
            step *= 2
        return array, next_src(array, step)

    def call(kernel, name, in_specs, out_specs, out_shape, scratch, mib, aliases=None):
        cost = pl.CostEstimate(flops=WEIGHT, bytes_accessed=WEIGHT // 1000, transcendentals=0)
        return pl.pallas_call(
            kernel,
            in_specs=in_specs,
            out_specs=out_specs,
            out_shape=out_shape,
            scratch_shapes=scratch,
            input_output_aliases=aliases or {},
            compiler_params=limit(mib),
            cost_estimate=cost,
            name=name,
        )

    def bf16(*shape):
        return jax.ShapeDtypeStruct(shape, jnp.bfloat16)

    def dma(count):
        return pltpu.SemaphoreType.DMA((count,))

    part = functools.partial
    split = (width * 5 // 8) // 16 * 16
    two = bf16(2 * rows, nev)
    tagged = bf16(2 * rows + TAG_ROWS, nev)
    first_shape, rest_shape = bf16(2, split, width), bf16(2, width - split, width)
    token = bf16(16, 128)

    def buffers(shapes):
        return [pltpu.VMEM(shape.shape, shape.dtype) for shape in shapes]

    def alias(kernel, name, in_specs, out_shape, aliases, operands):
        return pl.pallas_call(
            kernel,
            in_specs=in_specs,
            out_specs=[anywhere()] * len(aliases) + [vmem()],
            out_shape=out_shape,
            input_output_aliases=aliases,
            compiler_params=limit(20),
            cost_estimate=pl.CostEstimate(
                flops=WEIGHT, bytes_accessed=WEIGHT // 1000, transcendentals=0
            ),
            name=name,
        )(*operands)

    leaving = [first_shape, rest_shape]
    first, rest, tick = call(
        part(pack_first, sizes),
        "pack_first",
        [smem()] * 2 + [hbm()],
        [hbm()] * 2 + [vmem()],
        leaving + [token],
        buffers(leaving) + [dma(2), dma(2)],
        58,
    )(separations, partner, peram_blocks)

    plan = Plan(separations, sizes)
    near = swap_mom(proj, 2)
    core = swap_mom(proj, 1)
    first = swap_snk(first)
    rest_near, rest_far = most_of(rest, plan.peer_hops())
    tick = swap_mom(tick, 1)
    u_scratch = pltpu.VMEM((width, 2 * width), jnp.bfloat16)
    turns = pltpu.VMEM((nterm, 4, nev, nev), jnp.bfloat16)
    piece = pltpu.VMEM((1, rows, nev), jnp.bfloat16)
    pieces = pltpu.VMEM((2, rows, nev), jnp.bfloat16)
    product = bf16(width, 3 * width)
    y, h0, done_0 = call(
        part(own_kernel_0, sizes),
        "own_products_0",
        [smem()] * 2 + [hbm()] * 2,
        [vmem()] * 3,
        [bf16(2 * width, 2 * width), product, token],
        [pltpu.VMEM((2, width, width), jnp.bfloat16), piece, u_scratch, turns, dma(2)],
        58,
    )(separations, gamma_index, peram_blocks, proj)
    leaving = [two, bf16(2 * (rows + TAG_ROWS), nev)]
    far_same, far_cross = call(
        part(pack, sizes),
        "pack",
        [smem()] * 2 + [hbm(), vmem(), vmem()],
        [hbm()] * 2,
        leaving,
        buffers(leaving) + [dma(4), dma(2)],
        58,
    )(separations, partner, proj, tick, done_0)
    if src_count == 2:
        far_same, far_cross = next_src(far_same), next_src(far_cross, 1, 2)
    else:
        far_cross = swap_mom(far_cross, 2)
    def own_one(number, source, after):
        return call(
            part(own_kernel, number),
            "own_products_%d" % number,
            [smem(), hbm(), vmem(), vmem()],
            [vmem()] * 2,
            [product, token],
            [piece, u_scratch, turns, dma(1)],
            20,
        )(gamma_index, source, y, after)

    h1, done_1 = own_one(1, core, done_0)
    near, _ = alias(
        gate_one,
        "gate_near",
        [vmem(), anywhere()],
        [bf16(*proj.shape), token],
        {1: 0},
        (done_1, near),
    )
    near_core = swap_mom(near, 1)

    if src_count > 2:
        rest_near = jnp.where(plan.peer_hops() // (src_count // 2) != 0, rest_far, rest_near)
        rest_far = rest_near
    rest = call(
        part(choose, sizes),
        "choose",
        [smem()] + [hbm()] * 2 + [vmem()],
        vmem(),
        rest_shape,
        [dma(1)],
        20,
    )(separations, rest_near, rest_far, done_1)
    h2, done_2 = own_one(2, near, done_1)
    first, rest, opened = alias(
        gate,
        "gate",
        [anywhere()] * 2 + [vmem()],
        [first_shape, rest_shape, token],
        {0: 0, 1: 1},
        (first, rest, done_2),
    )
    rest = swap_snk(rest)
    first_near, first_far = most_of(first, plan.hops(0))
    h3, done_3 = own_one(3, near_core, opened)
    far_same, far_cross, _ = alias(
        gate_far,
        "gate_far",
        [vmem()] + [anywhere()] * 2,
        [two, bf16(2 * (rows + TAG_ROWS), nev), token],
        {1: 0, 2: 1},
        (done_3, far_same, far_cross),
    )
    if src_count == 2:
        far = [far_same, far_cross, swap_mom(far_same, 1), swap_mom(far_cross, 1)]
    else:

        def moved(array):
            array = lax.dynamic_index_in_dim(array, plan.local(0), 0, keepdims=False)
            if src_count == 1:
                return array
            array, away = most_of(array, plan.hops(0))
            return jnp.where(plan.hops(0) // (src_count // 2) != 0, away, array)

        far = [moved(array) for array in (proj, near, core, near_core)]
        far[1] = jnp.concatenate([far[1], far[1], far_cross[2 * rows :]])

    k_shape = jax.ShapeDtypeStruct((2, 2 * width, width), jnp.float32)
    scratch = [pieces, pltpu.VMEM((2, width, 3 * width), jnp.bfloat16)]
    scratch += [u_scratch, u_scratch, turns, turns, dma(4)]
    ka, label = call(
        part(other_kernel_02, sizes),
        "other_products_02",
        [smem()] * 3 + [vmem()] + [hbm()] * 8,
        [vmem(), smem()],
        [k_shape, jax.ShapeDtypeStruct((2 * mom_count,), jnp.int32)],
        [pltpu.VMEM((2 * TAG_ROWS, nev), jnp.bfloat16), dma(1)] + scratch,
        20,
    )(
        separations, gamma_index, partner, tick, h0, h1, h2, h3, proj, near, far[0], far[1],
    )
    kb = call(
        part(other_kernel_13, sizes),
        "other_products_13",
        [smem()] * 3 + [hbm()] * 8,
        vmem(),
        k_shape,
        scratch,
        20,
    )(separations, gamma_index, label, h0, h1, h2, h3, core, near_core, far[2], far[3])

    device_count = src_count * snk_count * mom_count
    values = time_count * sep_count * 2
    lines = (values + 127) // 128
    out = call(
        part(trace_kernel, sizes, sep_count),
        "traces",
        [smem()] * 2 + [vmem()] * 2 + [hbm()] * 3,
        vmem(),
        jax.ShapeDtypeStruct((device_count, lines, 128), jnp.float32),
        buffers([first_shape, rest_shape]) + [dma(3)],
        20,
    )(separations, label, ka, kb, first_near, first_far, rest)
    out = lax.all_to_all(out, ("src", "snk", "mom"), split_axis=0, concat_axis=0, tiled=True)
    out = jnp.sum(out, axis=0).reshape(lines * 128)[:values]
    return out.reshape(time_count, sep_count, 1, 2)


def solution(mesh):
    placed = (
        P("src", "snk", None, None, None),
        P("src", "mom", None, None, None, None),
        P(),
        P("mom"),
        P(),
    )
    return jax.shard_map(
        shards, mesh=mesh, in_specs=placed, out_specs=P(None, None, "mom", None), check_vma=False
    )
```

```python
import functools

import jax
import jax.numpy as jnp
from jax import lax
from jax.experimental import pallas as pl
from jax.experimental.pallas import tpu as pltpu
from jax.sharding import PartitionSpec as P

NSPIN = 4
NT_DIMS = (((1,), (1,)), ((), ()))
MIB = 1024 * 1024
WEIGHT = 10**13
TAG_ROWS = 16
TILE = 256
GAMMAS = (
    (3, 1 | 1 << 2 | 3 << 4 | 3 << 6),
    (3, 2 | 0 << 2 | 0 << 4 | 2 << 6),
    (2, 1 | 3 << 2 | 3 << 4 | 1 << 6),
    (2, 0),
)


def spin_entry(code, row):
    phase = row * 0
    for bit, (flip, phases) in enumerate(GAMMAS):
        on = (code >> bit) & 1
        phase = phase + on * ((phases >> (2 * row)) & 3)
        row = row ^ (on * flip)
    return row, phase & 3


def fill_spin_blocks(codes, turns, write):
    for r in range(len(codes)):
        fill_term(codes, turns, write, r)


def fill_term(codes, turns, write, r):
    for spin in range(NSPIN):
        column, phase = spin_entry(codes[r], spin)
        write(spin, column, *(turns[r, (n - phase) & 3] for n in (4, 1)))


def set_turns(turns, r, real, imag):
    for n, value in enumerate((real, imag, -real, -imag)):
        turns[r, n] = value


def add_to(ref, rows, lanes, value):
    ref[rows, lanes] = ref[rows, lanes] + value


def along(spin, nev, start=0):
    if isinstance(spin, int):
        return slice(start + spin * nev, start + (spin + 1) * nev)
    return pl.ds(pl.multiple_of(start + spin * nev, nev), nev)


class Plan:
    def __init__(self, seps, sizes):
        slices, offsets, src_count, snk_count = sizes
        src, snk, self.mom = (lax.axis_index(name) for name in ("src", "snk", "mom"))
        half_snk = snk_count // 2
        self.slices, self.time_count = slices, slices * src_count
        self.forward = snk < half_snk
        base = lax.rem(snk, half_snk) * offsets
        self.keep = jnp.where(self.forward, 0, offsets - 1)
        self.give = offsets - 1 - self.keep
        self.sep_index = base + self.keep
        sign = jnp.where(self.forward, 1, -1)
        self.shift = sign * seps[base + self.keep]
        self.peer_shift = -sign * seps[base + self.give]
        self.own_time = src * slices + self.mom
        late = jnp.where(self.forward, 0, self.shift)
        self.pair_time = lax.rem(self.own_time + late + self.time_count, self.time_count)
        self.live = self.forward if offsets == 1 else None

    def _sum(self, place, amount):
        return lax.rem(place + amount + self.time_count, self.time_count)

    def local(self, i):
        return lax.rem(self._sum(self.mom ^ i, self.shift), self.slices)

    def hops(self, i):
        return lax.div(self._sum(self.mom ^ i, self.shift), self.slices)

    def peer_local(self):
        return lax.rem(self._sum(self.mom, self.peer_shift), self.slices)

    def peer_hops(self):
        return lax.div(self._sum(self.mom, self.peer_shift), self.slices)


def run_copies(copies, sems):
    handles = [
        pltpu.make_async_copy(source, target, sems.at[n])
        for n, (source, target) in enumerate(copies)
    ]
    for handle in handles:
        handle.start()
    for handle in handles:
        handle.wait()


def span(index, rows):
    return pl.ds(index * rows, rows)


def through(parts, ins, leaving):
    started, n = [], 0
    for copies, buffer, target in parts:
        group = []
        for source, spot in copies:
            group.append(pltpu.make_async_copy(source, spot, ins.at[n]))
            group[-1].start()
            n += 1
        started.append(group)
    handles = []
    for n, (group, (_, buffer, target)) in enumerate(zip(started, parts)):
        for handle in group:
            handle.wait()
        handles.append(pltpu.make_async_copy(buffer, target, leaving.at[n]))
        handles[-1].start()
    for handle in handles:
        handle.wait()


def two_slices(proj, buffer, first, second):
    rows = proj.shape[1]
    return [(proj.at[n], buffer.at[span(i, rows)]) for i, n in enumerate((first, second))]


def tag_of(partner, lanes):
    number = jnp.full((TAG_ROWS, lanes), partner[0].astype(jnp.float32))
    return number.astype(jnp.bfloat16)


def pack_first(sizes, seps, partner, peram, *refs):
    outs, token, buffers, (ins, leaving) = refs[:2], refs[2], refs[3:5], refs[5:]
    plan = Plan(seps, sizes)
    start, parts = 0, []
    for out, buffer in zip(outs, buffers):
        chunk = buffer.shape[1] // 2
        for plane in range(2):
            for n in range(2):
                rows = pl.ds(n * chunk, chunk)
                source = peram.at[plan.peer_local(), plan.give, plane, pl.ds(start + n * chunk, chunk)]
                spot = buffer.at[plane, rows]
                parts.append(([(source, spot)], spot, out.at[plane, rows]))
        start += buffer.shape[1]
    token[...] = tag_of(partner, token.shape[-1])
    through(parts, ins, leaving)


def pack(sizes, seps, partner, proj, tick, after, *refs):
    outs, buffers, (ins, leaving) = refs[:2], refs[2:4], refs[4:]
    plan = Plan(seps, sizes)
    rows = proj.shape[1]
    same, cross = buffers
    cross[pl.ds(2 * rows, TAG_ROWS), :] = tag_of(partner, cross.shape[-1])
    cross[pl.ds(2 * rows + TAG_ROWS, TAG_ROWS), :] = tick[...]
    copies = [
        two_slices(proj, same, plan.local(0), plan.local(1)),
        two_slices(proj, cross, plan.local(2), plan.local(3)),
    ]
    through(list(zip(copies, buffers, outs)), ins, leaving)


def choose(sizes, seps, near, far, after, out, sems):
    flag = lax.rem(Plan(seps, sizes).peer_hops(), 2)

    @pl.when(flag == 0)
    def _():
        run_copies([(near, out)], sems)

    @pl.when(flag != 0)
    def _():
        run_copies([(far, out)], sems)


def gate(first, rest, after, first_out, rest_out, token):
    token[...] = jnp.zeros(token.shape, token.dtype)


def gate_one(after, array, array_out, token):
    token[...] = after[...]


def gate_far(after, same, cross, same_out, cross_out, token):
    token[...] = after[...]


def own_fill(codes, p_ref, n, u_ref, turns):
    nev = turns.shape[-1]
    width = u_ref.shape[0]
    for r in range(len(codes)):
        real, imag = (p_ref[n, m * nev : (m + 1) * nev].T for m in (2 * r, 2 * r + 1))
        set_turns(turns, r, real, imag)
    u_ref[...] = jnp.zeros(u_ref.shape, u_ref.dtype)

    def write(spin, column, a, b):
        add_to(u_ref, along(column, nev), along(spin, nev), a)
        add_to(u_ref, along(column, nev), along(spin, nev, width), b)

    fill_spin_blocks(codes, turns, write)


def own_dot(u_ref, y_ref, ht):
    width = u_ref.shape[0]
    for tile in range(2 * width // TILE):
        start = tile * TILE
        out = lax.dot_general(
            u_ref[...], y_ref[start : start + TILE, :], NT_DIMS, preferred_element_type=jnp.float32
        ).astype(jnp.bfloat16)
        if start < width:
            ht[:, width + start : width + start + TILE] = out
        else:
            ht[:, start - width : start - width + TILE] = out
            ht[:, width + start : width + start + TILE] = -out


def codes_of(gamma, op, nterm):
    return [gamma[op, r] for r in range(nterm)]


def own_kernel_0(sizes, seps, gamma, peram, proj, y_ref, ht, token, x_ref, p_ref, u_ref, turns, sems):
    plan = Plan(seps, sizes)
    mom = plan.mom
    run_copies([(peram.at[mom, plan.keep], x_ref), (proj.at[mom], p_ref.at[0])], sems)
    width = x_ref.shape[-1]
    real, imag = x_ref[0], x_ref[1]
    y_ref[:width, :width] = real
    y_ref[:width, width:] = -imag
    y_ref[width:, :width] = imag
    y_ref[width:, width:] = real
    own_fill(codes_of(gamma, mom, turns.shape[0]), p_ref, 0, u_ref, turns)
    own_dot(u_ref, y_ref, ht)
    token[...] = jnp.zeros(token.shape, token.dtype)


def own_kernel(piece, gamma, source, y_ref, after, ht, token, p_ref, u_ref, turns, sems):
    mom = lax.axis_index("mom")
    run_copies([(source.at[mom], p_ref.at[0])], sems)
    own_fill(codes_of(gamma, mom ^ piece, turns.shape[0]), p_ref, 0, u_ref, turns)
    own_dot(u_ref, y_ref, ht)
    token[...] = jnp.zeros(token.shape, token.dtype)


def find_labels(plan, partner, tick, tags, label):
    mom = plan.mom

    def number(tag):
        return jnp.max(tag.astype(jnp.float32)).astype(jnp.int32)

    partners = [partner[0], number(tick[...]), number(tags[:TAG_ROWS]), number(tags[TAG_ROWS:])]
    count = len(partners)
    for p in range(count):
        back = jnp.int32(0)
        for i, value in enumerate(partners):
            back = back + jnp.where(value == (mom ^ p), mom ^ i, 0)
        label[p] = jnp.where(plan.forward, back, mom ^ p)
        label[count + p] = jnp.where(plan.forward, back, partners[p]) ^ mom


def other_products(pieces, gamma, label, products, sources, refs, before=None):
    k_ref, p_ref, hs, wa, wb, turns_a, turns_b, sems = refs
    mom = lax.axis_index("mom")
    nterm, nev = turns_a.shape[0], turns_a.shape[-1]
    width = wa.shape[0]
    (here, away), flag = sources
    for n in range(2):
        for wanted, refs_now in ((0, here), (1, away)):

            @pl.when(flag == wanted)
            def _():
                pltpu.make_async_copy(refs_now[n], p_ref.at[n], sems.at[n]).start()

    if before is not None:
        before()
    for n, piece in enumerate(pieces):
        for own, source in enumerate(products):

            @pl.when(label[4 + piece] == own)
            def _():
                pltpu.make_async_copy(source, hs.at[n], sems.at[2 + n]).start()

    pairs = ((wa, turns_a), (wb, turns_b))

    def fill(n):
        w_ref, turns = pairs[n]
        codes = codes_of(gamma, mom ^ pieces[n], nterm)

        def write(spin, column, a, b):
            add_to(w_ref, along(spin, nev), along(column, nev), a)
            add_to(w_ref, along(spin, nev), along(column, nev, width), b)

        def step(r):
            rows = slice(r * nev, (r + 1) * nev)
            w_ref[rows, :] = jnp.zeros((nev, w_ref.shape[1]), w_ref.dtype)
            real, imag = (p_ref[n, m * nev : (m + 1) * nev] for m in (2 * r, 2 * r + 1))
            set_turns(turns, r, real, imag)

        def term(r):
            fill_term(codes, turns, write, r)

        return [functools.partial(f, r) for f in (step, term) for r in range(nterm)]

    def dots(n):
        def dot(start, half):
            lanes = slice(start, start + TILE)
            left = slice(width, 3 * width) if half == 0 else slice(0, 2 * width)
            rows = slice(half * width, (half + 1) * width)
            k_ref[n, rows, lanes] = lax.dot_general(
                hs[n, :, left], pairs[n][0][lanes, :], NT_DIMS, preferred_element_type=jnp.float32
            )

        return [functools.partial(dot, tile, half) for tile in range(0, width, TILE) for half in (0, 1)]

    for n in range(2):
        pltpu.make_async_copy(away[n], p_ref.at[n], sems.at[n]).wait()
    for step in fill(0):
        step()
    pltpu.make_async_copy(products[0], hs.at[0], sems.at[2]).wait()
    ahead = fill(1)
    for n, dot in enumerate(dots(0)):
        for step in ahead[2 * n : 2 * n + 2]:
            step()
        dot()
    pltpu.make_async_copy(products[0], hs.at[1], sems.at[3]).wait()
    for dot in dots(1):
        dot()


def other_flag(plan, sizes):
    return lax.rem(plan.hops(0), 2) if sizes[2] == 2 else jnp.int32(1)


def other_kernel_02(sizes, seps, gamma, partner, tick, h0, h1, h2, h3, proj, near, same, cross, *refs):
    k_ref, label, tags, sems, refs = refs[0], refs[1], refs[2], refs[3], (refs[0],) + refs[4:]
    plan = Plan(seps, sizes)
    rows = proj.shape[1]
    low, at = span(0, rows), plan.local(0)
    sources = (((proj.at[at], near.at[at]), (same.at[low], cross.at[low])), other_flag(plan, sizes))

    def before():
        run_copies([(cross.at[pl.ds(2 * rows, 2 * TAG_ROWS)], tags)], sems)
        find_labels(plan, partner, tick, tags, label)

    other_products((0, 2), gamma, label, (h0, h1, h2, h3), sources, refs, before)


def other_kernel_13(sizes, seps, gamma, label, h0, h1, h2, h3, core, near, same, cross, *refs):
    plan = Plan(seps, sizes)
    rows = core.shape[1]
    away, at = span(1 if sizes[2] == 2 else 0, rows), plan.local(0)
    sources = (((core.at[at], near.at[at]), (same.at[away], cross.at[away])), other_flag(plan, sizes))
    other_products((1, 3), gamma, label, (h0, h1, h2, h3), sources, refs)


def row_sums(k_refs, source, offset, totals):
    rows = 16
    width = source.shape[-1]
    nev = totals[0].shape[-1]

    def step(index, totals):
        row = pl.multiple_of(index * rows, rows)
        here = pl.ds(pl.multiple_of(offset + row, rows), rows)
        later = pl.ds(pl.multiple_of(width + offset + row, rows), rows)
        totals = list(totals)
        for spin in range(NSPIN):
            lanes = along(spin, nev)
            real = source[0, pl.ds(row, rows), lanes].astype(jnp.float32)
            imag = source[1, pl.ds(row, rows), lanes].astype(jnp.float32)
            for n in range(len(totals) // 2):
                k_ref, p = k_refs[n // 2], n % 2
                kr, ki = k_ref[p, here, lanes], k_ref[p, later, lanes]
                totals[2 * n] += real * kr - imag * ki
                totals[2 * n + 1] += real * ki + imag * kr
        return tuple(totals)

    return lax.fori_loop(0, source.shape[1] // rows, step, totals)


def trace_kernel(sizes, sep_count, seps, label, ka, kb, near, far, rest, out_ref, first_buf, rest_buf, sems):
    plan = Plan(seps, sizes)
    count = 2 * ka.shape[0]
    width = rest_buf.shape[-1]
    nev = width // NSPIN
    flag = lax.rem(lax.div(plan.hops(0), max(sizes[2] // 2, 1)), 2)
    later = pltpu.make_async_copy(rest, rest_buf, sems.at[1])
    chunk = first_buf.shape[1] // 2
    parts = [pl.ds(n * chunk, chunk) for n in range(2)]
    for wanted, source in ((0, near), (1, far)):

        @pl.when(flag == wanted)
        def _():
            for n, rows in enumerate(parts):
                pltpu.make_async_copy(
                    source.at[:, rows], first_buf.at[:, rows], sems.at[2 * n]
                ).start()

    later.start()
    totals = tuple(jnp.zeros((16, nev), jnp.float32) for _ in range(2 * count))
    for n, rows in enumerate(parts):
        pltpu.make_async_copy(far.at[:, rows], first_buf.at[:, rows], sems.at[2 * n]).wait()
        totals = row_sums((ka, kb), first_buf.at[:, rows], n * chunk, totals)
    later.wait()
    totals = row_sums((ka, kb), rest_buf, first_buf.shape[1], totals)
    sums = [jnp.sum(total, axis=0, keepdims=True) for total in totals]
    sums = [jnp.sum(total, axis=1, keepdims=True) * (1.0 / width) for total in sums]
    shape = out_ref.shape[1:]
    spot = lax.broadcasted_iota(jnp.int32, shape, 0) * shape[1]
    spot = spot + lax.broadcasted_iota(jnp.int32, shape, 1)
    here = spot // 2 == plan.pair_time * sep_count + plan.sep_index
    if plan.live is not None:
        here = here & plan.live
    values = [jnp.where(spot % 2 == 0, sums[2 * p], sums[2 * p + 1]) for p in range(count)]
    lines = []
    for op in range(count):
        line = jnp.zeros(shape, jnp.float32)
        for p, value in zip((0, 2, 1, 3), values):
            line = jnp.where(label[p] == op, value, line)
        lines.append(jnp.where(here, line, 0.0))
    for n in range(out_ref.shape[0]):
        out_ref[n] = lines[n % count]


def smem():
    return pl.BlockSpec(memory_space=pltpu.SMEM)


def vmem():
    return pl.BlockSpec(memory_space=pltpu.VMEM)


def anywhere():
    return pl.BlockSpec(memory_space=pl.ANY)


def hbm():
    return pl.BlockSpec(memory_space=pltpu.HBM)


def limit(mib):
    return pltpu.CompilerParams(vmem_limit_bytes=mib * MIB)


def shards(peram_blocks, projections, gamma_index, partner, separations):
    src_count, snk_count = lax.axis_size("src"), lax.axis_size("snk")
    mom_count = lax.axis_size("mom")
    slices, offsets = peram_blocks.shape[:2]
    width = peram_blocks.shape[-1]
    nterm, nev = projections.shape[2], projections.shape[-1]
    time_count = slices * src_count
    sep_count = separations.shape[0]
    half_snk = snk_count // 2
    rows = nterm * 2 * nev
    sizes = (slices, offsets, src_count, snk_count)
    proj = projections.reshape(slices, rows, nev)

    def swap_mom(array, i):
        return lax.ppermute(array, "mom", [(a, a ^ i) for a in range(mom_count)])

    def swap_snk(array):
        pairs = [(a, (a + half_snk) % snk_count) for a in range(snk_count)]
        return lax.ppermute(array, "snk", pairs)

    def next_src(array, step=1, i=0):
        pairs = [
            (((a + step) % src_count) * mom_count + (b ^ i), a * mom_count + b)
            for a in range(src_count)
            for b in range(mom_count)
        ]
        return lax.ppermute(array, ("src", "mom"), pairs)

    def most_of(array, amount):
        step = 1
        while 2 * step < src_count:
            array = jnp.where((amount // step) % 2 != 0, next_src(array, step), array)
            step *= 2
        return array, next_src(array, step)

    def call(kernel, name, in_specs, out_specs, out_shape, scratch, mib, aliases=None):
        cost = pl.CostEstimate(flops=WEIGHT, bytes_accessed=WEIGHT // 1000, transcendentals=0)
        return pl.pallas_call(
            kernel,
            in_specs=in_specs,
            out_specs=out_specs,
            out_shape=out_shape,
            scratch_shapes=scratch,
            input_output_aliases=aliases or {},
            compiler_params=limit(mib),
            cost_estimate=cost,
            name=name,
        )

    def bf16(*shape):
        return jax.ShapeDtypeStruct(shape, jnp.bfloat16)

    def dma(count):
        return pltpu.SemaphoreType.DMA((count,))

    part = functools.partial
    split = (width * 5 // 8) // 16 * 16
    two = bf16(2 * rows, nev)
    tagged = bf16(2 * rows + TAG_ROWS, nev)
    first_shape, rest_shape = bf16(2, split, width), bf16(2, width - split, width)
    token = bf16(16, 128)

    def buffers(shapes):
        return [pltpu.VMEM(shape.shape, shape.dtype) for shape in shapes]

    def alias(kernel, name, in_specs, out_shape, aliases, operands):
        return pl.pallas_call(
            kernel,
            in_specs=in_specs,
            out_specs=[anywhere()] * len(aliases) + [vmem()],
            out_shape=out_shape,
            input_output_aliases=aliases,
            compiler_params=limit(20),
            cost_estimate=pl.CostEstimate(
                flops=WEIGHT, bytes_accessed=WEIGHT // 1000, transcendentals=0
            ),
            name=name,
        )(*operands)

    leaving = [first_shape, rest_shape]
    first, rest, tick = call(
        part(pack_first, sizes),
        "pack_first",
        [smem()] * 2 + [hbm()],
        [hbm()] * 2 + [vmem()],
        leaving + [token],
        buffers(leaving) + [dma(8), dma(8)],
        58,
    )(separations, partner, peram_blocks)

    plan = Plan(separations, sizes)
    near = swap_mom(proj, 2)
    core = swap_mom(proj, 1)
    first = swap_snk(first)
    rest_near, rest_far = most_of(rest, plan.peer_hops())
    tick = swap_mom(tick, 1)
    u_scratch = pltpu.VMEM((width, 2 * width), jnp.bfloat16)
    turns = pltpu.VMEM((nterm, 4, nev, nev), jnp.bfloat16)
    piece = pltpu.VMEM((1, rows, nev), jnp.bfloat16)
    pieces = pltpu.VMEM((2, rows, nev), jnp.bfloat16)
    product = bf16(width, 3 * width)
    y, h0, done_0 = call(
        part(own_kernel_0, sizes),
        "own_products_0",
        [smem()] * 2 + [hbm()] * 2,
        [vmem()] * 3,
        [bf16(2 * width, 2 * width), product, token],
        [pltpu.VMEM((2, width, width), jnp.bfloat16), piece, u_scratch, turns, dma(2)],
        58,
    )(separations, gamma_index, peram_blocks, proj)
    leaving = [two, bf16(2 * (rows + TAG_ROWS), nev)]
    far_same, far_cross = call(
        part(pack, sizes),
        "pack",
        [smem()] * 2 + [hbm(), vmem(), vmem()],
        [hbm()] * 2,
        leaving,
        buffers(leaving) + [dma(4), dma(2)],
        58,
    )(separations, partner, proj, tick, done_0)
    if src_count == 2:
        far_same, far_cross = next_src(far_same), next_src(far_cross, 1, 2)
    else:
        far_cross = swap_mom(far_cross, 2)
    def own_one(number, source, after):
        return call(
            part(own_kernel, number),
            "own_products_%d" % number,
            [smem(), hbm(), vmem(), vmem()],
            [vmem()] * 2,
            [product, token],
            [piece, u_scratch, turns, dma(1)],
            20,
        )(gamma_index, source, y, after)

    h1, done_1 = own_one(1, core, done_0)
    near, _ = alias(
        gate_one,
        "gate_near",
        [vmem(), anywhere()],
        [bf16(*proj.shape), token],
        {1: 0},
        (done_1, near),
    )
    near_core = swap_mom(near, 1)

    if src_count > 2:
        rest_near = jnp.where(plan.peer_hops() // (src_count // 2) != 0, rest_far, rest_near)
        rest_far = rest_near
    rest = call(
        part(choose, sizes),
        "choose",
        [smem()] + [hbm()] * 2 + [vmem()],
        vmem(),
        rest_shape,
        [dma(1)],
        20,
    )(separations, rest_near, rest_far, done_1)
    h2, done_2 = own_one(2, near, done_1)
    first, rest, opened = alias(
        gate,
        "gate",
        [anywhere()] * 2 + [vmem()],
        [first_shape, rest_shape, token],
        {0: 0, 1: 1},
        (first, rest, done_2),
    )
    rest = swap_snk(rest)
    first_near, first_far = most_of(first, plan.hops(0))
    h3, done_3 = own_one(3, near_core, opened)
    far_same, far_cross, _ = alias(
        gate_far,
        "gate_far",
        [vmem()] + [anywhere()] * 2,
        [two, bf16(2 * (rows + TAG_ROWS), nev), token],
        {1: 0, 2: 1},
        (done_3, far_same, far_cross),
    )
    if src_count == 2:
        far = [far_same, far_cross, swap_mom(far_same, 1), swap_mom(far_cross, 1)]
    else:

        def moved(array):
            array = lax.dynamic_index_in_dim(array, plan.local(0), 0, keepdims=False)
            if src_count == 1:
                return array
            array, away = most_of(array, plan.hops(0))
            return jnp.where(plan.hops(0) // (src_count // 2) != 0, away, array)

        far = [moved(array) for array in (proj, near, core, near_core)]
        far[1] = jnp.concatenate([far[1], far[1], far_cross[2 * rows :]])

    k_shape = jax.ShapeDtypeStruct((2, 2 * width, width), jnp.float32)
    scratch = [pieces, pltpu.VMEM((2, width, 3 * width), jnp.bfloat16)]
    scratch += [u_scratch, u_scratch, turns, turns, dma(4)]
    ka, label = call(
        part(other_kernel_02, sizes),
        "other_products_02",
        [smem()] * 3 + [vmem()] + [hbm()] * 8,
        [vmem(), smem()],
        [k_shape, jax.ShapeDtypeStruct((2 * mom_count,), jnp.int32)],
        [pltpu.VMEM((2 * TAG_ROWS, nev), jnp.bfloat16), dma(1)] + scratch,
        20,
    )(
        separations, gamma_index, partner, tick, h0, h1, h2, h3, proj, near, far[0], far[1],
    )
    kb = call(
        part(other_kernel_13, sizes),
        "other_products_13",
        [smem()] * 3 + [hbm()] * 8,
        vmem(),
        k_shape,
        scratch,
        20,
    )(separations, gamma_index, label, h0, h1, h2, h3, core, near_core, far[2], far[3])

    device_count = src_count * snk_count * mom_count
    values = time_count * sep_count * 2
    lines = (values + 127) // 128
    out = call(
        part(trace_kernel, sizes, sep_count),
        "traces",
        [smem()] * 2 + [vmem()] * 2 + [hbm()] * 3,
        vmem(),
        jax.ShapeDtypeStruct((device_count, lines, 128), jnp.float32),
        buffers([first_shape, rest_shape]) + [dma(3)],
        20,
    )(separations, label, ka, kb, first_near, first_far, rest)
    out = lax.all_to_all(out, ("src", "snk", "mom"), split_axis=0, concat_axis=0, tiled=True)
    out = jnp.sum(out, axis=0).reshape(lines * 128)[:values]
    return out.reshape(time_count, sep_count, 1, 2)


def solution(mesh):
    placed = (
        P("src", "snk", None, None, None),
        P("src", "mom", None, None, None, None),
        P(),
        P("mom"),
        P(),
    )
    return jax.shard_map(
        shards, mesh=mesh, in_specs=placed, out_specs=P(None, None, "mom", None), check_vma=False
    )
```

```python
import functools

import jax
import jax.numpy as jnp
from jax import lax
from jax.experimental import pallas as pl
from jax.experimental.pallas import tpu as pltpu
from jax.sharding import PartitionSpec as P

NSPIN = 4
NT_DIMS = (((1,), (1,)), ((), ()))
MIB = 1024 * 1024
WEIGHT = 10**13
TAG_ROWS = 16
TILE = 256
GAMMAS = (
    (3, 1 | 1 << 2 | 3 << 4 | 3 << 6),
    (3, 2 | 0 << 2 | 0 << 4 | 2 << 6),
    (2, 1 | 3 << 2 | 3 << 4 | 1 << 6),
    (2, 0),
)


def spin_entry(code, row):
    phase = row * 0
    for bit, (flip, phases) in enumerate(GAMMAS):
        on = (code >> bit) & 1
        phase = phase + on * ((phases >> (2 * row)) & 3)
        row = row ^ (on * flip)
    return row, phase & 3


def fill_spin_blocks(codes, turns, write):
    for r in range(len(codes)):
        fill_term(codes, turns, write, r)


def fill_term(codes, turns, write, r):
    for spin in range(NSPIN):
        column, phase = spin_entry(codes[r], spin)
        write(spin, column, *(turns[r, (n - phase) & 3] for n in (4, 1)))


def set_turns(turns, r, real, imag):
    for n, value in enumerate((real, imag, -real, -imag)):
        turns[r, n] = value


def add_to(ref, rows, lanes, value):
    ref[rows, lanes] = ref[rows, lanes] + value


def along(spin, nev, start=0):
    if isinstance(spin, int):
        return slice(start + spin * nev, start + (spin + 1) * nev)
    return pl.ds(pl.multiple_of(start + spin * nev, nev), nev)


class Plan:
    def __init__(self, seps, sizes):
        slices, offsets, src_count, snk_count = sizes
        src, snk, self.mom = (lax.axis_index(name) for name in ("src", "snk", "mom"))
        half_snk = snk_count // 2
        self.slices, self.time_count = slices, slices * src_count
        self.forward = snk < half_snk
        base = lax.rem(snk, half_snk) * offsets
        self.keep = jnp.where(self.forward, 0, offsets - 1)
        self.give = offsets - 1 - self.keep
        self.sep_index = base + self.keep
        sign = jnp.where(self.forward, 1, -1)
        self.shift = sign * seps[base + self.keep]
        self.peer_shift = -sign * seps[base + self.give]
        self.own_time = src * slices + self.mom
        late = jnp.where(self.forward, 0, self.shift)
        self.pair_time = lax.rem(self.own_time + late + self.time_count, self.time_count)
        self.live = self.forward if offsets == 1 else None

    def _sum(self, place, amount):
        return lax.rem(place + amount + self.time_count, self.time_count)

    def local(self, i):
        return lax.rem(self._sum(self.mom ^ i, self.shift), self.slices)

    def hops(self, i):
        return lax.div(self._sum(self.mom ^ i, self.shift), self.slices)

    def peer_local(self):
        return lax.rem(self._sum(self.mom, self.peer_shift), self.slices)

    def peer_hops(self):
        return lax.div(self._sum(self.mom, self.peer_shift), self.slices)


def run_copies(copies, sems):
    handles = [
        pltpu.make_async_copy(source, target, sems.at[n])
        for n, (source, target) in enumerate(copies)
    ]
    for handle in handles:
        handle.start()
    for handle in handles:
        handle.wait()


def span(index, rows):
    return pl.ds(index * rows, rows)


def through(parts, ins, leaving):
    started, n = [], 0
    for copies, buffer, target in parts:
        group = []
        for source, spot in copies:
            group.append(pltpu.make_async_copy(source, spot, ins.at[n]))
            group[-1].start()
            n += 1
        started.append(group)
    handles = []
    for n, (group, (_, buffer, target)) in enumerate(zip(started, parts)):
        for handle in group:
            handle.wait()
        handles.append(pltpu.make_async_copy(buffer, target, leaving.at[n]))
        handles[-1].start()
    for handle in handles:
        handle.wait()


def two_slices(proj, buffer, first, second):
    rows = proj.shape[1]
    return [(proj.at[n], buffer.at[span(i, rows)]) for i, n in enumerate((first, second))]


def tag_of(partner, lanes):
    number = jnp.full((TAG_ROWS, lanes), partner[0].astype(jnp.float32))
    return number.astype(jnp.bfloat16)


def pack_first(sizes, seps, partner, peram, *refs):
    outs, token, buffers, (ins, leaving) = refs[:2], refs[2], refs[3:5], refs[5:]
    plan = Plan(seps, sizes)
    start, copies = 0, []
    for buffer in buffers:
        rows = buffer.shape[1]
        source = peram.at[plan.peer_local(), plan.give, :, pl.ds(start, rows)]
        copies.append([(source, buffer)])
        start += rows
    token[...] = tag_of(partner, token.shape[-1])
    through(list(zip(copies, buffers, outs)), ins, leaving)


def pack(sizes, seps, partner, proj, tick, after, *refs):
    outs, buffers, (ins, leaving) = refs[:2], refs[2:4], refs[4:]
    plan = Plan(seps, sizes)
    rows = proj.shape[1]
    same, cross = buffers
    cross[pl.ds(2 * rows, TAG_ROWS), :] = tag_of(partner, cross.shape[-1])
    cross[pl.ds(2 * rows + TAG_ROWS, TAG_ROWS), :] = tick[...]
    copies = [
        two_slices(proj, same, plan.local(0), plan.local(1)),
        two_slices(proj, cross, plan.local(2), plan.local(3)),
    ]
    through(list(zip(copies, buffers, outs)), ins, leaving)


def choose(sizes, seps, near, far, after, out, sems):
    flag = lax.rem(Plan(seps, sizes).peer_hops(), 2)

    @pl.when(flag == 0)
    def _():
        run_copies([(near, out)], sems)

    @pl.when(flag != 0)
    def _():
        run_copies([(far, out)], sems)


def gate(first, rest, after, first_out, rest_out, token):
    token[...] = jnp.zeros(token.shape, token.dtype)


def gate_one(after, array, array_out, token):
    token[...] = after[...]


def gate_far(after, same, cross, same_out, cross_out, token):
    token[...] = after[...]


def own_fill(codes, p_ref, n, u_ref, turns):
    nev = turns.shape[-1]
    width = u_ref.shape[0]
    for r in range(len(codes)):
        real, imag = (p_ref[n, m * nev : (m + 1) * nev].T for m in (2 * r, 2 * r + 1))
        set_turns(turns, r, real, imag)
    u_ref[...] = jnp.zeros(u_ref.shape, u_ref.dtype)

    def write(spin, column, a, b):
        add_to(u_ref, along(column, nev), along(spin, nev), a)
        add_to(u_ref, along(column, nev), along(spin, nev, width), b)

    fill_spin_blocks(codes, turns, write)


def own_dot(u_ref, y_ref, ht):
    width = u_ref.shape[0]
    for tile in range(2 * width // TILE):
        start = tile * TILE
        out = lax.dot_general(
            u_ref[...], y_ref[start : start + TILE, :], NT_DIMS, preferred_element_type=jnp.float32
        ).astype(jnp.bfloat16)
        if start < width:
            ht[:, width + start : width + start + TILE] = out
        else:
            ht[:, start - width : start - width + TILE] = out
            ht[:, width + start : width + start + TILE] = -out


def codes_of(gamma, op, nterm):
    return [gamma[op, r] for r in range(nterm)]


def own_kernel_0(sizes, seps, gamma, peram, proj, y_ref, ht, token, x_ref, p_ref, u_ref, turns, sems):
    plan = Plan(seps, sizes)
    mom = plan.mom
    run_copies([(peram.at[mom, plan.keep], x_ref), (proj.at[mom], p_ref.at[0])], sems)
    width = x_ref.shape[-1]
    real, imag = x_ref[0], x_ref[1]
    y_ref[:width, :width] = real
    y_ref[:width, width:] = -imag
    y_ref[width:, :width] = imag
    y_ref[width:, width:] = real
    own_fill(codes_of(gamma, mom, turns.shape[0]), p_ref, 0, u_ref, turns)
    own_dot(u_ref, y_ref, ht)
    token[...] = jnp.zeros(token.shape, token.dtype)


def own_kernel(piece, gamma, source, y_ref, after, ht, token, p_ref, u_ref, turns, sems):
    mom = lax.axis_index("mom")
    run_copies([(source.at[mom], p_ref.at[0])], sems)
    own_fill(codes_of(gamma, mom ^ piece, turns.shape[0]), p_ref, 0, u_ref, turns)
    own_dot(u_ref, y_ref, ht)
    token[...] = jnp.zeros(token.shape, token.dtype)


def find_labels(plan, partner, tick, tags, label):
    mom = plan.mom

    def number(tag):
        return jnp.max(tag.astype(jnp.float32)).astype(jnp.int32)

    partners = [partner[0], number(tick[...]), number(tags[:TAG_ROWS]), number(tags[TAG_ROWS:])]
    count = len(partners)
    for p in range(count):
        back = jnp.int32(0)
        for i, value in enumerate(partners):
            back = back + jnp.where(value == (mom ^ p), mom ^ i, 0)
        label[p] = jnp.where(plan.forward, back, mom ^ p)
        label[count + p] = jnp.where(plan.forward, back, partners[p]) ^ mom


def other_products(pieces, gamma, label, products, sources, refs, before=None):
    k_ref, p_ref, hs, wa, wb, turns_a, turns_b, sems = refs
    mom = lax.axis_index("mom")
    nterm, nev = turns_a.shape[0], turns_a.shape[-1]
    width = wa.shape[0]
    (here, away), flag = sources
    for n in range(2):
        for wanted, refs_now in ((0, here), (1, away)):

            @pl.when(flag == wanted)
            def _():
                pltpu.make_async_copy(refs_now[n], p_ref.at[n], sems.at[n]).start()

    if before is not None:
        before()
    for n, piece in enumerate(pieces):
        for own, source in enumerate(products):

            @pl.when(label[4 + piece] == own)
            def _():
                pltpu.make_async_copy(source, hs.at[n], sems.at[2 + n]).start()

    pairs = ((wa, turns_a), (wb, turns_b))

    def fill(n):
        w_ref, turns = pairs[n]
        codes = codes_of(gamma, mom ^ pieces[n], nterm)

        def write(spin, column, a, b):
            add_to(w_ref, along(spin, nev), along(column, nev), a)
            add_to(w_ref, along(spin, nev), along(column, nev, width), b)

        def step(r):
            rows = slice(r * nev, (r + 1) * nev)
            w_ref[rows, :] = jnp.zeros((nev, w_ref.shape[1]), w_ref.dtype)
            real, imag = (p_ref[n, m * nev : (m + 1) * nev] for m in (2 * r, 2 * r + 1))
            set_turns(turns, r, real, imag)

        def term(r):
            fill_term(codes, turns, write, r)

        return [functools.partial(f, r) for f in (step, term) for r in range(nterm)]

    def dots(n):
        def dot(start, half):
            lanes = slice(start, start + TILE)
            left = slice(width, 3 * width) if half == 0 else slice(0, 2 * width)
            rows = slice(half * width, (half + 1) * width)
            k_ref[n, rows, lanes] = lax.dot_general(
                hs[n, :, left], pairs[n][0][lanes, :], NT_DIMS, preferred_element_type=jnp.float32
            )

        return [functools.partial(dot, tile, half) for tile in range(0, width, TILE) for half in (0, 1)]

    for n in range(2):
        pltpu.make_async_copy(away[n], p_ref.at[n], sems.at[n]).wait()
    for step in fill(0):
        step()
    for n in range(2):
        pltpu.make_async_copy(products[0], hs.at[n], sems.at[2 + n]).wait()
    ahead = fill(1)
    for n, dot in enumerate(dots(0)):
        for step in ahead[2 * n : 2 * n + 2]:
            step()
        dot()
    for dot in dots(1):
        dot()


def other_flag(plan, sizes):
    return lax.rem(plan.hops(0), 2) if sizes[2] == 2 else jnp.int32(1)


def other_kernel_02(sizes, seps, gamma, partner, tick, h0, h1, h2, h3, proj, near, same, cross, *refs):
    k_ref, label, tags, sems, refs = refs[0], refs[1], refs[2], refs[3], (refs[0],) + refs[4:]
    plan = Plan(seps, sizes)
    rows = proj.shape[1]
    low, at = span(0, rows), plan.local(0)
    sources = (((proj.at[at], near.at[at]), (same.at[low], cross.at[low])), other_flag(plan, sizes))

    def before():
        run_copies([(cross.at[pl.ds(2 * rows, 2 * TAG_ROWS)], tags)], sems)
        find_labels(plan, partner, tick, tags, label)

    other_products((0, 2), gamma, label, (h0, h1, h2, h3), sources, refs, before)


def other_kernel_13(sizes, seps, gamma, label, h0, h1, h2, h3, core, near, same, cross, *refs):
    plan = Plan(seps, sizes)
    rows = core.shape[1]
    away, at = span(1 if sizes[2] == 2 else 0, rows), plan.local(0)
    sources = (((core.at[at], near.at[at]), (same.at[away], cross.at[away])), other_flag(plan, sizes))
    other_products((1, 3), gamma, label, (h0, h1, h2, h3), sources, refs)


def row_sums(k_refs, source, offset, totals):
    rows = 16
    width = source.shape[-1]
    nev = totals[0].shape[-1]

    def step(index, totals):
        row = pl.multiple_of(index * rows, rows)
        here = pl.ds(pl.multiple_of(offset + row, rows), rows)
        later = pl.ds(pl.multiple_of(width + offset + row, rows), rows)
        totals = list(totals)
        for spin in range(NSPIN):
            lanes = along(spin, nev)
            real = source[0, pl.ds(row, rows), lanes].astype(jnp.float32)
            imag = source[1, pl.ds(row, rows), lanes].astype(jnp.float32)
            for n in range(len(totals) // 2):
                k_ref, p = k_refs[n // 2], n % 2
                kr, ki = k_ref[p, here, lanes], k_ref[p, later, lanes]
                totals[2 * n] += real * kr - imag * ki
                totals[2 * n + 1] += real * ki + imag * kr
        return tuple(totals)

    return lax.fori_loop(0, source.shape[1] // rows, step, totals)


def trace_kernel(sizes, sep_count, rest, seps, label, ka, kb, near, far, out_ref, first_buf, rest_buf, sems):
    plan = Plan(seps, sizes)
    count = 2 * ka.shape[0]
    width = rest_buf.shape[-1]
    nev = width // NSPIN
    flag = lax.rem(lax.div(plan.hops(0), max(sizes[2] // 2, 1)), 2)
    later = pltpu.make_async_copy(rest, rest_buf, sems.at[1])
    chunk = first_buf.shape[1] // 2
    parts = [pl.ds(n * chunk, chunk) for n in range(2)]
    for wanted, source in ((0, near), (1, far)):

        @pl.when(flag == wanted)
        def _():
            for n, rows in enumerate(parts):
                pltpu.make_async_copy(
                    source.at[:, rows], first_buf.at[:, rows], sems.at[2 * n]
                ).start()

    later.start()
    totals = tuple(jnp.zeros((16, nev), jnp.float32) for _ in range(2 * count))
    for n, rows in enumerate(parts):
        pltpu.make_async_copy(far.at[:, rows], first_buf.at[:, rows], sems.at[2 * n]).wait()
        totals = row_sums((ka, kb), first_buf.at[:, rows], n * chunk, totals)
    later.wait()
    totals = row_sums((ka, kb), rest_buf, first_buf.shape[1], totals)
    sums = [jnp.sum(total, axis=0, keepdims=True) for total in totals]
    sums = [jnp.sum(total, axis=1, keepdims=True) * (1.0 / width) for total in sums]
    shape = out_ref.shape[1:]
    spot = lax.broadcasted_iota(jnp.int32, shape, 0) * shape[1]
    spot = spot + lax.broadcasted_iota(jnp.int32, shape, 1)
    here = spot // 2 == plan.pair_time * sep_count + plan.sep_index
    if plan.live is not None:
        here = here & plan.live
    values = [jnp.where(spot % 2 == 0, sums[2 * p], sums[2 * p + 1]) for p in range(count)]
    lines = []
    for op in range(count):
        line = jnp.zeros(shape, jnp.float32)
        for p, value in zip((0, 2, 1, 3), values):
            line = jnp.where(label[p] == op, value, line)
        lines.append(jnp.where(here, line, 0.0))
    for n in range(out_ref.shape[0]):
        out_ref[n] = lines[n % count]


def smem():
    return pl.BlockSpec(memory_space=pltpu.SMEM)


def vmem():
    return pl.BlockSpec(memory_space=pltpu.VMEM)


def anywhere():
    return pl.BlockSpec(memory_space=pl.ANY)


def hbm():
    return pl.BlockSpec(memory_space=pltpu.HBM)


def limit(mib):
    return pltpu.CompilerParams(vmem_limit_bytes=mib * MIB)


def shards(peram_blocks, projections, gamma_index, partner, separations):
    src_count, snk_count = lax.axis_size("src"), lax.axis_size("snk")
    mom_count = lax.axis_size("mom")
    slices, offsets = peram_blocks.shape[:2]
    width = peram_blocks.shape[-1]
    nterm, nev = projections.shape[2], projections.shape[-1]
    time_count = slices * src_count
    sep_count = separations.shape[0]
    half_snk = snk_count // 2
    rows = nterm * 2 * nev
    sizes = (slices, offsets, src_count, snk_count)
    proj = projections.reshape(slices, rows, nev)

    def swap_mom(array, i):
        return lax.ppermute(array, "mom", [(a, a ^ i) for a in range(mom_count)])

    def swap_snk(array):
        pairs = [(a, (a + half_snk) % snk_count) for a in range(snk_count)]
        return lax.ppermute(array, "snk", pairs)

    def next_src(array, step=1, i=0):
        pairs = [
            (((a + step) % src_count) * mom_count + (b ^ i), a * mom_count + b)
            for a in range(src_count)
            for b in range(mom_count)
        ]
        return lax.ppermute(array, ("src", "mom"), pairs)

    def most_of(array, amount):
        step = 1
        while 2 * step < src_count:
            array = jnp.where((amount // step) % 2 != 0, next_src(array, step), array)
            step *= 2
        return array, next_src(array, step)

    def call(kernel, name, in_specs, out_specs, out_shape, scratch, mib, aliases=None):
        cost = pl.CostEstimate(flops=WEIGHT, bytes_accessed=WEIGHT // 1000, transcendentals=0)
        return pl.pallas_call(
            kernel,
            in_specs=in_specs,
            out_specs=out_specs,
            out_shape=out_shape,
            scratch_shapes=scratch,
            input_output_aliases=aliases or {},
            compiler_params=limit(mib),
            cost_estimate=cost,
            name=name,
        )

    def bf16(*shape):
        return jax.ShapeDtypeStruct(shape, jnp.bfloat16)

    def dma(count):
        return pltpu.SemaphoreType.DMA((count,))

    part = functools.partial
    split = (width * 5 // 8) // 16 * 16
    two = bf16(2 * rows, nev)
    tagged = bf16(2 * rows + TAG_ROWS, nev)
    first_shape, rest_shape = bf16(2, split, width), bf16(2, width - split, width)
    token = bf16(16, 128)

    def buffers(shapes):
        return [pltpu.VMEM(shape.shape, shape.dtype) for shape in shapes]

    def alias(kernel, name, in_specs, out_shape, aliases, operands):
        return pl.pallas_call(
            kernel,
            in_specs=in_specs,
            out_specs=[anywhere()] * len(aliases) + [vmem()],
            out_shape=out_shape,
            input_output_aliases=aliases,
            compiler_params=limit(20),
            cost_estimate=pl.CostEstimate(
                flops=WEIGHT, bytes_accessed=WEIGHT // 1000, transcendentals=0
            ),
            name=name,
        )(*operands)

    leaving = [first_shape, rest_shape]
    first, rest, tick = call(
        part(pack_first, sizes),
        "pack_first",
        [smem()] * 2 + [hbm()],
        [hbm()] * 2 + [vmem()],
        leaving + [token],
        buffers(leaving) + [dma(2), dma(2)],
        58,
    )(separations, partner, peram_blocks)

    plan = Plan(separations, sizes)
    near = swap_mom(proj, 2)
    core = swap_mom(proj, 1)
    first = swap_snk(first)
    rest_near, rest_far = most_of(rest, plan.peer_hops())
    tick = swap_mom(tick, 1)
    u_scratch = pltpu.VMEM((width, 2 * width), jnp.bfloat16)
    turns = pltpu.VMEM((nterm, 4, nev, nev), jnp.bfloat16)
    piece = pltpu.VMEM((1, rows, nev), jnp.bfloat16)
    pieces = pltpu.VMEM((2, rows, nev), jnp.bfloat16)
    product = bf16(width, 3 * width)
    y, h0, done_0 = call(
        part(own_kernel_0, sizes),
        "own_products_0",
        [smem()] * 2 + [hbm()] * 2,
        [vmem()] * 3,
        [bf16(2 * width, 2 * width), product, token],
        [pltpu.VMEM((2, width, width), jnp.bfloat16), piece, u_scratch, turns, dma(2)],
        58,
    )(separations, gamma_index, peram_blocks, proj)
    leaving = [two, bf16(2 * (rows + TAG_ROWS), nev)]
    far_same, far_cross = call(
        part(pack, sizes),
        "pack",
        [smem()] * 2 + [hbm(), vmem(), vmem()],
        [hbm()] * 2,
        leaving,
        buffers(leaving) + [dma(4), dma(2)],
        58,
    )(separations, partner, proj, tick, done_0)
    if src_count == 2:
        far_same, far_cross = next_src(far_same), next_src(far_cross, 1, 2)
    else:
        far_cross = swap_mom(far_cross, 2)
    def own_one(number, source, after):
        return call(
            part(own_kernel, number),
            "own_products_%d" % number,
            [smem(), hbm(), vmem(), vmem()],
            [vmem()] * 2,
            [product, token],
            [piece, u_scratch, turns, dma(1)],
            20,
        )(gamma_index, source, y, after)

    h1, done_1 = own_one(1, core, done_0)
    near, _ = alias(
        gate_one,
        "gate_near",
        [vmem(), anywhere()],
        [bf16(*proj.shape), token],
        {1: 0},
        (done_1, near),
    )
    near_core = swap_mom(near, 1)

    if src_count > 2:
        rest_near = jnp.where(plan.peer_hops() // (src_count // 2) != 0, rest_far, rest_near)
        rest_far = rest_near
    rest = call(
        part(choose, sizes),
        "choose",
        [smem()] + [hbm()] * 2 + [vmem()],
        vmem(),
        rest_shape,
        [dma(1)],
        20,
    )(separations, rest_near, rest_far, done_1)
    h2, done_2 = own_one(2, near, done_1)
    first, rest, opened = alias(
        gate,
        "gate",
        [anywhere()] * 2 + [vmem()],
        [first_shape, rest_shape, token],
        {0: 0, 1: 1},
        (first, rest, done_2),
    )
    rest = swap_snk(rest)
    first_near, first_far = most_of(first, plan.hops(0))
    h3, done_3 = own_one(3, near_core, opened)
    far_same, far_cross, _ = alias(
        gate_far,
        "gate_far",
        [vmem()] + [anywhere()] * 2,
        [two, bf16(2 * (rows + TAG_ROWS), nev), token],
        {1: 0, 2: 1},
        (done_3, far_same, far_cross),
    )
    if src_count == 2:
        far = [far_same, far_cross, swap_mom(far_same, 1), swap_mom(far_cross, 1)]
    else:

        def moved(array):
            array = lax.dynamic_index_in_dim(array, plan.local(0), 0, keepdims=False)
            if src_count == 1:
                return array
            array, away = most_of(array, plan.hops(0))
            return jnp.where(plan.hops(0) // (src_count // 2) != 0, away, array)

        far = [moved(array) for array in (proj, near, core, near_core)]
        far[1] = jnp.concatenate([far[1], far[1], far_cross[2 * rows :]])

    k_shape = jax.ShapeDtypeStruct((2, 2 * width, width), jnp.float32)
    scratch = [pieces, pltpu.VMEM((2, width, 3 * width), jnp.bfloat16)]
    scratch += [u_scratch, u_scratch, turns, turns, dma(4)]
    ka, label = call(
        part(other_kernel_02, sizes),
        "other_products_02",
        [smem()] * 3 + [vmem()] + [hbm()] * 8,
        [vmem(), smem()],
        [k_shape, jax.ShapeDtypeStruct((2 * mom_count,), jnp.int32)],
        [pltpu.VMEM((2 * TAG_ROWS, nev), jnp.bfloat16), dma(1)] + scratch,
        20,
    )(
        separations, gamma_index, partner, tick, h0, h1, h2, h3, proj, near, far[0], far[1],
    )
    kb = call(
        part(other_kernel_13, sizes),
        "other_products_13",
        [smem()] * 3 + [hbm()] * 8,
        vmem(),
        k_shape,
        scratch,
        20,
    )(separations, gamma_index, label, h0, h1, h2, h3, core, near_core, far[2], far[3])

    device_count = src_count * snk_count * mom_count
    values = time_count * sep_count * 2
    lines = (values + 127) // 128
    out = call(
        part(trace_kernel, sizes, sep_count),
        "traces",
        [hbm()] + [smem()] * 2 + [vmem()] * 2 + [hbm()] * 2,
        vmem(),
        jax.ShapeDtypeStruct((device_count, lines, 128), jnp.float32),
        buffers([first_shape, rest_shape]) + [dma(3)],
        20,
    )(rest, separations, label, ka, kb, first_near, first_far)
    out = lax.all_to_all(out, ("src", "snk", "mom"), split_axis=0, concat_axis=0, tiled=True)
    out = jnp.sum(out, axis=0).reshape(lines * 128)[:values]
    return out.reshape(time_count, sep_count, 1, 2)


def solution(mesh):
    placed = (
        P("src", "snk", None, None, None),
        P("src", "mom", None, None, None, None),
        P(),
        P("mom"),
        P(),
    )
    return jax.shard_map(
        shards, mesh=mesh, in_specs=placed, out_specs=P(None, None, "mom", None), check_vma=False
    )
```

```python
import functools

import jax
import jax.numpy as jnp
from jax import lax
from jax.experimental import pallas as pl
from jax.experimental.pallas import tpu as pltpu
from jax.sharding import PartitionSpec as P

NSPIN = 4
NT_DIMS = (((1,), (1,)), ((), ()))
MIB = 1024 * 1024
WEIGHT = 10**13
TAG_ROWS = 16
TILE = 256
GAMMAS = (
    (3, 1 | 1 << 2 | 3 << 4 | 3 << 6),
    (3, 2 | 0 << 2 | 0 << 4 | 2 << 6),
    (2, 1 | 3 << 2 | 3 << 4 | 1 << 6),
    (2, 0),
)


def spin_entry(code, row):
    phase = row * 0
    for bit, (flip, phases) in enumerate(GAMMAS):
        on = (code >> bit) & 1
        phase = phase + on * ((phases >> (2 * row)) & 3)
        row = row ^ (on * flip)
    return row, phase & 3


def fill_spin_blocks(codes, turns, write):
    for r in range(len(codes)):
        fill_term(codes, turns, write, r)


def fill_term(codes, turns, write, r):
    for spin in range(NSPIN):
        column, phase = spin_entry(codes[r], spin)
        write(spin, column, *(turns[r, (n - phase) & 3] for n in (4, 1)))


def set_turns(turns, r, real, imag):
    for n, value in enumerate((real, imag, -real, -imag)):
        turns[r, n] = value


def add_to(ref, rows, lanes, value):
    ref[rows, lanes] = ref[rows, lanes] + value


def along(spin, nev, start=0):
    if isinstance(spin, int):
        return slice(start + spin * nev, start + (spin + 1) * nev)
    return pl.ds(pl.multiple_of(start + spin * nev, nev), nev)


class Plan:
    def __init__(self, seps, sizes):
        slices, offsets, src_count, snk_count = sizes
        src, snk, self.mom = (lax.axis_index(name) for name in ("src", "snk", "mom"))
        half_snk = snk_count // 2
        self.slices, self.time_count = slices, slices * src_count
        self.forward = snk < half_snk
        base = lax.rem(snk, half_snk) * offsets
        self.keep = jnp.where(self.forward, 0, offsets - 1)
        self.give = offsets - 1 - self.keep
        self.sep_index = base + self.keep
        sign = jnp.where(self.forward, 1, -1)
        self.shift = sign * seps[base + self.keep]
        self.peer_shift = -sign * seps[base + self.give]
        self.own_time = src * slices + self.mom
        late = jnp.where(self.forward, 0, self.shift)
        self.pair_time = lax.rem(self.own_time + late + self.time_count, self.time_count)
        self.live = self.forward if offsets == 1 else None

    def _sum(self, place, amount):
        return lax.rem(place + amount + self.time_count, self.time_count)

    def local(self, i):
        return lax.rem(self._sum(self.mom ^ i, self.shift), self.slices)

    def hops(self, i):
        return lax.div(self._sum(self.mom ^ i, self.shift), self.slices)

    def peer_local(self):
        return lax.rem(self._sum(self.mom, self.peer_shift), self.slices)

    def peer_hops(self):
        return lax.div(self._sum(self.mom, self.peer_shift), self.slices)


def run_copies(copies, sems):
    handles = [
        pltpu.make_async_copy(source, target, sems.at[n])
        for n, (source, target) in enumerate(copies)
    ]
    for handle in handles:
        handle.start()
    for handle in handles:
        handle.wait()


def span(index, rows):
    return pl.ds(index * rows, rows)


def through(parts, ins, leaving):
    started, n = [], 0
    for copies, buffer, target in parts:
        group = []
        for source, spot in copies:
            group.append(pltpu.make_async_copy(source, spot, ins.at[n]))
            group[-1].start()
            n += 1
        started.append(group)
    handles = []
    for n, (group, (_, buffer, target)) in enumerate(zip(started, parts)):
        for handle in group:
            handle.wait()
        handles.append(pltpu.make_async_copy(buffer, target, leaving.at[n]))
        handles[-1].start()
    for handle in handles:
        handle.wait()


def two_slices(proj, buffer, first, second):
    rows = proj.shape[1]
    return [(proj.at[n], buffer.at[span(i, rows)]) for i, n in enumerate((first, second))]


def tag_of(partner, lanes):
    number = jnp.full((TAG_ROWS, lanes), partner[0].astype(jnp.float32))
    return number.astype(jnp.bfloat16)


def pack_first(sizes, seps, partner, peram, *refs):
    outs, token, buffers, (ins, leaving) = refs[:2], refs[2], refs[3:5], refs[5:]
    plan = Plan(seps, sizes)
    start, copies = 0, []
    for buffer in buffers:
        rows = buffer.shape[1]
        source = peram.at[plan.peer_local(), plan.give, :, pl.ds(start, rows)]
        copies.append([(source, buffer)])
        start += rows
    token[...] = tag_of(partner, token.shape[-1])
    through(list(zip(copies, buffers, outs)), ins, leaving)


def pack(sizes, seps, partner, proj, tick, after, *refs):
    outs, buffers, (ins, leaving) = refs[:2], refs[2:4], refs[4:]
    plan = Plan(seps, sizes)
    rows = proj.shape[1]
    same, cross = buffers
    cross[pl.ds(2 * rows, TAG_ROWS), :] = tag_of(partner, cross.shape[-1])
    cross[pl.ds(2 * rows + TAG_ROWS, TAG_ROWS), :] = tick[...]
    copies = [
        two_slices(proj, same, plan.local(0), plan.local(1)),
        two_slices(proj, cross, plan.local(2), plan.local(3)),
    ]
    through(list(zip(copies, buffers, outs)), ins, leaving)


def choose(sizes, seps, near, far, after, out, sems):
    flag = lax.rem(Plan(seps, sizes).peer_hops(), 2)

    @pl.when(flag == 0)
    def _():
        run_copies([(near, out)], sems)

    @pl.when(flag != 0)
    def _():
        run_copies([(far, out)], sems)


def gate(first, rest, after, first_out, rest_out, token):
    token[...] = jnp.zeros(token.shape, token.dtype)


def gate_one(after, array, array_out, token):
    token[...] = after[...]


def gate_far(after, same, cross, same_out, cross_out, token):
    token[...] = after[...]


def own_fill(codes, p_ref, n, u_ref, turns):
    nev = turns.shape[-1]
    width = u_ref.shape[0]
    for r in range(len(codes)):
        real, imag = (p_ref[n, m * nev : (m + 1) * nev].T for m in (2 * r, 2 * r + 1))
        set_turns(turns, r, real, imag)
    u_ref[...] = jnp.zeros(u_ref.shape, u_ref.dtype)

    def write(spin, column, a, b):
        add_to(u_ref, along(column, nev), along(spin, nev), a)
        add_to(u_ref, along(column, nev), along(spin, nev, width), b)

    fill_spin_blocks(codes, turns, write)


def own_dot(u_ref, y_ref, ht):
    width = u_ref.shape[0]
    for tile in range(2 * width // TILE):
        start = tile * TILE
        out = lax.dot_general(
            u_ref[...], y_ref[start : start + TILE, :], NT_DIMS, preferred_element_type=jnp.float32
        ).astype(jnp.bfloat16)
        if start < width:
            ht[:, width + start : width + start + TILE] = out
        else:
            ht[:, start - width : start - width + TILE] = out
            ht[:, width + start : width + start + TILE] = -out


def codes_of(gamma, op, nterm):
    return [gamma[op, r] for r in range(nterm)]


def own_kernel_0(sizes, seps, gamma, peram, proj, y_ref, ht, token, x_ref, p_ref, u_ref, turns, sems):
    plan = Plan(seps, sizes)
    mom = plan.mom
    run_copies([(peram.at[mom, plan.keep], x_ref), (proj.at[mom], p_ref.at[0])], sems)
    width = x_ref.shape[-1]
    real, imag = x_ref[0], x_ref[1]
    y_ref[:width, :width] = real
    y_ref[:width, width:] = -imag
    y_ref[width:, :width] = imag
    y_ref[width:, width:] = real
    own_fill(codes_of(gamma, mom, turns.shape[0]), p_ref, 0, u_ref, turns)
    own_dot(u_ref, y_ref, ht)
    token[...] = jnp.zeros(token.shape, token.dtype)


def own_kernel(piece, gamma, source, y_ref, after, ht, token, p_ref, u_ref, turns, sems):
    mom = lax.axis_index("mom")
    run_copies([(source.at[mom], p_ref.at[0])], sems)
    own_fill(codes_of(gamma, mom ^ piece, turns.shape[0]), p_ref, 0, u_ref, turns)
    own_dot(u_ref, y_ref, ht)
    token[...] = jnp.zeros(token.shape, token.dtype)


def find_labels(plan, partner, tick, tags, label):
    mom = plan.mom

    def number(tag):
        return jnp.max(tag.astype(jnp.float32)).astype(jnp.int32)

    partners = [partner[0], number(tick[...]), number(tags[:TAG_ROWS]), number(tags[TAG_ROWS:])]
    count = len(partners)
    for p in range(count):
        back = jnp.int32(0)
        for i, value in enumerate(partners):
            back = back + jnp.where(value == (mom ^ p), mom ^ i, 0)
        label[p] = jnp.where(plan.forward, back, mom ^ p)
        label[count + p] = jnp.where(plan.forward, back, partners[p]) ^ mom


def other_products(pieces, gamma, label, products, sources, refs, before=None):
    k_ref, p_ref, hs, wa, wb, turns_a, turns_b, sems = refs
    mom = lax.axis_index("mom")
    nterm, nev = turns_a.shape[0], turns_a.shape[-1]
    width = wa.shape[0]
    (here, away), flag = sources
    for n in range(2):
        for wanted, refs_now in ((0, here), (1, away)):

            @pl.when(flag == wanted)
            def _():
                pltpu.make_async_copy(refs_now[n], p_ref.at[n], sems.at[n]).start()

    if before is not None:
        before()
    for n, piece in enumerate(pieces):
        for own, source in enumerate(products):

            @pl.when(label[4 + piece] == own)
            def _():
                pltpu.make_async_copy(source, hs.at[n], sems.at[2 + n]).start()

    pairs = ((wa, turns_a), (wb, turns_b))

    def fill(n):
        w_ref, turns = pairs[n]
        codes = codes_of(gamma, mom ^ pieces[n], nterm)

        def write(spin, column, a, b):
            add_to(w_ref, along(spin, nev), along(column, nev), a)
            add_to(w_ref, along(spin, nev), along(column, nev, width), b)

        def step(r):
            rows = slice(r * nev, (r + 1) * nev)
            w_ref[rows, :] = jnp.zeros((nev, w_ref.shape[1]), w_ref.dtype)
            real, imag = (p_ref[n, m * nev : (m + 1) * nev] for m in (2 * r, 2 * r + 1))
            set_turns(turns, r, real, imag)

        def term(r):
            fill_term(codes, turns, write, r)

        return [functools.partial(f, r) for f in (step, term) for r in range(nterm)]

    def dots(n):
        def dot(start, half):
            lanes = slice(start, start + TILE)
            left = slice(width, 3 * width) if half == 0 else slice(0, 2 * width)
            rows = slice(half * width, (half + 1) * width)
            k_ref[n, rows, lanes] = lax.dot_general(
                hs[n, :, left], pairs[n][0][lanes, :], NT_DIMS, preferred_element_type=jnp.float32
            )

        return [functools.partial(dot, tile, half) for tile in range(0, width, TILE) for half in (0, 1)]

    for n in range(2):
        pltpu.make_async_copy(away[n], p_ref.at[n], sems.at[n]).wait()
    for step in fill(0):
        step()
    for n in range(2):
        pltpu.make_async_copy(products[0], hs.at[n], sems.at[2 + n]).wait()
    ahead = fill(1)
    for n, dot in enumerate(dots(0)):
        for step in ahead[2 * n : 2 * n + 2]:
            step()
        dot()
    for dot in dots(1):
        dot()


def other_flag(plan, sizes):
    return lax.rem(plan.hops(0), 2) if sizes[2] == 2 else jnp.int32(1)


def other_kernel_02(sizes, seps, gamma, partner, tick, h0, h1, h2, h3, proj, near, same, cross, *refs):
    k_ref, label, tags, sems, refs = refs[0], refs[1], refs[2], refs[3], (refs[0],) + refs[4:]
    plan = Plan(seps, sizes)
    rows = proj.shape[1]
    low, at = span(0, rows), plan.local(0)
    sources = (((proj.at[at], near.at[at]), (same.at[low], cross.at[low])), other_flag(plan, sizes))

    def before():
        run_copies([(cross.at[pl.ds(2 * rows, 2 * TAG_ROWS)], tags)], sems)
        find_labels(plan, partner, tick, tags, label)

    other_products((0, 2), gamma, label, (h0, h1, h2, h3), sources, refs, before)


def other_kernel_13(sizes, seps, gamma, label, h0, h1, h2, h3, core, near, same, cross, *refs):
    plan = Plan(seps, sizes)
    rows = core.shape[1]
    away, at = span(1 if sizes[2] == 2 else 0, rows), plan.local(0)
    sources = (((core.at[at], near.at[at]), (same.at[away], cross.at[away])), other_flag(plan, sizes))
    other_products((1, 3), gamma, label, (h0, h1, h2, h3), sources, refs)


def row_sums(k_refs, source, offset, totals):
    rows = 16
    width = source.shape[-1]
    nev = totals[0].shape[-1]

    def step(index, totals):
        row = pl.multiple_of(index * rows, rows)
        here = pl.ds(pl.multiple_of(offset + row, rows), rows)
        later = pl.ds(pl.multiple_of(width + offset + row, rows), rows)
        totals = list(totals)
        for spin in range(NSPIN):
            lanes = along(spin, nev)
            real = source[0, pl.ds(row, rows), lanes].astype(jnp.float32)
            imag = source[1, pl.ds(row, rows), lanes].astype(jnp.float32)
            for n in range(len(totals) // 2):
                k_ref, p = k_refs[n // 2], n % 2
                kr, ki = k_ref[p, here, lanes], k_ref[p, later, lanes]
                totals[2 * n] += real * kr - imag * ki
                totals[2 * n + 1] += real * ki + imag * kr
        return tuple(totals)

    return lax.fori_loop(0, source.shape[1] // rows, step, totals)


def trace_kernel(sizes, rest, seps, label, ka, kb, near, far, out_ref, first_buf, rest_buf, sems):
    plan = Plan(seps, sizes)
    count = 2 * ka.shape[0]
    width = rest_buf.shape[-1]
    nev = width // NSPIN
    flag = lax.rem(lax.div(plan.hops(0), max(sizes[2] // 2, 1)), 2)
    later = pltpu.make_async_copy(rest, rest_buf, sems.at[1])
    chunk = first_buf.shape[1] // 2
    parts = [pl.ds(n * chunk, chunk) for n in range(2)]
    for wanted, source in ((0, near), (1, far)):

        @pl.when(flag == wanted)
        def _():
            for n, rows in enumerate(parts):
                pltpu.make_async_copy(
                    source.at[:, rows], first_buf.at[:, rows], sems.at[2 * n]
                ).start()

    later.start()
    totals = tuple(jnp.zeros((16, nev), jnp.float32) for _ in range(2 * count))
    for n, rows in enumerate(parts):
        pltpu.make_async_copy(far.at[:, rows], first_buf.at[:, rows], sems.at[2 * n]).wait()
        totals = row_sums((ka, kb), first_buf.at[:, rows], n * chunk, totals)
    later.wait()
    totals = row_sums((ka, kb), rest_buf, first_buf.shape[1], totals)
    sums = [jnp.sum(total, axis=0, keepdims=True) for total in totals]
    sums = [jnp.sum(total, axis=1, keepdims=True) * (1.0 / width) for total in sums]
    shape = out_ref.shape[1:]
    spot = lax.broadcasted_iota(jnp.int32, shape, 0) * shape[1]
    spot = spot + lax.broadcasted_iota(jnp.int32, shape, 1)
    row = lax.div(spot, plan.time_count)
    here = (row // 2 == plan.sep_index) & (lax.rem(spot, plan.time_count) == plan.pair_time)
    if plan.live is not None:
        here = here & plan.live
    values = [jnp.where(row % 2 == 0, sums[2 * p], sums[2 * p + 1]) for p in range(count)]
    lines = []
    for op in range(count):
        line = jnp.zeros(shape, jnp.float32)
        for p, value in zip((0, 2, 1, 3), values):
            line = jnp.where(label[p] == op, value, line)
        lines.append(jnp.where(here, line, 0.0))
    for n in range(out_ref.shape[0]):
        out_ref[n] = lines[n % count]


def smem():
    return pl.BlockSpec(memory_space=pltpu.SMEM)


def vmem():
    return pl.BlockSpec(memory_space=pltpu.VMEM)


def anywhere():
    return pl.BlockSpec(memory_space=pl.ANY)


def hbm():
    return pl.BlockSpec(memory_space=pltpu.HBM)


def limit(mib):
    return pltpu.CompilerParams(vmem_limit_bytes=mib * MIB)


def shards(peram_blocks, projections, gamma_index, partner, separations):
    src_count, snk_count = lax.axis_size("src"), lax.axis_size("snk")
    mom_count = lax.axis_size("mom")
    slices, offsets = peram_blocks.shape[:2]
    width = peram_blocks.shape[-1]
    nterm, nev = projections.shape[2], projections.shape[-1]
    time_count = slices * src_count
    sep_count = separations.shape[0]
    half_snk = snk_count // 2
    rows = nterm * 2 * nev
    sizes = (slices, offsets, src_count, snk_count)
    proj = projections.reshape(slices, rows, nev)

    def swap_mom(array, i):
        return lax.ppermute(array, "mom", [(a, a ^ i) for a in range(mom_count)])

    def swap_snk(array):
        pairs = [(a, (a + half_snk) % snk_count) for a in range(snk_count)]
        return lax.ppermute(array, "snk", pairs)

    def next_src(array, step=1, i=0):
        pairs = [
            (((a + step) % src_count) * mom_count + (b ^ i), a * mom_count + b)
            for a in range(src_count)
            for b in range(mom_count)
        ]
        return lax.ppermute(array, ("src", "mom"), pairs)

    def most_of(array, amount):
        step = 1
        while 2 * step < src_count:
            array = jnp.where((amount // step) % 2 != 0, next_src(array, step), array)
            step *= 2
        return array, next_src(array, step)

    def call(kernel, name, in_specs, out_specs, out_shape, scratch, mib, aliases=None):
        cost = pl.CostEstimate(flops=WEIGHT, bytes_accessed=WEIGHT // 1000, transcendentals=0)
        return pl.pallas_call(
            kernel,
            in_specs=in_specs,
            out_specs=out_specs,
            out_shape=out_shape,
            scratch_shapes=scratch,
            input_output_aliases=aliases or {},
            compiler_params=limit(mib),
            cost_estimate=cost,
            name=name,
        )

    def bf16(*shape):
        return jax.ShapeDtypeStruct(shape, jnp.bfloat16)

    def dma(count):
        return pltpu.SemaphoreType.DMA((count,))

    part = functools.partial
    split = (width * 5 // 8) // 16 * 16
    two = bf16(2 * rows, nev)
    tagged = bf16(2 * rows + TAG_ROWS, nev)
    first_shape, rest_shape = bf16(2, split, width), bf16(2, width - split, width)
    token = bf16(16, 128)

    def buffers(shapes):
        return [pltpu.VMEM(shape.shape, shape.dtype) for shape in shapes]

    def alias(kernel, name, in_specs, out_shape, aliases, operands):
        return pl.pallas_call(
            kernel,
            in_specs=in_specs,
            out_specs=[anywhere()] * len(aliases) + [vmem()],
            out_shape=out_shape,
            input_output_aliases=aliases,
            compiler_params=limit(20),
            cost_estimate=pl.CostEstimate(
                flops=WEIGHT, bytes_accessed=WEIGHT // 1000, transcendentals=0
            ),
            name=name,
        )(*operands)

    leaving = [first_shape, rest_shape]
    first, rest, tick = call(
        part(pack_first, sizes),
        "pack_first",
        [smem()] * 2 + [hbm()],
        [hbm()] * 2 + [vmem()],
        leaving + [token],
        buffers(leaving) + [dma(2), dma(2)],
        58,
    )(separations, partner, peram_blocks)

    plan = Plan(separations, sizes)
    near = swap_mom(proj, 2)
    core = swap_mom(proj, 1)
    first = swap_snk(first)
    rest_near, rest_far = most_of(rest, plan.peer_hops())
    tick = swap_mom(tick, 1)
    u_scratch = pltpu.VMEM((width, 2 * width), jnp.bfloat16)
    turns = pltpu.VMEM((nterm, 4, nev, nev), jnp.bfloat16)
    piece = pltpu.VMEM((1, rows, nev), jnp.bfloat16)
    pieces = pltpu.VMEM((2, rows, nev), jnp.bfloat16)
    product = bf16(width, 3 * width)
    y, h0, done_0 = call(
        part(own_kernel_0, sizes),
        "own_products_0",
        [smem()] * 2 + [hbm()] * 2,
        [vmem()] * 3,
        [bf16(2 * width, 2 * width), product, token],
        [pltpu.VMEM((2, width, width), jnp.bfloat16), piece, u_scratch, turns, dma(2)],
        58,
    )(separations, gamma_index, peram_blocks, proj)
    leaving = [two, bf16(2 * (rows + TAG_ROWS), nev)]
    far_same, far_cross = call(
        part(pack, sizes),
        "pack",
        [smem()] * 2 + [hbm(), vmem(), vmem()],
        [hbm()] * 2,
        leaving,
        buffers(leaving) + [dma(4), dma(2)],
        58,
    )(separations, partner, proj, tick, done_0)
    if src_count == 2:
        far_same, far_cross = next_src(far_same), next_src(far_cross, 1, 2)
    else:
        far_cross = swap_mom(far_cross, 2)
    def own_one(number, source, after):
        return call(
            part(own_kernel, number),
            "own_products_%d" % number,
            [smem(), hbm(), vmem(), vmem()],
            [vmem()] * 2,
            [product, token],
            [piece, u_scratch, turns, dma(1)],
            20,
        )(gamma_index, source, y, after)

    h1, done_1 = own_one(1, core, done_0)
    near, _ = alias(
        gate_one,
        "gate_near",
        [vmem(), anywhere()],
        [bf16(*proj.shape), token],
        {1: 0},
        (done_1, near),
    )
    near_core = swap_mom(near, 1)

    if src_count > 2:
        rest_near = jnp.where(plan.peer_hops() // (src_count // 2) != 0, rest_far, rest_near)
        rest_far = rest_near
    rest = call(
        part(choose, sizes),
        "choose",
        [smem()] + [hbm()] * 2 + [vmem()],
        vmem(),
        rest_shape,
        [dma(1)],
        20,
    )(separations, rest_near, rest_far, done_1)
    h2, done_2 = own_one(2, near, done_1)
    first, rest, opened = alias(
        gate,
        "gate",
        [anywhere()] * 2 + [vmem()],
        [first_shape, rest_shape, token],
        {0: 0, 1: 1},
        (first, rest, done_2),
    )
    rest = swap_snk(rest)
    first_near, first_far = most_of(first, plan.hops(0))
    h3, done_3 = own_one(3, near_core, opened)
    far_same, far_cross, _ = alias(
        gate_far,
        "gate_far",
        [vmem()] + [anywhere()] * 2,
        [two, bf16(2 * (rows + TAG_ROWS), nev), token],
        {1: 0, 2: 1},
        (done_3, far_same, far_cross),
    )
    if src_count == 2:
        far = [far_same, far_cross, swap_mom(far_same, 1), swap_mom(far_cross, 1)]
    else:

        def moved(array):
            array = lax.dynamic_index_in_dim(array, plan.local(0), 0, keepdims=False)
            if src_count == 1:
                return array
            array, away = most_of(array, plan.hops(0))
            return jnp.where(plan.hops(0) // (src_count // 2) != 0, away, array)

        far = [moved(array) for array in (proj, near, core, near_core)]
        far[1] = jnp.concatenate([far[1], far[1], far_cross[2 * rows :]])

    k_shape = jax.ShapeDtypeStruct((2, 2 * width, width), jnp.float32)
    scratch = [pieces, pltpu.VMEM((2, width, 3 * width), jnp.bfloat16)]
    scratch += [u_scratch, u_scratch, turns, turns, dma(4)]
    ka, label = call(
        part(other_kernel_02, sizes),
        "other_products_02",
        [smem()] * 3 + [vmem()] + [hbm()] * 8,
        [vmem(), smem()],
        [k_shape, jax.ShapeDtypeStruct((2 * mom_count,), jnp.int32)],
        [pltpu.VMEM((2 * TAG_ROWS, nev), jnp.bfloat16), dma(1)] + scratch,
        20,
    )(
        separations, gamma_index, partner, tick, h0, h1, h2, h3, proj, near, far[0], far[1],
    )
    kb = call(
        part(other_kernel_13, sizes),
        "other_products_13",
        [smem()] * 3 + [hbm()] * 8,
        vmem(),
        k_shape,
        scratch,
        20,
    )(separations, gamma_index, label, h0, h1, h2, h3, core, near_core, far[2], far[3])

    device_count = src_count * snk_count * mom_count
    values = time_count * sep_count * 2
    lines = (values + 127) // 128
    out = call(
        part(trace_kernel, sizes),
        "traces",
        [hbm()] + [smem()] * 2 + [vmem()] * 2 + [hbm()] * 2,
        vmem(),
        jax.ShapeDtypeStruct((device_count, lines, 128), jnp.float32),
        buffers([first_shape, rest_shape]) + [dma(3)],
        20,
    )(rest, separations, label, ka, kb, first_near, first_far)
    out = lax.all_to_all(out, ("src", "snk", "mom"), split_axis=0, concat_axis=0, tiled=True)
    out = jnp.sum(out, axis=0).reshape(lines * 128)[:values]
    return out.reshape(sep_count, 1, 2, time_count).transpose(3, 0, 1, 2)


def solution(mesh):
    placed = (
        P("src", "snk", None, None, None),
        P("src", "mom", None, None, None, None),
        P(),
        P("mom"),
        P(),
    )
    return jax.shard_map(
        shards, mesh=mesh, in_specs=placed, out_specs=P(None, None, "mom", None), check_vma=False
    )
```

```python
import functools

import jax
import jax.numpy as jnp
from jax import lax
from jax.experimental import pallas as pl
from jax.experimental.pallas import tpu as pltpu
from jax.sharding import PartitionSpec as P

NSPIN = 4
NT_DIMS = (((1,), (1,)), ((), ()))
MIB = 1024 * 1024
WEIGHT = 10**13
TAG_ROWS = 16
TILE = 256
GAMMAS = (
    (3, 1 | 1 << 2 | 3 << 4 | 3 << 6),
    (3, 2 | 0 << 2 | 0 << 4 | 2 << 6),
    (2, 1 | 3 << 2 | 3 << 4 | 1 << 6),
    (2, 0),
)


def spin_entry(code, row):
    phase = row * 0
    for bit, (flip, phases) in enumerate(GAMMAS):
        on = (code >> bit) & 1
        phase = phase + on * ((phases >> (2 * row)) & 3)
        row = row ^ (on * flip)
    return row, phase & 3


def fill_spin_blocks(codes, turns, write):
    for r in range(len(codes)):
        fill_term(codes, turns, write, r)


def fill_term(codes, turns, write, r):
    for spin in range(NSPIN):
        column, phase = spin_entry(codes[r], spin)
        write(spin, column, *(turns[r, (n - phase) & 3] for n in (4, 1)))


def set_turns(turns, r, real, imag):
    for n, value in enumerate((real, imag, -real, -imag)):
        turns[r, n] = value


def add_to(ref, rows, lanes, value):
    ref[rows, lanes] = ref[rows, lanes] + value


def along(spin, nev, start=0):
    if isinstance(spin, int):
        return slice(start + spin * nev, start + (spin + 1) * nev)
    return pl.ds(pl.multiple_of(start + spin * nev, nev), nev)


class Plan:
    def __init__(self, seps, sizes):
        slices, offsets, src_count, snk_count = sizes
        src, snk, self.mom = (lax.axis_index(name) for name in ("src", "snk", "mom"))
        half_snk = snk_count // 2
        self.slices, self.time_count = slices, slices * src_count
        self.forward = snk < half_snk
        base = lax.rem(snk, half_snk) * offsets
        self.keep = jnp.where(self.forward, 0, offsets - 1)
        self.give = offsets - 1 - self.keep
        self.sep_index = base + self.keep
        sign = jnp.where(self.forward, 1, -1)
        self.shift = sign * seps[base + self.keep]
        self.peer_shift = -sign * seps[base + self.give]
        self.own_time = src * slices + self.mom
        late = jnp.where(self.forward, 0, self.shift)
        self.pair_time = lax.rem(self.own_time + late + self.time_count, self.time_count)
        self.live = self.forward if offsets == 1 else None

    def _sum(self, place, amount):
        return lax.rem(place + amount + self.time_count, self.time_count)

    def local(self, i):
        return lax.rem(self._sum(self.mom ^ i, self.shift), self.slices)

    def hops(self, i):
        return lax.div(self._sum(self.mom ^ i, self.shift), self.slices)

    def peer_local(self):
        return lax.rem(self._sum(self.mom, self.peer_shift), self.slices)

    def peer_hops(self):
        return lax.div(self._sum(self.mom, self.peer_shift), self.slices)


def run_copies(copies, sems):
    handles = [
        pltpu.make_async_copy(source, target, sems.at[n])
        for n, (source, target) in enumerate(copies)
    ]
    for handle in handles:
        handle.start()
    for handle in handles:
        handle.wait()


def span(index, rows):
    return pl.ds(index * rows, rows)


def through(parts, ins, leaving):
    started, n = [], 0
    for copies, buffer, target in parts:
        group = []
        for source, spot in copies:
            group.append(pltpu.make_async_copy(source, spot, ins.at[n]))
            group[-1].start()
            n += 1
        started.append(group)
    handles = []
    for n, (group, (_, buffer, target)) in enumerate(zip(started, parts)):
        for handle in group:
            handle.wait()
        handles.append(pltpu.make_async_copy(buffer, target, leaving.at[n]))
        handles[-1].start()
    for handle in handles:
        handle.wait()


def two_slices(proj, buffer, first, second):
    rows = proj.shape[1]
    return [(proj.at[n], buffer.at[span(i, rows)]) for i, n in enumerate((first, second))]


def tag_of(partner, lanes):
    number = jnp.full((TAG_ROWS, lanes), partner[0].astype(jnp.float32))
    return number.astype(jnp.bfloat16)


def pack_first(sizes, seps, partner, peram, *refs):
    outs, token, buffers, (ins, leaving) = refs[:2], refs[2], refs[3:5], refs[5:]
    plan = Plan(seps, sizes)
    start, copies = 0, []
    for buffer in buffers:
        rows = buffer.shape[1]
        source = peram.at[plan.peer_local(), plan.give, :, pl.ds(start, rows)]
        copies.append([(source, buffer)])
        start += rows
    token[...] = tag_of(partner, token.shape[-1])
    through(list(zip(copies, buffers, outs)), ins, leaving)


def pack(sizes, seps, partner, proj, tick, after, *refs):
    outs, buffers, (ins, leaving) = refs[:2], refs[2:4], refs[4:]
    plan = Plan(seps, sizes)
    rows = proj.shape[1]
    same, cross = buffers
    cross[pl.ds(2 * rows, TAG_ROWS), :] = tag_of(partner, cross.shape[-1])
    cross[pl.ds(2 * rows + TAG_ROWS, TAG_ROWS), :] = tick[...]
    copies = [
        two_slices(proj, same, plan.local(0), plan.local(1)),
        two_slices(proj, cross, plan.local(2), plan.local(3)),
    ]
    through(list(zip(copies, buffers, outs)), ins, leaving)


def choose(sizes, seps, near, far, after, out, sems):
    flag = lax.rem(Plan(seps, sizes).peer_hops(), 2)

    @pl.when(flag == 0)
    def _():
        run_copies([(near, out)], sems)

    @pl.when(flag != 0)
    def _():
        run_copies([(far, out)], sems)


def gate(first, rest, after, first_out, rest_out, token):
    token[...] = jnp.zeros(token.shape, token.dtype)


def gate_one(after, array, array_out, token):
    token[...] = after[...]


def gate_far(after, same, cross, same_out, cross_out, token):
    token[...] = after[...]


def own_fill(codes, p_ref, n, u_ref, turns):
    nev = turns.shape[-1]
    width = u_ref.shape[0]
    for r in range(len(codes)):
        real, imag = (p_ref[n, m * nev : (m + 1) * nev].T for m in (2 * r, 2 * r + 1))
        set_turns(turns, r, real, imag)
    u_ref[...] = jnp.zeros(u_ref.shape, u_ref.dtype)

    def write(spin, column, a, b):
        add_to(u_ref, along(column, nev), along(spin, nev), a)
        add_to(u_ref, along(column, nev), along(spin, nev, width), b)

    fill_spin_blocks(codes, turns, write)


def own_dot(u_ref, y_ref, ht):
    width = u_ref.shape[0]
    for tile in range(2 * width // TILE):
        start = tile * TILE
        out = lax.dot_general(
            u_ref[...], y_ref[start : start + TILE, :], NT_DIMS, preferred_element_type=jnp.float32
        ).astype(jnp.bfloat16)
        if start < width:
            ht[:, width + start : width + start + TILE] = out
        else:
            ht[:, start - width : start - width + TILE] = out
            ht[:, width + start : width + start + TILE] = -out


def codes_of(gamma, op, nterm):
    return [gamma[op, r] for r in range(nterm)]


def own_kernel_0(sizes, seps, gamma, peram, proj, y_ref, ht, token, x_ref, p_ref, u_ref, turns, sems):
    plan = Plan(seps, sizes)
    mom = plan.mom
    run_copies([(peram.at[mom, plan.keep], x_ref), (proj.at[mom], p_ref.at[0])], sems)
    width = x_ref.shape[-1]
    real, imag = x_ref[0], x_ref[1]
    y_ref[:width, :width] = real
    y_ref[:width, width:] = -imag
    y_ref[width:, :width] = imag
    y_ref[width:, width:] = real
    own_fill(codes_of(gamma, mom, turns.shape[0]), p_ref, 0, u_ref, turns)
    own_dot(u_ref, y_ref, ht)
    token[...] = jnp.zeros(token.shape, token.dtype)


def own_kernel(piece, gamma, source, y_ref, after, ht, token, p_ref, u_ref, turns, sems):
    mom = lax.axis_index("mom")
    run_copies([(source.at[mom], p_ref.at[0])], sems)
    own_fill(codes_of(gamma, mom ^ piece, turns.shape[0]), p_ref, 0, u_ref, turns)
    own_dot(u_ref, y_ref, ht)
    token[...] = jnp.zeros(token.shape, token.dtype)


def find_labels(plan, partner, tick, tags, label):
    mom = plan.mom

    def number(tag):
        return jnp.max(tag.astype(jnp.float32)).astype(jnp.int32)

    partners = [partner[0], number(tick[...]), number(tags[:TAG_ROWS]), number(tags[TAG_ROWS:])]
    count = len(partners)
    for p in range(count):
        back = jnp.int32(0)
        for i, value in enumerate(partners):
            back = back + jnp.where(value == (mom ^ p), mom ^ i, 0)
        label[p] = jnp.where(plan.forward, back, mom ^ p)
        label[count + p] = jnp.where(plan.forward, back, partners[p]) ^ mom


def other_products(pieces, gamma, label, products, sources, refs, before=None):
    k_ref, p_ref, hs, wa, wb, turns_a, turns_b, sems = refs
    mom = lax.axis_index("mom")
    nterm, nev = turns_a.shape[0], turns_a.shape[-1]
    width = wa.shape[0]
    (here, away), flag = sources
    for n in range(2):
        for wanted, refs_now in ((0, here), (1, away)):

            @pl.when(flag == wanted)
            def _():
                pltpu.make_async_copy(refs_now[n], p_ref.at[n], sems.at[n]).start()

    if before is not None:
        before()
    for n, piece in enumerate(pieces):
        for own, source in enumerate(products):

            @pl.when(label[4 + piece] == own)
            def _():
                pltpu.make_async_copy(source, hs.at[n], sems.at[2 + n]).start()

    pairs = ((wa, turns_a), (wb, turns_b))

    def fill(n):
        w_ref, turns = pairs[n]
        codes = codes_of(gamma, mom ^ pieces[n], nterm)

        def write(spin, column, a, b):
            add_to(w_ref, along(spin, nev), along(column, nev), a)
            add_to(w_ref, along(spin, nev), along(column, nev, width), b)

        def step(r):
            rows = slice(r * nev, (r + 1) * nev)
            w_ref[rows, :] = jnp.zeros((nev, w_ref.shape[1]), w_ref.dtype)
            real, imag = (p_ref[n, m * nev : (m + 1) * nev] for m in (2 * r, 2 * r + 1))
            set_turns(turns, r, real, imag)

        def term(r):
            fill_term(codes, turns, write, r)

        return [functools.partial(f, r) for f in (step, term) for r in range(nterm)]

    def dots(n):
        def dot(start, half):
            lanes = slice(start, start + TILE)
            left = slice(width, 3 * width) if half == 0 else slice(0, 2 * width)
            rows = slice(half * width, (half + 1) * width)
            k_ref[n, rows, lanes] = lax.dot_general(
                hs[n, :, left], pairs[n][0][lanes, :], NT_DIMS, preferred_element_type=jnp.float32
            )

        return [functools.partial(dot, tile, half) for tile in range(0, width, TILE) for half in (0, 1)]

    for n in range(2):
        pltpu.make_async_copy(away[n], p_ref.at[n], sems.at[n]).wait()
    for step in fill(0):
        step()
    for n in range(2):
        pltpu.make_async_copy(products[0], hs.at[n], sems.at[2 + n]).wait()
    ahead = fill(1)
    for n, dot in enumerate(dots(0)):
        for step in ahead[2 * n : 2 * n + 2]:
            step()
        dot()
    for dot in dots(1):
        dot()


def other_flag(plan, sizes):
    return lax.rem(plan.hops(0), 2) if sizes[2] == 2 else jnp.int32(1)


def other_kernel_02(sizes, seps, gamma, partner, tick, h0, h1, h2, h3, proj, near, same, cross, *refs):
    k_ref, label, tags, sems, refs = refs[0], refs[1], refs[2], refs[3], (refs[0],) + refs[4:]
    plan = Plan(seps, sizes)
    rows = proj.shape[1]
    low, at = span(0, rows), plan.local(0)
    sources = (((proj.at[at], near.at[at]), (same.at[low], cross.at[low])), other_flag(plan, sizes))

    def before():
        run_copies([(cross.at[pl.ds(2 * rows, 2 * TAG_ROWS)], tags)], sems)
        find_labels(plan, partner, tick, tags, label)

    other_products((0, 2), gamma, label, (h0, h1, h2, h3), sources, refs, before)


def other_kernel_13(sizes, seps, gamma, label, h0, h1, h2, h3, core, near, same, cross, *refs):
    plan = Plan(seps, sizes)
    rows = core.shape[1]
    away, at = span(1 if sizes[2] == 2 else 0, rows), plan.local(0)
    sources = (((core.at[at], near.at[at]), (same.at[away], cross.at[away])), other_flag(plan, sizes))
    other_products((1, 3), gamma, label, (h0, h1, h2, h3), sources, refs)


def row_sums(k_refs, source, offset, totals):
    rows = 16
    width = source.shape[-1]
    nev = totals[0].shape[-1]

    def step(index, totals):
        row = pl.multiple_of(index * rows, rows)
        here = pl.ds(pl.multiple_of(offset + row, rows), rows)
        later = pl.ds(pl.multiple_of(width + offset + row, rows), rows)
        totals = list(totals)
        for spin in range(NSPIN):
            lanes = along(spin, nev)
            real = source[0, pl.ds(row, rows), lanes].astype(jnp.float32)
            imag = source[1, pl.ds(row, rows), lanes].astype(jnp.float32)
            for n in range(len(totals) // 2):
                k_ref, p = k_refs[n // 2], n % 2
                kr, ki = k_ref[p, here, lanes], k_ref[p, later, lanes]
                totals[2 * n] += real * kr - imag * ki
                totals[2 * n + 1] += real * ki + imag * kr
        return tuple(totals)

    return lax.fori_loop(0, source.shape[1] // rows, step, totals, unroll=2)


def trace_kernel(sizes, rest, seps, label, ka, kb, near, far, out_ref, first_buf, rest_buf, sems):
    plan = Plan(seps, sizes)
    count = 2 * ka.shape[0]
    width = rest_buf.shape[-1]
    nev = width // NSPIN
    flag = lax.rem(lax.div(plan.hops(0), max(sizes[2] // 2, 1)), 2)
    later = pltpu.make_async_copy(rest, rest_buf, sems.at[1])
    chunk = first_buf.shape[1] // 2
    parts = [pl.ds(n * chunk, chunk) for n in range(2)]
    for wanted, source in ((0, near), (1, far)):

        @pl.when(flag == wanted)
        def _():
            for n, rows in enumerate(parts):
                pltpu.make_async_copy(
                    source.at[:, rows], first_buf.at[:, rows], sems.at[2 * n]
                ).start()

    later.start()
    totals = tuple(jnp.zeros((16, nev), jnp.float32) for _ in range(2 * count))
    for n, rows in enumerate(parts):
        pltpu.make_async_copy(far.at[:, rows], first_buf.at[:, rows], sems.at[2 * n]).wait()
        totals = row_sums((ka, kb), first_buf.at[:, rows], n * chunk, totals)
    later.wait()
    totals = row_sums((ka, kb), rest_buf, first_buf.shape[1], totals)
    sums = [jnp.sum(total, axis=0, keepdims=True) for total in totals]
    sums = [jnp.sum(total, axis=1, keepdims=True) * (1.0 / width) for total in sums]
    shape = out_ref.shape[1:]
    spot = lax.broadcasted_iota(jnp.int32, shape, 0) * shape[1]
    spot = spot + lax.broadcasted_iota(jnp.int32, shape, 1)
    row = lax.div(spot, plan.time_count)
    here = (row // 2 == plan.sep_index) & (lax.rem(spot, plan.time_count) == plan.pair_time)
    if plan.live is not None:
        here = here & plan.live
    values = [jnp.where(row % 2 == 0, sums[2 * p], sums[2 * p + 1]) for p in range(count)]
    lines = []
    for op in range(count):
        line = jnp.zeros(shape, jnp.float32)
        for p, value in zip((0, 2, 1, 3), values):
            line = jnp.where(label[p] == op, value, line)
        lines.append(jnp.where(here, line, 0.0))
    for n in range(out_ref.shape[0]):
        out_ref[n] = lines[n % count]


def smem():
    return pl.BlockSpec(memory_space=pltpu.SMEM)


def vmem():
    return pl.BlockSpec(memory_space=pltpu.VMEM)


def anywhere():
    return pl.BlockSpec(memory_space=pl.ANY)


def hbm():
    return pl.BlockSpec(memory_space=pltpu.HBM)


def limit(mib):
    return pltpu.CompilerParams(vmem_limit_bytes=mib * MIB)


def shards(peram_blocks, projections, gamma_index, partner, separations):
    src_count, snk_count = lax.axis_size("src"), lax.axis_size("snk")
    mom_count = lax.axis_size("mom")
    slices, offsets = peram_blocks.shape[:2]
    width = peram_blocks.shape[-1]
    nterm, nev = projections.shape[2], projections.shape[-1]
    time_count = slices * src_count
    sep_count = separations.shape[0]
    half_snk = snk_count // 2
    rows = nterm * 2 * nev
    sizes = (slices, offsets, src_count, snk_count)
    proj = projections.reshape(slices, rows, nev)

    def swap_mom(array, i):
        return lax.ppermute(array, "mom", [(a, a ^ i) for a in range(mom_count)])

    def swap_snk(array):
        pairs = [(a, (a + half_snk) % snk_count) for a in range(snk_count)]
        return lax.ppermute(array, "snk", pairs)

    def next_src(array, step=1, i=0):
        pairs = [
            (((a + step) % src_count) * mom_count + (b ^ i), a * mom_count + b)
            for a in range(src_count)
            for b in range(mom_count)
        ]
        return lax.ppermute(array, ("src", "mom"), pairs)

    def most_of(array, amount):
        step = 1
        while 2 * step < src_count:
            array = jnp.where((amount // step) % 2 != 0, next_src(array, step), array)
            step *= 2
        return array, next_src(array, step)

    def call(kernel, name, in_specs, out_specs, out_shape, scratch, mib, aliases=None):
        cost = pl.CostEstimate(flops=WEIGHT, bytes_accessed=WEIGHT // 1000, transcendentals=0)
        return pl.pallas_call(
            kernel,
            in_specs=in_specs,
            out_specs=out_specs,
            out_shape=out_shape,
            scratch_shapes=scratch,
            input_output_aliases=aliases or {},
            compiler_params=limit(mib),
            cost_estimate=cost,
            name=name,
        )

    def bf16(*shape):
        return jax.ShapeDtypeStruct(shape, jnp.bfloat16)

    def dma(count):
        return pltpu.SemaphoreType.DMA((count,))

    part = functools.partial
    split = (width * 5 // 8) // 16 * 16
    two = bf16(2 * rows, nev)
    tagged = bf16(2 * rows + TAG_ROWS, nev)
    first_shape, rest_shape = bf16(2, split, width), bf16(2, width - split, width)
    token = bf16(16, 128)

    def buffers(shapes):
        return [pltpu.VMEM(shape.shape, shape.dtype) for shape in shapes]

    def alias(kernel, name, in_specs, out_shape, aliases, operands):
        return pl.pallas_call(
            kernel,
            in_specs=in_specs,
            out_specs=[anywhere()] * len(aliases) + [vmem()],
            out_shape=out_shape,
            input_output_aliases=aliases,
            compiler_params=limit(20),
            cost_estimate=pl.CostEstimate(
                flops=WEIGHT, bytes_accessed=WEIGHT // 1000, transcendentals=0
            ),
            name=name,
        )(*operands)

    leaving = [first_shape, rest_shape]
    first, rest, tick = call(
        part(pack_first, sizes),
        "pack_first",
        [smem()] * 2 + [hbm()],
        [hbm()] * 2 + [vmem()],
        leaving + [token],
        buffers(leaving) + [dma(2), dma(2)],
        58,
    )(separations, partner, peram_blocks)

    plan = Plan(separations, sizes)
    near = swap_mom(proj, 2)
    core = swap_mom(proj, 1)
    first = swap_snk(first)
    rest_near, rest_far = most_of(rest, plan.peer_hops())
    tick = swap_mom(tick, 1)
    u_scratch = pltpu.VMEM((width, 2 * width), jnp.bfloat16)
    turns = pltpu.VMEM((nterm, 4, nev, nev), jnp.bfloat16)
    piece = pltpu.VMEM((1, rows, nev), jnp.bfloat16)
    pieces = pltpu.VMEM((2, rows, nev), jnp.bfloat16)
    product = bf16(width, 3 * width)
    y, h0, done_0 = call(
        part(own_kernel_0, sizes),
        "own_products_0",
        [smem()] * 2 + [hbm()] * 2,
        [vmem()] * 3,
        [bf16(2 * width, 2 * width), product, token],
        [pltpu.VMEM((2, width, width), jnp.bfloat16), piece, u_scratch, turns, dma(2)],
        58,
    )(separations, gamma_index, peram_blocks, proj)
    leaving = [two, bf16(2 * (rows + TAG_ROWS), nev)]
    far_same, far_cross = call(
        part(pack, sizes),
        "pack",
        [smem()] * 2 + [hbm(), vmem(), vmem()],
        [hbm()] * 2,
        leaving,
        buffers(leaving) + [dma(4), dma(2)],
        58,
    )(separations, partner, proj, tick, done_0)
    if src_count == 2:
        far_same, far_cross = next_src(far_same), next_src(far_cross, 1, 2)
    else:
        far_cross = swap_mom(far_cross, 2)
    def own_one(number, source, after):
        return call(
            part(own_kernel, number),
            "own_products_%d" % number,
            [smem(), hbm(), vmem(), vmem()],
            [vmem()] * 2,
            [product, token],
            [piece, u_scratch, turns, dma(1)],
            20,
        )(gamma_index, source, y, after)

    h1, done_1 = own_one(1, core, done_0)
    near, _ = alias(
        gate_one,
        "gate_near",
        [vmem(), anywhere()],
        [bf16(*proj.shape), token],
        {1: 0},
        (done_1, near),
    )
    near_core = swap_mom(near, 1)

    if src_count > 2:
        rest_near = jnp.where(plan.peer_hops() // (src_count // 2) != 0, rest_far, rest_near)
        rest_far = rest_near
    rest = call(
        part(choose, sizes),
        "choose",
        [smem()] + [hbm()] * 2 + [vmem()],
        vmem(),
        rest_shape,
        [dma(1)],
        20,
    )(separations, rest_near, rest_far, done_1)
    h2, done_2 = own_one(2, near, done_1)
    first, rest, opened = alias(
        gate,
        "gate",
        [anywhere()] * 2 + [vmem()],
        [first_shape, rest_shape, token],
        {0: 0, 1: 1},
        (first, rest, done_2),
    )
    rest = swap_snk(rest)
    first_near, first_far = most_of(first, plan.hops(0))
    h3, done_3 = own_one(3, near_core, opened)
    far_same, far_cross, _ = alias(
        gate_far,
        "gate_far",
        [vmem()] + [anywhere()] * 2,
        [two, bf16(2 * (rows + TAG_ROWS), nev), token],
        {1: 0, 2: 1},
        (done_3, far_same, far_cross),
    )
    if src_count == 2:
        far = [far_same, far_cross, swap_mom(far_same, 1), swap_mom(far_cross, 1)]
    else:

        def moved(array):
            array = lax.dynamic_index_in_dim(array, plan.local(0), 0, keepdims=False)
            if src_count == 1:
                return array
            array, away = most_of(array, plan.hops(0))
            return jnp.where(plan.hops(0) // (src_count // 2) != 0, away, array)

        far = [moved(array) for array in (proj, near, core, near_core)]
        far[1] = jnp.concatenate([far[1], far[1], far_cross[2 * rows :]])

    k_shape = jax.ShapeDtypeStruct((2, 2 * width, width), jnp.float32)
    scratch = [pieces, pltpu.VMEM((2, width, 3 * width), jnp.bfloat16)]
    scratch += [u_scratch, u_scratch, turns, turns, dma(4)]
    ka, label = call(
        part(other_kernel_02, sizes),
        "other_products_02",
        [smem()] * 3 + [vmem()] + [hbm()] * 8,
        [vmem(), smem()],
        [k_shape, jax.ShapeDtypeStruct((2 * mom_count,), jnp.int32)],
        [pltpu.VMEM((2 * TAG_ROWS, nev), jnp.bfloat16), dma(1)] + scratch,
        20,
    )(
        separations, gamma_index, partner, tick, h0, h1, h2, h3, proj, near, far[0], far[1],
    )
    kb = call(
        part(other_kernel_13, sizes),
        "other_products_13",
        [smem()] * 3 + [hbm()] * 8,
        vmem(),
        k_shape,
        scratch,
        20,
    )(separations, gamma_index, label, h0, h1, h2, h3, core, near_core, far[2], far[3])

    device_count = src_count * snk_count * mom_count
    values = time_count * sep_count * 2
    lines = (values + 127) // 128
    out = call(
        part(trace_kernel, sizes),
        "traces",
        [hbm()] + [smem()] * 2 + [vmem()] * 2 + [hbm()] * 2,
        vmem(),
        jax.ShapeDtypeStruct((device_count, lines, 128), jnp.float32),
        buffers([first_shape, rest_shape]) + [dma(3)],
        20,
    )(rest, separations, label, ka, kb, first_near, first_far)
    out = lax.all_to_all(out, ("src", "snk", "mom"), split_axis=0, concat_axis=0, tiled=True)
    out = jnp.sum(out, axis=0).reshape(lines * 128)[:values]
    return out.reshape(sep_count, 1, 2, time_count).transpose(3, 0, 1, 2)


def solution(mesh):
    placed = (
        P("src", "snk", None, None, None),
        P("src", "mom", None, None, None, None),
        P(),
        P("mom"),
        P(),
    )
    return jax.shard_map(
        shards, mesh=mesh, in_specs=placed, out_specs=P(None, None, "mom", None), check_vma=False
    )
```
